32 devices in a mesh: dp: 4 (over y, core), ctx: 4 (over z), tp: 2 (over x).
Axes of the slice: x: 2, y: 2, z: 4, core: 2. Of those that a mesh axis runs over, the one named last changes fastest.
Arguments:
- tokens: bfloat16 [8, 1536, 2048], P('dp', ('ctx', 'tp')), may hold values from -6 to 6
- cotangent: bfloat16 [8, 1536, 2048], P('dp', ('ctx', 'tp')), may hold values from -6 to 6
- lengths: int32 [8, 3], P('dp'), may hold values from 129 to 1024, as said below
- head_counts: int32 [2], replicated, may hold values from 8 to 12, as said below
- norm1_gain: float32 [2048], replicated, may hold values from 0.25 to 1.75
- norm2_gain: float32 [2048], replicated, may hold values from 0.25 to 1.75
- q_gain: float32 [64], replicated, may hold values from 0.25 to 1.75
- k_gain: float32 [64], replicated, may hold values from 0.25 to 1.75
- w_query: bfloat16 [2048, 1536], P(('dp', 'ctx'), 'tp'), may hold values from -0.125 to 0.125
- w_key: bfloat16 [2048, 320], replicated, may hold values from -0.125 to 0.125
- w_value: bfloat16 [2048, 320], replicated, may hold values from -0.125 to 0.125
- w_out: bfloat16 [1536, 2048], P('tp', ('dp', 'ctx')), may hold values from -1.25 to 1.25
- w_gate: bfloat16 [2048, 8192], P(('dp', 'ctx'), 'tp'), may hold values from -0.125 to 0.125
- w_up: bfloat16 [2048, 8192], P(('dp', 'ctx'), 'tp'), may hold values from -0.125 to 0.125
- w_down: bfloat16 [8192, 2048], P('tp', ('dp', 'ctx')), may hold values from -0.0625 to 0.0625
Outputs:
- output: bfloat16 [8, 1536, 2048], P('dp', ('ctx', 'tp'))
- d_input: float32 [8, 1536, 2048], P('dp', ('ctx', 'tp'))
- d_norm1: float32 [2048], replicated
- d_norm2: float32 [2048], replicated
- d_qgain: float32 [64], replicated
- d_kgain: float32 [64], replicated
- d_query: float32 [2048, 1536], P(('dp', 'ctx'), 'tp')
- d_key: float32 [2048, 320], replicated
- d_value: float32 [2048, 320], replicated
- d_out: float32 [1536, 2048], P('tp', ('dp', 'ctx'))
- d_gate: float32 [2048, 8192], P(('dp', 'ctx'), 'tp')
- d_up: float32 [2048, 8192], P(('dp', 'ctx'), 'tp')
- d_down: float32 [8192, 2048], P('tp', ('dp', 'ctx'))
The draws below stay inside these ranges and needn't reach their ends.
Inputs may be any that keep to these rules, and one draw needn't show every extreme that they name: `lengths`: each packed row of 1536 tokens holds three documents: the middle one has 1024 tokens, starts before token 384 and ends after token 1152; the first and the last sum to 512. The counts sum to 20; index t of tp holds the query heads offset_t to offset_t + head_counts[t] - 1, offset_t being the sum over lower indices; some index holds 12.
All inputs are finite; a program needn't handle non-finite values.
Results may differ from the reference program's by a relative error of at most 0.019.
Values may be sent and summed in bfloat16 or wider, within the bound.
No kernel may reach another device: no remote copies, remote signals or barrier semaphores. Data moves between devices by JAX's collectives and lax.ppermute only.
A program may use at most 640 MiB of HBM per device.

```python
import math
import jax
import jax.numpy as jnp
from jax import lax

MODEL_DIM = 2048
HEADS = 20
KVH = 5
HEAD_DIM = 64
FF = 8192
LONG_DOC_TOKENS = 1024
SHORT = 256
ROW_TOKENS = 1536
PACKED_ROWS = 8
CONTEXT_SPAN = 384
TOKENS = 12288
HSLOT = 12
QUERY_SLOTS = 24
N_TP = 2


def draw_lengths(key, part):
    lowest_value = ROW_TOKENS - CONTEXT_SPAN - LONG_DOC_TOKENS + 1
    highest = min(CONTEXT_SPAN, 2 * SHORT) - 1
    key_one, key_two = jax.random.split(key)
    leading = jax.random.randint(key_one, (PACKED_ROWS,), lowest_value, highest + 1)
    chosen = jax.random.randint(key_two, (), 0, PACKED_ROWS)
    groups = jnp.arange(PACKED_ROWS)
    leading = jnp.where(groups == chosen, lowest_value, leading)
    leading = jnp.where(groups == (chosen + 1) % PACKED_ROWS, highest, leading)
    middle = jnp.full((PACKED_ROWS,), LONG_DOC_TOKENS, jnp.int32)
    return jnp.stack([leading, middle, 2 * SHORT - leading], axis=1).astype(jnp.int32)


def draw_head_counts(key, part):
    base_count = HEADS // N_TP
    remainder = HEADS - base_count * N_TP
    if remainder >= 2:
        shifts = [2] + [1] * (remainder - 2) + [0] * (N_TP - remainder + 1)
    else:
        shifts = [2, remainder - 2] + [0] * (N_TP - 2)
    count_table = jnp.array([base_count + change_by for change_by in shifts], dtype=jnp.int32)
    return count_table[jax.random.permutation(key, N_TP)]


def levels(key, extent, cuts, least, top_value):
    def one(dim, parts):
        heights = jax.random.uniform(jax.random.fold_in(jax.random.fold_in(key, 6), dim), (parts,), jnp.float32, least / len(cuts), top_value / len(cuts))
        return jnp.repeat(jnp.exp(heights), extent[dim] // parts).reshape((-1,) + (1,) * (len(extent) - dim - 1))

    level = one(*cuts[0])
    for cut in cuts[1:]:
        level = level * one(*cut)
    return level


def gaussian(stream_key, extent, spread, limit, cuts=(), kind=jnp.bfloat16):
    result = jax.random.normal(stream_key, extent, jnp.float32) * spread
    if len(cuts) > 0:
        result = levels(stream_key, extent, cuts, -0.22, 0.18) * result
    return jnp.clip(result, min=-limit, max=limit).astype(kind)


def setup_inputs(seed: int = 0) -> dict:
    key_list = jax.random.split(jax.random.key(seed), 16)
    return {
        "tokens": gaussian(key_list[0], (PACKED_ROWS, ROW_TOKENS, MODEL_DIM), 1.0, 6.0, ((0, 4), (1, 8))),
        "cotangent": gaussian(key_list[1], (PACKED_ROWS, ROW_TOKENS, MODEL_DIM), 1.0, 6.0, ((0, 4), (1, 8))),
        "lengths": draw_lengths(jax.random.fold_in(key_list[15], 71), 0),
        "head_counts": draw_head_counts(jax.random.fold_in(key_list[15], 71), 0),
        "norm1_gain": jnp.clip(1.0 + 0.15 * jax.random.normal(key_list[4], (MODEL_DIM,), jnp.float32), 0.25, 1.75),
        "norm2_gain": jnp.clip(1.0 + 0.15 * jax.random.normal(key_list[5], (MODEL_DIM,), jnp.float32), 0.25, 1.75),
        "q_gain": jnp.clip(1.0 + 0.15 * jax.random.normal(key_list[6], (HEAD_DIM,), jnp.float32), 0.25, 1.75),
        "k_gain": jnp.clip(1.0 + 0.15 * jax.random.normal(key_list[7], (HEAD_DIM,), jnp.float32), 0.25, 1.75),
        "w_query": gaussian(key_list[8], (MODEL_DIM, QUERY_SLOTS * HEAD_DIM), MODEL_DIM ** -0.5, 0.125, ((0, 16), (1, 2))),
        "w_key": gaussian(key_list[9], (MODEL_DIM, KVH * HEAD_DIM), MODEL_DIM ** -0.5, 0.125),
        "w_value": gaussian(key_list[10], (MODEL_DIM, KVH * HEAD_DIM), MODEL_DIM ** -0.5, 0.125),
        "w_out": gaussian(key_list[11], (QUERY_SLOTS * HEAD_DIM, MODEL_DIM), (HEADS * HEAD_DIM // 64) ** -0.5, 1.25, ((0, 2), (1, 16))),
        "w_gate": gaussian(key_list[12], (MODEL_DIM, FF), MODEL_DIM ** -0.5, 0.125, ((0, 16), (1, 2))),
        "w_up": gaussian(key_list[13], (MODEL_DIM, FF), MODEL_DIM ** -0.5, 0.125, ((0, 16), (1, 2))),
        "w_down": gaussian(key_list[14], (FF, MODEL_DIM), FF ** -0.5, 0.0625, ((0, 2), (1, 16))),
    }


@jax.custom_vjp
def low(v):
    return lax.optimization_barrier(v.astype(jnp.bfloat16)).astype(jnp.float32)

@jax.custom_vjp
def low_back(v):
    return v

def low_keep(v):
    return (low(v), None)

def low_pass(kept, grad):
    return (grad,)

def back_keep(v):
    return (v, None)

def back_low(kept, grad):
    return (low(grad),)
low.defvjp(low_keep, low_pass)
low_back.defvjp(back_keep, back_low)
EPSILON = 1e-05
THETA = 10000.0
MASKED = -1e+30
HIGHEST = lax.Precision.HIGHEST

def rms_norm(value_tensor, gain):
    return value_tensor * lax.rsqrt(lax.optimization_barrier(jnp.mean(value_tensor * value_tensor, axis=-1, keepdims=True)) + EPSILON) * gain

def rotary(value_tensor, positions):
    half_width = value_tensor.shape[-1] // 2
    indices = jnp.arange(half_width).astype(jnp.float32)
    frequency = jnp.exp(indices * (-2.0 * math.log(THETA) / value_tensor.shape[-1]))
    angles = positions.astype(jnp.float32)[:, None] * frequency[None, :]
    cosine = jnp.cos(angles)[:, None, :]
    sine_of = jnp.sin(angles)[:, None, :]
    first_half = value_tensor[..., :half_width]
    second_half = value_tensor[..., half_width:]
    return jnp.concatenate([first_half * cosine - second_half * sine_of, first_half * sine_of + second_half * cosine], axis=-1)

def head_path(projected, gain, positions):
    shaped = projected.reshape(projected.shape[0], projected.shape[1] // HEAD_DIM, HEAD_DIM)
    return rotary(rms_norm(shaped, gain), positions)

def matmul(left, right):
    return jnp.dot(left, right, precision=HIGHEST, preferred_element_type=jnp.float32)

def attend_one(query, keys, values, allowed):
    scores = low_back(matmul(query, keys.T) * HEAD_DIM ** (-0.5))
    scores = jnp.where(allowed, scores, MASKED)
    peak = lax.optimization_barrier(jnp.max(scores, axis=1, keepdims=True))
    exp_scores = jnp.exp(scores - peak)
    probs = exp_scores / lax.optimization_barrier(jnp.sum(exp_scores, axis=1, keepdims=True))
    return matmul(low(probs), values)

def attend_group(pieces):
    query, keys, values, doc_ids = pieces
    token_places = jnp.arange(ROW_TOKENS, dtype=jnp.int32)
    allowed = (doc_ids[:, None] == doc_ids[None, :]) & (token_places[:, None] >= token_places[None, :])
    step_fn = jax.checkpoint(lambda slot_pieces: attend_one(slot_pieces[0], slot_pieces[1], slot_pieces[2], allowed))
    return lax.map(step_fn, (query, keys, values))

def tables(lengths, head_counts):
    doc_ends = jnp.cumsum(lengths, axis=1).astype(jnp.int32)
    doc_starts = (doc_ends - lengths).astype(jnp.int32)
    token_places = jnp.arange(ROW_TOKENS, dtype=jnp.int32)[None, :]
    doc_ids = (token_places >= doc_ends[:, 0:1]).astype(jnp.int32) + (token_places >= doc_ends[:, 1:2]).astype(jnp.int32)
    begins = jnp.take_along_axis(doc_starts, doc_ids, axis=1)
    positions = (token_places - begins).reshape(TOKENS)
    offsets = (jnp.cumsum(head_counts) - head_counts).astype(jnp.int32)
    slot_ids = jnp.arange(QUERY_SLOTS, dtype=jnp.int32)
    owner = slot_ids // HSLOT
    within = slot_ids % HSLOT
    valid = (within < head_counts[owner]).astype(jnp.float32)
    kv_head = jnp.minimum((offsets[owner] + within) // (HEADS // KVH), KVH - 1).astype(jnp.int32)
    return (doc_ids, positions, valid, kv_head)

def grouped(value_tensor):
    return jnp.moveaxis(value_tensor.reshape(PACKED_ROWS, ROW_TOKENS, QUERY_SLOTS, HEAD_DIM), 2, 1)

def layer(inputs, gain_one, gain_two, gain_query, gain_key, w_query, w_key, w_value, w_out, w_gate, w_up, w_down, doc_ids, positions, valid, kv_head):
    normed_one = low(rms_norm(inputs, gain_one))
    key_slots = jnp.take(w_key.reshape(MODEL_DIM, KVH, HEAD_DIM), kv_head, axis=1).reshape(MODEL_DIM, QUERY_SLOTS * HEAD_DIM)
    value_slots = jnp.take(w_value.reshape(MODEL_DIM, KVH, HEAD_DIM), kv_head, axis=1).reshape(MODEL_DIM, QUERY_SLOTS * HEAD_DIM)
    query_proj = low_back(matmul(normed_one, w_query))
    key_proj = low_back(matmul(normed_one, key_slots))
    value_low = low(low_back(matmul(normed_one, value_slots)))
    query_low = low(head_path(query_proj, gain_query, positions))
    key_low = low(head_path(key_proj, gain_key, positions))
    attended = lax.map(attend_group, (grouped(query_low), grouped(key_low), grouped(value_low.reshape(TOKENS, QUERY_SLOTS, HEAD_DIM)), doc_ids))
    attended = jnp.moveaxis(attended, 1, 2).reshape(TOKENS, QUERY_SLOTS, HEAD_DIM) * valid[None, :, None]
    out_low = low_back(low(attended.reshape(TOKENS, QUERY_SLOTS * HEAD_DIM)))
    residual = inputs + low_back(matmul(out_low, w_out))
    normed_two = low(rms_norm(residual, gain_two))
    gate = low_back(matmul(normed_two, w_gate))
    up_proj = low_back(matmul(normed_two, w_up))
    hidden = low(gate * jax.nn.sigmoid(gate) * up_proj)
    return residual + matmul(hidden, w_down)

def reference(tokens, cotangent, lengths, head_counts, norm1_gain, norm2_gain, q_gain, k_gain, w_query, w_key, w_value, w_out, w_gate, w_up, w_down):
    doc_ids, positions, valid, kv_head = tables(lengths, head_counts)
    floats = [array_in.astype(jnp.float32) for array_in in (tokens.reshape(TOKENS, MODEL_DIM), norm1_gain, norm2_gain, q_gain, k_gain, w_query, w_key, w_value, w_out, w_gate, w_up, w_down)]

    def forward(inputs, gain_one, gain_two, gain_query, gain_key, wq_in, wk_in, wv_in, wo_in, wg_in, wu_in, wd_in):
        return layer(inputs, gain_one, gain_two, gain_query, gain_key, wq_in, wk_in, wv_in, wo_in, wg_in, wu_in, wd_in, doc_ids, positions, valid, kv_head)
    layer_result, pullback = jax.vjp(forward, *floats)
    layer_gradients = pullback(cotangent.reshape(TOKENS, MODEL_DIM).astype(jnp.float32))
    return (layer_result.astype(jnp.bfloat16).reshape(PACKED_ROWS, ROW_TOKENS, MODEL_DIM), layer_gradients[0].reshape(PACKED_ROWS, ROW_TOKENS, MODEL_DIM), layer_gradients[1], layer_gradients[2], layer_gradients[3], layer_gradients[4], layer_gradients[5], layer_gradients[6], layer_gradients[7], layer_gradients[8], layer_gradients[9], layer_gradients[10], layer_gradients[11])
```

```python
import math

import jax
import jax.numpy as jnp
from jax import lax
from jax.experimental import pallas as pl
from jax.experimental.pallas import tpu as pltpu
from jax.sharding import Mesh
from jax.sharding import PartitionSpec as P

HEADS = 20
KVH = 5
HEAD_DIM = 64
GROUP = HEADS // KVH

EPSILON = 1e-05
THETA = 10000.0
SCALE = HEAD_DIM ** (-0.5)
EXP2_SCALE = SCALE / math.log(2.0)

BF16 = jnp.bfloat16
F32 = jnp.float32


def dot(left, right, contract):
    return lax.dot_general(left, right, ((contract[:1], contract[1:]), ((), ())), preferred_element_type=F32)


def swap(value, axis, bit=1):
    size = lax.axis_size(axis)
    return lax.ppermute(value, axis, [(i, i ^ bit) for i in range(size)])


def join(value, axis, dimension, bit=1):
    return jnp.concatenate([value, swap(value, axis, bit)], axis=dimension)


def fold(value, axis, dimension, bit=1):
    size = value.shape[dimension] // 2
    got = swap(lax.slice_in_dim(value, size, 2 * size, axis=dimension), axis, bit)
    return sum32(lax.slice_in_dim(value, 0, size, axis=dimension), got)


def sum32(left, right):
    return (left.astype(F32) + right.astype(F32)).astype(BF16)


def stacked(ref, slots, head, begin, span):
    return jnp.concatenate(
        [ref[slots[head * GROUP + i], :, begin : begin + span] for i in range(GROUP)], axis=1
    )


def attend_kernel(
    order, counts, starts, slots, q_ref, k_ref, v_ref, first_ref, place_ref, o_ref, total_ref
):
    head = pl.program_id(0)
    pack, _, wide = first_ref.shape
    span = wide // GROUP

    @pl.when(head == 0)
    def _():
        o_ref[...] = jnp.zeros_like(o_ref)

    place = place_ref[...]
    for row in range(pack):
        begin = row * span
        query = stacked(q_ref, slots, head, begin, span)
        first = first_ref[row]

        def step(i, carry):
            acc, total = carry
            block = order[row, i]
            scores = dot(k_ref[block, :, begin : begin + span].T, query, (1, 0))
            keys = starts[block] + lax.broadcasted_iota(jnp.int32, scores.shape, 0)
            weight = jnp.where((keys >= first) & (keys <= place), jnp.exp2(scores * EXP2_SCALE), 0.0)
            total = total + jnp.sum(weight, axis=0, keepdims=True)
            acc = acc + dot(v_ref[block, :, begin : begin + span], weight.astype(BF16), (1, 0))
            return acc, total

        acc, total = lax.fori_loop(
            0, counts[row], step, (jnp.zeros((HEAD_DIM, wide), F32), jnp.zeros((1, wide), F32))
        )
        total_ref[0, row] = total
        acc = (acc / total).astype(o_ref.dtype)
        for i in range(GROUP):
            o_ref[slots[head * GROUP + i], :, begin : begin + span] = acc[:, i * span : (i + 1) * span]


def attention_specs(query, keyvalue, first):
    slot_count, _, lanes = query.shape
    pack, _, wide = first.shape
    blocks = keyvalue.shape[0]
    whole = pl.BlockSpec((slot_count, HEAD_DIM, lanes), lambda g, *_: (0, 0, 0))
    keys = pl.BlockSpec((blocks, HEAD_DIM, lanes), lambda g, *_: (0, g, 0))
    values = pl.BlockSpec((blocks, HEAD_DIM, lanes), lambda g, *_: (0, KVH + g, 0))
    totals = pl.BlockSpec((1, pack, 1, wide), lambda g, *_: (g, 0, 0, 0))
    bounds = [
        pl.BlockSpec((pack, 1, wide), lambda g, *_: (0, 0, 0)),
        pl.BlockSpec((1, wide), lambda g, *_: (0, 0)),
    ]
    work = HEADS * lanes * blocks * (wide // GROUP)
    return whole, keys, values, totals, bounds, work


def attend(query, keyvalue, tables):
    order, counts, starts, slots, first, place = tables
    pack, _, wide = first.shape
    whole, keys, values, totals, bounds, work = attention_specs(query, keyvalue, first)
    spec = pltpu.PrefetchScalarGridSpec(
        num_scalar_prefetch=4,
        grid=(KVH,),
        in_specs=[whole, keys, values, *bounds],
        out_specs=[whole, totals],
    )
    return pl.pallas_call(
        attend_kernel,
        grid_spec=spec,
        out_shape=[jax.ShapeDtypeStruct(query.shape, BF16), jax.ShapeDtypeStruct((KVH, pack, 1, wide), F32)],
        compiler_params=pltpu.CompilerParams(dimension_semantics=("arbitrary",), vmem_limit_bytes=40 * 2**20),
        cost_estimate=pl.CostEstimate(flops=work * 1024, bytes_accessed=8 * 2**20, transcendentals=work),
        name="attend",
    )(order, counts, starts, slots, query, keyvalue, keyvalue, first, place)


def attend_back_kernel(
    order, counts, starts, slots, q_ref, g_ref, o_ref, k_ref, v_ref, total_ref, first_ref, place_ref,
    dq_ref, dkv_ref,
):
    head = pl.program_id(0)
    pack, _, wide = first_ref.shape
    span = wide // GROUP

    @pl.when(head == 0)
    def _():
        dq_ref[...] = jnp.zeros_like(dq_ref)

    dkv_ref[...] = jnp.zeros_like(dkv_ref)
    place = place_ref[...]
    for row in range(pack):
        begin = row * span
        query, grad, out = (stacked(ref, slots, head, begin, span) for ref in (q_ref, g_ref, o_ref))
        inner = jnp.sum(grad.astype(F32) * out.astype(F32), axis=0, keepdims=True)
        lift = jnp.log2(total_ref[0, row])
        first = first_ref[row]

        def step(i, acc):
            block = order[row, i]
            key, value = (ref[block, :, begin : begin + span] for ref in (k_ref, v_ref))
            scores = dot(key.T, query, (1, 0))
            keys = starts[block] + lax.broadcasted_iota(jnp.int32, scores.shape, 0)
            probs = jnp.where((keys >= first) & (keys <= place), jnp.exp2(scores * EXP2_SCALE - lift), 0.0)
            grad_probs = dot(value.T, grad, (1, 0))
            grad_scores = (probs * (grad_probs - inner)).astype(BF16)
            dkv_ref[block, 0, :, begin : begin + span] = (
                (dot(grad_scores, query, (1, 1)) * SCALE).T.astype(dkv_ref.dtype)
            )
            dkv_ref[block, 1, :, begin : begin + span] = (
                dot(probs.astype(BF16), grad, (1, 1)).T.astype(dkv_ref.dtype)
            )
            return acc + dot(key, grad_scores, (1, 0))

        acc = lax.fori_loop(0, counts[row], step, jnp.zeros((HEAD_DIM, wide), F32)) * SCALE
        for i in range(GROUP):
            dq_ref[slots[head * GROUP + i], :, begin : begin + span] = acc[:, i * span : (i + 1) * span]


def attend_back(query, grad, out, keyvalue, totals_in, tables):
    order, counts, starts, slots, first, place = tables
    whole, keys, values, totals, bounds, work = attention_specs(query, keyvalue, first)
    blocks, _, lanes = keyvalue.shape
    spec = pltpu.PrefetchScalarGridSpec(
        num_scalar_prefetch=4,
        grid=(KVH,),
        in_specs=[whole, whole, whole, keys, values, totals, *bounds],
        out_specs=[whole, pl.BlockSpec((blocks, 2, HEAD_DIM, lanes), lambda g, *_: (0, 0, g, 0))],
    )
    return pl.pallas_call(
        attend_back_kernel,
        grid_spec=spec,
        out_shape=[
            jax.ShapeDtypeStruct(query.shape, F32),
            jax.ShapeDtypeStruct((blocks, 2, KVH * HEAD_DIM, lanes), BF16),
        ],
        compiler_params=pltpu.CompilerParams(dimension_semantics=("arbitrary",), vmem_limit_bytes=48 * 2**20),
        cost_estimate=pl.CostEstimate(flops=work * 2560, bytes_accessed=16 * 2**20, transcendentals=work),
        name="attend_back",
    )(order, counts, starts, slots, query, grad, out, keyvalue, keyvalue, totals_in, first, place)


def strip_of(ref, index, strip):
    return ref[:, pl.ds(pl.multiple_of(index * strip, strip), strip)]


def rate_of(value):
    return lax.rsqrt(jnp.mean(value * value, axis=-1, keepdims=True) + EPSILON)


def norm_one_kernel(near, tokens_ref, gain_ref, normed_ref, near_ref):
    value = tokens_ref[...].astype(F32)
    normed_ref[...] = (value * rate_of(value) * gain_ref[...]).astype(BF16)
    strip = value.shape[1] // near.shape[0]
    for j in range(near.shape[0]):
        near_ref[:, j * strip : (j + 1) * strip] = strip_of(normed_ref, near[j], strip)


def norm_two_kernel(place, tokens_ref, attended_ref, gain_ref, residual_ref, normed_ref):
    strip = tokens_ref.shape[1] // place.shape[0]
    for i in range(place.shape[0]):
        columns = slice(i * strip, (i + 1) * strip)
        residual_ref[:, columns] = tokens_ref[:, columns].astype(F32) + strip_of(attended_ref, place[i], strip)
    value = residual_ref[...]
    normed_ref[...] = (value * rate_of(value) * gain_ref[...]).astype(BF16)


def norm_back(value, gain, grad):
    rate = rate_of(value)
    normed = value * rate
    scaled = grad * gain
    back = rate * (scaled - normed * jnp.mean(scaled * normed, axis=-1, keepdims=True))
    return back, jnp.sum(grad * normed, axis=0, keepdims=True)


def add_up(ref, value):
    @pl.when(pl.program_id(0) == 0)
    def _():
        ref[...] = jnp.zeros_like(ref)

    ref[...] += value


def back_two_kernel(near, grad_ref, residual_ref, cotangent_ref, gain_ref, out_ref, near_ref, gain_grad_ref):
    back, gain_grad = norm_back(residual_ref[...], gain_ref[...], grad_ref[...])
    out_ref[...] = cotangent_ref[...].astype(F32) + back
    add_up(gain_grad_ref, gain_grad)
    strip = grad_ref.shape[1] // near.shape[0]
    for j in range(near.shape[0]):
        near_ref[:, j * strip : (j + 1) * strip] = strip_of(out_ref, near[j], strip).astype(BF16)


def back_one_kernel(place, grad_ref, near_ref, tokens_ref, above_ref, gain_ref, out_ref, gain_grad_ref):
    strip = tokens_ref.shape[1] // place.shape[0]
    for i in range(place.shape[0]):
        columns = slice(i * strip, (i + 1) * strip)
        out_ref[:, columns] = grad_ref[:, columns] + strip_of(near_ref, place[i], strip)
    back, gain_grad = norm_back(tokens_ref[...].astype(F32), gain_ref[...], out_ref[...])
    out_ref[...] = above_ref[...] + back
    add_up(gain_grad_ref, gain_grad)


def by_tokens(kernel, table, arrays, gain, outs, gain_grad=False):
    tokens, width = arrays[0].shape
    block = tokens // 3
    tile = pl.BlockSpec((block, width), lambda i, *_: (i, 0))
    line = pl.BlockSpec((1, width), lambda i, *_: (0, 0))
    spec = pltpu.PrefetchScalarGridSpec(
        num_scalar_prefetch=1,
        grid=(3,),
        in_specs=[tile] * len(arrays) + [line],
        out_specs=[tile] * len(outs) + [line] * gain_grad,
    )
    shapes = [jax.ShapeDtypeStruct((tokens, width), t) for t in outs]
    shapes += [jax.ShapeDtypeStruct((1, width), F32)] * gain_grad
    return pl.pallas_call(
        kernel,
        grid_spec=spec,
        out_shape=shapes,
        compiler_params=pltpu.CompilerParams(dimension_semantics=("arbitrary",), vmem_limit_bytes=40 * 2**20),
        cost_estimate=pl.CostEstimate(flops=16 * tokens * width, bytes_accessed=16 * tokens * width, transcendentals=0),
    )(table, *arrays, gain[None, :])


def unfold_kernel(place, total_ref, key_ref, value_ref, small_ref):
    width = key_ref.shape[0]
    strip = total_ref.shape[1] // place.shape[0]
    for i in range(place.shape[0]):
        columns = slice(i * strip, (i + 1) * strip)
        block = strip_of(total_ref, place[i], strip).astype(F32)
        key_ref[:, columns] = block[:width]
        value_ref[:, columns] = block[width : 2 * width]
        small_ref[:, columns] = block[2 * width : 2 * width + 16]


def unfold(place, total, width):
    model = total.shape[1]
    spec = pltpu.PrefetchScalarGridSpec(
        num_scalar_prefetch=1,
        grid=(1,),
        in_specs=[pl.BlockSpec(total.shape, lambda i, *_: (0, 0))],
        out_specs=[
            pl.BlockSpec((width, model), lambda i, *_: (0, 0)),
            pl.BlockSpec((width, model), lambda i, *_: (0, 0)),
            pl.BlockSpec((16, model), lambda i, *_: (0, 0)),
        ],
    )
    return pl.pallas_call(
        unfold_kernel,
        grid_spec=spec,
        out_shape=[
            jax.ShapeDtypeStruct((width, model), F32),
            jax.ShapeDtypeStruct((width, model), F32),
            jax.ShapeDtypeStruct((16, model), F32),
        ],
        compiler_params=pltpu.CompilerParams(dimension_semantics=("arbitrary",), vmem_limit_bytes=40 * 2**20),
    )(place, total)


def head_forward(projected, gain, turn):
    cosine, sine = turn
    half = HEAD_DIM // 2
    rate = lax.rsqrt(jnp.mean(projected * projected, axis=1, keepdims=True) + EPSILON)
    value = projected * rate * gain[:, None]
    low, high = value[:, :half], value[:, half:]
    return jnp.concatenate([low * cosine - high * sine, low * sine + high * cosine], axis=1)


def head_back(projected, gain, turn, grad):
    cosine, sine = turn
    half = HEAD_DIM // 2
    low, high = grad[:, :half], grad[:, half:]
    grad = jnp.concatenate([low * cosine + high * sine, high * cosine - low * sine], axis=1)
    rate = lax.rsqrt(jnp.mean(projected * projected, axis=1, keepdims=True) + EPSILON)
    normed = projected * rate
    scaled = grad * gain[:, None]
    back = rate * (scaled - normed * jnp.mean(scaled * normed, axis=1, keepdims=True))
    return back, jnp.sum(grad * normed, axis=(0, 2))


def paired():
    return lax.axis_size("tp") == 2 and lax.axis_size("row") == 2


def plane_sum(value):
    return lax.psum_scatter(value, ("row", "core", "tp"), scatter_dimension=0, tiled=True)


def both_cores(chunk):
    return jnp.concatenate([chunk, swap(chunk, "core")])


def other_half(part):
    return part[part.shape[0] // 2 :]


def own_half(part, got):
    return part[: part.shape[0] // 2].astype(F32) + got.astype(F32)


def far_hops(far):
    middle = far.shape[0] // 2
    return swap(far[:middle], "row"), swap(far[middle:], "tp")


def near_sends(near, hop_y, hop_x):
    half = near.shape[0] // 2
    return (
        (near[:half] + hop_y[half:].astype(F32)).astype(BF16),
        (near[half:] + hop_x[half:].astype(F32)).astype(BF16),
    )


def plane_total(own, hop_y, hop_x, top_x, bottom_y):
    half = own.shape[0] // 2
    return own + jnp.concatenate(
        [hop_y[:half].astype(F32) + top_x.astype(F32), hop_x[:half].astype(F32) + bottom_y.astype(F32)]
    )


def stage(*values):
    return lax.optimization_barrier(values)


def body(
    tokens, cotangent, lengths, head_counts, norm1_gain, norm2_gain, q_gain, k_gain,
    w_query, w_key, w_value, w_out, w_gate, w_up, w_down,
):
    pack, span, width = tokens.shape
    rows, cores, ctx, tp = (lax.axis_size(a) for a in ("row", "core", "ctx", "tp"))
    own_tokens = pack * span
    slot_count = w_query.shape[1] // HEAD_DIM
    all_slots = slot_count * tp
    devices = rows * cores * ctx
    strip = width // devices
    row_index, core_index, ctx_index, tp_index = (lax.axis_index(a) for a in ("row", "core", "ctx", "tp"))

    plane = rows * cores

    def ordered(mine, other, index):
        first = index == 0
        return jnp.where(first, mine, other), jnp.where(first, other, mine)

    part = w_gate.shape[1] // plane
    down_turned = w_down.T

    def first_hop(pick):
        mine = jnp.stack([pick(r, core_index) for r in range(rows)])
        return mine, swap(jnp.stack([pick(r, 1 - core_index) for r in range(rows)]), "core")

    def second_hop(mine, got):
        both = ordered(mine, got, core_index)
        mine = jnp.stack([lax.dynamic_index_in_dim(x, row_index, 0, False) for x in both])
        got = swap(jnp.stack([lax.dynamic_index_in_dim(x, 1 - row_index, 0, False) for x in both]), "row")
        low, high = ordered(mine, got, row_index)
        return jnp.concatenate([low, high])

    def pick_columns(r, c):
        return jnp.concatenate(
            [lax.dynamic_slice_in_dim(w, (r * cores + c) * part, part, 1) for w in (w_gate, w_up, down_turned)]
        )

    def by_weight(blocks, first, last):
        return jnp.concatenate([blocks[:, i * strip : (i + 1) * strip] for i in range(first, last)])

    def row_out(grad):
        view = grad.reshape(rows, cores, *grad.shape[1:])
        mine = lax.dynamic_index_in_dim(view, row_index, 0, False)
        got = swap(lax.dynamic_index_in_dim(view, 1 - row_index, 0, False), "row")
        return jnp.stack(ordered(mine, got, row_index))

    def core_out(both):
        mine = lax.dynamic_index_in_dim(both, core_index, 1, False)
        got = swap(lax.dynamic_index_in_dim(both, 1 - core_index, 1, False), "core")
        low, high = ordered(mine, got, core_index)
        return [x for r in range(rows) for x in (low[r], high[r])]

    def from_tp(value, axis):
        if tp == 2:
            return join(value, "tp", axis)
        return lax.all_gather(value, "tp", axis=axis, tiled=True)

    def up(value):
        return lax.ppermute(value, "ctx", [(i, i + 1) for i in range(ctx - 1)])

    def beside(value):
        if tp == 2:
            return jnp.stack([value, swap(value, "tp")])
        return lax.all_gather(value, "tp", axis=0)

    length = span * tp * ctx
    first_end = lengths[:, 0:1]
    second_end = first_end + lengths[:, 1:2]
    own_start = (ctx_index * tp + tp_index) * span
    places = own_start + jnp.arange(span, dtype=jnp.int32)[None, :]
    begins = jnp.where(places >= second_end, second_end, jnp.where(places >= first_end, first_end, 0))
    angles_of = (places - begins).astype(F32)
    frequency = jnp.exp(jnp.arange(HEAD_DIM // 2).astype(F32) * (-2.0 * math.log(THETA) / HEAD_DIM))
    angles = frequency[:, None] * angles_of.reshape(1, own_tokens)
    turn = (jnp.cos(angles), jnp.sin(angles))
    offsets = [jnp.int32(0)]
    for i in range(tp):
        offsets.append(offsets[-1] + head_counts[i])
    heads = jnp.arange(HEADS, dtype=jnp.int32)
    slots = jnp.zeros((HEADS,), jnp.int32)
    for i in range(tp):
        inside = (heads >= offsets[i]) & (heads < offsets[i + 1])
        holder = jnp.bitwise_xor(i, tp_index) if tp == 2 else i
        slots = jnp.where(inside, holder * slot_count + heads - offsets[i], slots)
    ranks = jnp.arange(devices, dtype=jnp.int32)
    near_strips = (
        (jnp.bitwise_xor(ranks // ctx % rows, row_index) * cores + jnp.bitwise_xor(ranks // (ctx * rows), core_index))
        * ctx + jnp.bitwise_xor(ranks % ctx, ctx_index)
    )
    strip_places = (
        (jnp.bitwise_xor(ranks // ctx % cores, core_index) * rows + jnp.bitwise_xor(ranks // (ctx * cores), row_index))
        * ctx + jnp.bitwise_xor(ranks % ctx, ctx_index)
    )
    blocks = ctx * tp
    steps = jnp.arange(blocks, dtype=jnp.int32) // tp
    partner = jnp.arange(blocks, dtype=jnp.int32) % tp
    if tp == 2:
        partner = jnp.bitwise_xor(partner, tp_index)
    starts = ((ctx_index - steps) * tp + partner) * span
    seen = (starts[None, :] >= 0) & (starts[None, :] <= own_start) & (starts[None, :] + span > begins[:, :1])
    counts = jnp.sum(seen.astype(jnp.int32), axis=1)
    turns = jnp.sum(
        (seen[:, None, :] & (jnp.arange(blocks)[None, None, :] < jnp.arange(blocks)[None, :, None])).astype(jnp.int32),
        axis=2,
    )
    order = jnp.sum(
        jnp.where(
            seen[:, None, :] & (turns[:, None, :] == jnp.arange(blocks)[None, :, None]),
            jnp.arange(blocks, dtype=jnp.int32)[None, None, :],
            0,
        ),
        axis=2,
    )
    tables = (
        order,
        counts,
        starts,
        slots,
        jnp.concatenate([begins] * GROUP, axis=1)[:, None, :],
        jnp.concatenate([places] * GROUP, axis=1),
    )

    half = own_tokens // 2
    two = paired()
    key_value = jnp.concatenate([w_key, w_value], axis=1)
    flat = tokens.reshape(own_tokens, width)
    grad_low = cotangent.reshape(own_tokens, width)
    normed_one, normed_near = by_tokens(norm_one_kernel, near_strips, [flat], norm1_gain, [BF16, BF16])
    kv_width = KVH * HEAD_DIM
    projected = dot(key_value, normed_one, (0, 1))
    key_proj = projected[:kv_width].reshape(KVH, HEAD_DIM, own_tokens)
    key_low = head_forward(key_proj, k_gain, turn).astype(BF16).reshape(kv_width, own_tokens)
    own_kv = jnp.concatenate([key_low, projected[kv_width:].astype(BF16)])

    mine, got = first_hop(pick_columns)
    query_part = join(w_query, "ctx", 0)
    out_part = join(w_out, "ctx", 1)
    got, query_part, out_part, own_kv = stage(got, query_part, out_part, own_kv)

    packed = second_hop(mine, got)
    going, arrived = up(own_kv), [beside(own_kv)]
    query_part = join(query_part, "ctx", 0, 2)
    packed, going, arrived[0], query_part = stage(packed, going, arrived[0], query_part)
    gate_up = lax.all_gather(by_weight(packed, 0, 2), "ctx", axis=1, tiled=True)

    arrived.append(beside(going))
    going = up(going)
    query_part = join(query_part, "row", 0)
    going, arrived[1], query_part, packed = stage(going, arrived[1], query_part, packed)

    arrived.append(beside(going))
    going = up(going)
    query_part = from_tp(query_part, 1)
    out_part = join(out_part, "ctx", 1, 2)
    going, arrived[2], query_part, out_part, packed = stage(going, arrived[2], query_part, out_part, packed)

    arrived.append(beside(going))
    query_full = join(query_part, "core", 0)
    out_part = join(out_part, "row", 1)
    arrived[3], query_full, out_part, packed = stage(arrived[3], query_full, out_part, packed)
    keyvalue = jnp.concatenate(arrived)

    query_proj = dot(query_full, normed_near, (0, 1)).reshape(all_slots, HEAD_DIM, own_tokens)
    query_low = head_forward(query_proj, q_gain, turn).astype(BF16)
    out_low, totals = attend(query_low, keyvalue, tables)
    out_part = from_tp(out_part, 0)
    top, bottom = grad_low[:half], grad_low[half:]
    grad_near = (swap(top, "tp"), swap(bottom, "row")) if two else (top, bottom)
    out_low, totals, out_part, grad_near, packed = stage(out_low, totals, out_part, grad_near, packed)
    down_full = lax.all_gather(by_weight(packed, 2, 3), "ctx", axis=1, tiled=True)
    out_full = join(out_part, "core", 1)
    out_flat = out_low.reshape(all_slots * HEAD_DIM, own_tokens)
    attended = dot(out_flat, out_full, (0, 0))
    residual, normed_two = by_tokens(norm_two_kernel, strip_places, [flat, attended], norm2_gain, [F32, BF16])
    normed_two, residual, out_full = stage(normed_two, residual, out_full)

    def forward(chunk):
        gate, up_proj = dot(chunk, gate_full, (1, 0)), dot(chunk, up_full, (1, 0))
        return gate, up_proj, (gate * jax.nn.sigmoid(gate) * up_proj).astype(BF16)

    if two:
        top, bottom = normed_two[:half], normed_two[half:]
        near = swap(top, "tp"), swap(bottom, "row")
        normed_all = [both_cores(normed_two)]
        near, normed_all[0] = stage(near, normed_all[0])
        far = swap(jnp.concatenate([top, near[0]]), "row"), swap(jnp.concatenate([bottom, near[1]]), "tp")
        normed_all.append(both_cores(jnp.concatenate(near)))
        far, normed_all, gate_up = stage(far, normed_all, gate_up)
    gate_full, up_full = (gate_up[i * plane : (i + 1) * plane].reshape(width, part) for i in range(2))
    if two:
        top, bottom = grad_low[:half], grad_low[half:]
        normed_all.append(both_cores(jnp.concatenate(far)))
        ready = [forward(x) for x in normed_all]
        grad_far = (
            swap(jnp.concatenate([top, grad_near[0]]), "row"), swap(jnp.concatenate([bottom, grad_near[1]]), "tp")
        )
        grad_all = [both_cores(grad_low), both_cores(jnp.concatenate(grad_near))]
        ready, grad_far, grad_all, normed_all = stage(ready, grad_far, grad_all, normed_all)
        grad_all.append(both_cores(jnp.concatenate(grad_far)))
    else:
        normed_all = [lax.all_gather(normed_two, ("row", "core", "tp"), axis=0, tiled=True)]
        grad_all = [lax.all_gather(grad_low, ("row", "core", "tp"), axis=0, tiled=True)]
        ready = [forward(normed_all[0])]
    chunks = range(len(normed_all))
    hidden = [x[2] for x in ready]

    def column_gradient(values, grads):
        summed = sum(dot(values[i], grads[i], (0, 0)) for i in chunks)
        return summed.astype(BF16).reshape(plane, strip * ctx, part)

    grad_down = column_gradient(grad_all, hidden)
    grad_down, gate_full, up_full, down_full, ready, grad_all = stage(
        grad_down, gate_full, up_full, down_full, ready, grad_all
    )
    down_full = down_full.reshape(width, part)
    grad_down = lax.psum_scatter(grad_down, "ctx", scatter_dimension=1, tiled=True)
    hidden = [x[2] for x in ready]

    def hidden_grads(i):
        gate, up_proj, _ = ready[i]
        sigmoid_gate = jax.nn.sigmoid(gate)
        grad_hidden = dot(grad_all[i], down_full, (1, 0))
        return (
            (grad_hidden * up_proj * sigmoid_gate * (1.0 + gate * (1.0 - sigmoid_gate))).astype(BF16),
            (grad_hidden * gate * sigmoid_gate).astype(BF16),
        )

    def input_part(grads):
        return (dot(grads[0], gate_full, (1, 1)) + dot(grads[1], up_full, (1, 1))).astype(BF16)

    def column_part(kind, values, pairs):
        return sum(dot(values[i], pairs[i][kind], (0, 0)) for i in chunks[:-1]) if two else 0.0

    def column_rest(kind, values, pairs, summed):
        summed = summed + dot(values[-1], pairs[-1][kind], (0, 0))
        return summed.astype(BF16).reshape(plane, strip * ctx, part)

    def output_part(i):
        return dot(hidden[i], down_full, (1, 1)).astype(BF16)

    grads = [None] * len(chunks)
    if two:
        grads[2] = hidden_grads(2)
        far_part = input_part(grads[2])
        grads[2], far_part, far_send, grad_all = stage(grads[2], far_part, other_half(far_part), grad_all)
        far = own_half(far_part, swap(far_send, "core")).astype(BF16)
        grads[1] = hidden_grads(1)
        far, grads[1], grad_all = stage(far, grads[1], grad_all)
        hops = far_hops(far)
        near_part = input_part(grads[1])
        grads[0] = hidden_grads(0)
        own_part = input_part(grads[0])
        hops, near_part, own_part, grads, hidden = stage(hops, near_part, own_part, grads, hidden)
        near = own_half(near_part, swap(other_half(near_part), "core"))
        own = own_half(own_part, swap(other_half(own_part), "core"))
        sends = near_sends(near, *hops)
        far_part = output_part(2)
        sends, own, far_part, normed_all = stage(sends, own, far_part, normed_all)
        top_x, bottom_y = swap(sends[0], "tp"), swap(sends[1], "row")
        output_far = own_half(far_part, swap(other_half(far_part), "core")).astype(BF16)
        gate_parts = column_part(0, normed_all, grads)
        top_x, bottom_y, output_far, grads, normed_all, gate_parts = stage(
            top_x, bottom_y, output_far, grads, normed_all, gate_parts
        )
        output_hops = far_hops(output_far)
        grad_normed_two = plane_total(own, *hops, top_x, bottom_y)
    else:
        grads[0] = hidden_grads(0)
        gate_parts = column_part(0, normed_all, grads)
        grad_normed_two = plane_sum(input_part(grads[0])).astype(F32)
        output_hops = grad_normed_two
    grad_residual, grad_attn, grad_norm_two = by_tokens(
        back_two_kernel, near_strips, [grad_normed_two, residual, grad_low], norm2_gain, [F32, BF16], True
    )

    grad_out = dot(out_full, grad_attn, (1, 1)).astype(BF16).reshape(all_slots, HEAD_DIM, own_tokens)
    grad_query, grad_kv = attend_back(query_low, grad_out, out_low, keyvalue, totals, tables)
    grad_out_w = dot(out_flat, grad_attn, (1, 0)).astype(BF16)
    grad_out_w = fold(grad_out_w, "core", 1)
    output_hops, grad_query, grad_kv, grads, grad_out_w, grad_down = stage(
        output_hops, grad_query, grad_kv, grads, grad_out_w, grad_down
    )
    grad_kv = grad_kv.reshape(ctx, tp, 2 * kv_width, own_tokens)

    def to_tp(value, axis):
        if tp == 2:
            return fold(value, "tp", axis)
        return lax.psum_scatter(value, "tp", scatter_dimension=axis, tiled=True)

    def to_owner(value):
        if tp == 2:
            return value[0].astype(F32) + swap(value[1], "tp").astype(F32)
        return lax.psum_scatter(value, "tp", scatter_dimension=0, tiled=False).astype(F32)

    def down(value):
        return lax.ppermute(value.astype(BF16), "ctx", [(j, j - 1) for j in range(1, ctx)]).astype(F32)

    summed = to_owner(grad_kv[ctx - 1])
    grad_gate_w = column_rest(0, normed_all, grads, gate_parts)
    out_w_low, out_w_high = grad_out_w[: all_slots * 32], grad_out_w[all_slots * 32 :]
    out_w_low = fold(out_w_low, "row", 1)
    summed, grad_gate_w, grad_kv, grad_query, out_w_low, out_w_high, normed_all, grads = stage(
        summed, grad_gate_w, grad_kv, grad_query, out_w_low, out_w_high, normed_all, grads
    )
    grad_gate_w = lax.psum_scatter(grad_gate_w, "ctx", scatter_dimension=1, tiled=True)

    summed = to_owner(grad_kv[2]) + down(summed)
    up_parts = column_part(1, normed_all, grads)
    out_w_high = fold(out_w_high, "row", 1)
    summed, grad_kv, grad_query, out_w_low, out_w_high, normed_all, grads, up_parts = stage(
        summed, grad_kv, grad_query, out_w_low, out_w_high, normed_all, grads, up_parts
    )

    summed = to_owner(grad_kv[1]) + down(summed)
    grad_up_w = column_rest(1, normed_all, grads, up_parts)
    grad_query_proj, grad_q_gain = head_back(query_proj, q_gain, turn, grad_query)
    grad_query_low = grad_query_proj.astype(BF16).reshape(all_slots * HEAD_DIM, own_tokens)
    grad_down = row_out(grad_down)
    summed, grad_query_low, grad_q_gain, grad_kv, grad_up_w, grad_gate_w, grad_down, out_w_low, out_w_high = stage(
        summed, grad_query_low, grad_q_gain, grad_kv, grad_up_w, grad_gate_w, grad_down, out_w_low, out_w_high
    )
    grad_up_w = lax.psum_scatter(grad_up_w, "ctx", scatter_dimension=1, tiled=True)

    summed = to_owner(grad_kv[0]) + down(summed)
    grad_query_w = dot(normed_near, grad_query_low, (0, 1)).astype(BF16)
    grad_query_w = fold(grad_query_w, "core", 0)
    grad_down = core_out(grad_down)
    grad_gate_w = row_out(grad_gate_w)
    summed, grad_query_w, grad_query_low, grad_down, grad_gate_w, out_w_low, out_w_high = stage(
        summed, grad_query_w, grad_query_low, grad_down, grad_gate_w, out_w_low, out_w_high
    )

    grad_normed_near = dot(grad_query_low, query_full, (0, 1))
    grad_gate_w = core_out(grad_gate_w)
    grad_key_proj, grad_k_gain = head_back(
        key_proj, k_gain, turn, summed[:kv_width].reshape(KVH, HEAD_DIM, own_tokens)
    )
    grad_kv_low = jnp.concatenate(
        [grad_key_proj.reshape(kv_width, own_tokens).astype(BF16), summed[kv_width:].astype(BF16)]
    )
    padded = jnp.pad(grad_kv_low, ((0, 32), (0, 0)))
    total = dot(padded, normed_near if two else normed_one, (1, 0))
    grad_normed_one = dot(grad_kv_low, key_value, (0, 1))
    grad_inputs, grad_norm_one = by_tokens(
        back_one_kernel, strip_places, [grad_normed_one, grad_normed_near, flat, grad_residual], norm1_gain, [F32], True
    )
    gains = jnp.concatenate([grad_q_gain, grad_k_gain, jnp.zeros((width - 2 * HEAD_DIM,), F32)])
    small = jnp.concatenate([grad_norm_one, grad_norm_two, gains[None]])
    moved = (near_strips if two else ranks)[:, None] == ranks[None, :]
    small = jnp.sum(
        jnp.where(moved[None, :, :, None], small.reshape(3, 1, devices, strip), 0.0), axis=2
    ).reshape(3, width)
    total = lax.dynamic_update_slice(total, small, (2 * kv_width, 0)).astype(BF16)
    query_w_low, query_w_high = grad_query_w[:, : all_slots * 32], grad_query_w[:, all_slots * 32 :]
    query_w_low = fold(query_w_low, "row", 0)
    grad_out_w = to_tp(jnp.concatenate([out_w_low, out_w_high]), 0)
    total, query_w_low, query_w_high, grad_out_w, grad_gate_w, hidden = stage(
        total, query_w_low, query_w_high, grad_out_w, grad_gate_w, hidden
    )

    if not two:
        total = lax.psum(total, ("row", "core", "ctx", "tp"))
        output = residual + plane_sum(output_part(0)).astype(F32)
        grad_query_w = jnp.concatenate([query_w_low, fold(query_w_high, "row", 0)], axis=1)
        grad_query_w = to_tp(grad_query_w, 1)
        grad_query_w = fold(fold(grad_query_w, "ctx", 0, 2), "ctx", 0)
        grad_out_w = fold(fold(grad_out_w, "ctx", 1, 2), "ctx", 1)
        grad_up_w = core_out(row_out(grad_up_w))
    else:
        total = fold(total, "core", 1)
        near_part = output_part(1)
        query_w_high = fold(query_w_high, "row", 0)
        total, near_part, query_w_low, query_w_high, grad_out_w = stage(
            total, near_part, query_w_low, query_w_high, grad_out_w
        )
        size = total.shape[0] // 2
        got = swap(lax.dynamic_slice_in_dim(total, (1 - tp_index) * size, size, 0), "tp")
        total = sum32(lax.dynamic_slice_in_dim(total, tp_index * size, size, 0), got)
        own_part = output_part(0)
        near = own_half(near_part, swap(other_half(near_part), "core"))
        grad_out_w = fold(grad_out_w, "ctx", 1, 2)
        total, grad_out_w, query_w_low, query_w_high, own_part, near = stage(
            total, grad_out_w, query_w_low, query_w_high, own_part, near
        )
        total = fold(total, "row", 1)
        grad_query_w = fold(jnp.concatenate([query_w_low, query_w_high], axis=1), "tp", 1)
        own = own_half(own_part, swap(other_half(own_part), "core"))
        total, grad_query_w, own, grad_out_w = stage(total, grad_query_w, own, grad_out_w)
        total = fold(total, "ctx", 1, 2)
        sends = near_sends(near, *output_hops)
        top_x, bottom_y = swap(sends[0], "tp"), swap(sends[1], "row")
        grad_out_w = fold(grad_out_w, "ctx", 1)
        total, top_x, bottom_y, grad_query_w, grad_out_w = stage(total, top_x, bottom_y, grad_query_w, grad_out_w)
        total = fold(total, "ctx", 1)
        grad_query_w = fold(grad_query_w, "ctx", 0, 2)
        total, grad_query_w, grad_up_w = stage(total, grad_query_w, grad_up_w)
        total = join(total, "ctx", 1)
        output = residual + plane_total(own, *output_hops, top_x, bottom_y)
        grad_up_w = row_out(grad_up_w)
        total, grad_query_w, grad_up_w, output = stage(total, grad_query_w, grad_up_w, output)
        total = join(total, "ctx", 1, 2)
        total, grad_query_w, grad_up_w = stage(total, grad_query_w, grad_up_w)
        total = join(total, "row", 1)
        grad_query_w = fold(grad_query_w, "ctx", 0)
        grad_up_w = core_out(grad_up_w)
        total, grad_query_w, grad_up_w = stage(total, grad_query_w, grad_up_w)
        other = swap(total, "tp")
        first = tp_index == 0
        total = jnp.concatenate([jnp.where(first, total, other), jnp.where(first, other, total)])
        (total,) = stage(total)
        total = join(total, "core", 1)
    grad_key_w, grad_value_w, small = unfold(strip_places if two else ranks, total, kv_width)

    return (
        output.astype(BF16).reshape(pack, span, width),
        grad_inputs.reshape(pack, span, width),
        small[0],
        small[1],
        small[2, :HEAD_DIM],
        small[2, HEAD_DIM : 2 * HEAD_DIM],
        grad_query_w.astype(F32),
        grad_key_w.T,
        grad_value_w.T,
        grad_out_w.astype(F32),
        jnp.concatenate(grad_gate_w, axis=1).astype(F32),
        jnp.concatenate(grad_up_w, axis=1).astype(F32),
        jnp.concatenate([x.T for x in grad_down]).astype(F32),
    )


def solution(mesh):
    dp, ctx, tp = (mesh.shape[a] for a in ("dp", "ctx", "tp"))
    split = Mesh(mesh.devices.reshape(dp // 2, 2, ctx, tp), ("row", "core", "ctx", "tp"))
    dp = ("row", "core")
    every = ("row", "core", "ctx")
    token = P(dp, ("ctx", "tp"), None)
    by_row, by_column = P(every, "tp"), P("tp", every)
    return jax.shard_map(
        body,
        mesh=split,
        in_specs=(
            token, token, P(dp, None), P(), P(), P(), P(), P(),
            by_row, P(), P(), by_column, by_row, by_row, by_column,
        ),
        out_specs=(
            token, token, P(), P(), P(), P(),
            by_row, P(), P(), by_column, by_row, by_row, by_column,
        ),
        check_vma=False,
    )
```

```python
import math

import jax
import jax.numpy as jnp
from jax import lax
from jax.experimental import pallas as pl
from jax.experimental.pallas import tpu as pltpu
from jax.sharding import Mesh
from jax.sharding import PartitionSpec as P

HEADS = 20
KVH = 5
HEAD_DIM = 64
GROUP = HEADS // KVH

EPSILON = 1e-05
THETA = 10000.0
SCALE = HEAD_DIM ** (-0.5)
EXP2_SCALE = SCALE / math.log(2.0)

BF16 = jnp.bfloat16
F32 = jnp.float32


def dot(left, right, contract):
    return lax.dot_general(left, right, ((contract[:1], contract[1:]), ((), ())), preferred_element_type=F32)


def swap(value, axis, bit=1):
    size = lax.axis_size(axis)
    return lax.ppermute(value, axis, [(i, i ^ bit) for i in range(size)])


def join(value, axis, dimension, bit=1):
    return jnp.concatenate([value, swap(value, axis, bit)], axis=dimension)


def fold(value, axis, dimension, bit=1):
    size = value.shape[dimension] // 2
    got = swap(lax.slice_in_dim(value, size, 2 * size, axis=dimension), axis, bit)
    return sum32(lax.slice_in_dim(value, 0, size, axis=dimension), got)


def sum32(left, right):
    return (left.astype(F32) + right.astype(F32)).astype(BF16)


def stacked(ref, slots, head, begin, span):
    return jnp.concatenate(
        [ref[slots[head * GROUP + i], :, begin : begin + span] for i in range(GROUP)], axis=1
    )


def attend_kernel(
    order, counts, starts, slots, q_ref, k_ref, v_ref, first_ref, place_ref, o_ref, total_ref
):
    head = pl.program_id(0)
    pack, _, wide = first_ref.shape
    span = wide // GROUP

    @pl.when(head == 0)
    def _():
        o_ref[...] = jnp.zeros_like(o_ref)

    place = place_ref[...]
    for row in range(pack):
        begin = row * span
        query = stacked(q_ref, slots, head, begin, span)
        first = first_ref[row]

        def step(i, carry):
            acc, total = carry
            block = order[row, i]
            scores = dot(k_ref[block, :, begin : begin + span].T, query, (1, 0))
            keys = starts[block] + lax.broadcasted_iota(jnp.int32, scores.shape, 0)
            weight = jnp.where((keys >= first) & (keys <= place), jnp.exp2(scores * EXP2_SCALE), 0.0)
            total = total + jnp.sum(weight, axis=0, keepdims=True)
            acc = acc + dot(v_ref[block, :, begin : begin + span], weight.astype(BF16), (1, 0))
            return acc, total

        acc, total = lax.fori_loop(
            0, counts[row], step, (jnp.zeros((HEAD_DIM, wide), F32), jnp.zeros((1, wide), F32))
        )
        total_ref[0, row] = total
        acc = (acc / total).astype(o_ref.dtype)
        for i in range(GROUP):
            o_ref[slots[head * GROUP + i], :, begin : begin + span] = acc[:, i * span : (i + 1) * span]


def attention_specs(query, keyvalue, first):
    slot_count, _, lanes = query.shape
    pack, _, wide = first.shape
    blocks = keyvalue.shape[0]
    whole = pl.BlockSpec((slot_count, HEAD_DIM, lanes), lambda g, *_: (0, 0, 0))
    keys = pl.BlockSpec((blocks, HEAD_DIM, lanes), lambda g, *_: (0, g, 0))
    values = pl.BlockSpec((blocks, HEAD_DIM, lanes), lambda g, *_: (0, KVH + g, 0))
    totals = pl.BlockSpec((1, pack, 1, wide), lambda g, *_: (g, 0, 0, 0))
    bounds = [
        pl.BlockSpec((pack, 1, wide), lambda g, *_: (0, 0, 0)),
        pl.BlockSpec((1, wide), lambda g, *_: (0, 0)),
    ]
    work = HEADS * lanes * blocks * (wide // GROUP)
    return whole, keys, values, totals, bounds, work


def attend(query, keyvalue, tables):
    order, counts, starts, slots, first, place = tables
    pack, _, wide = first.shape
    whole, keys, values, totals, bounds, work = attention_specs(query, keyvalue, first)
    spec = pltpu.PrefetchScalarGridSpec(
        num_scalar_prefetch=4,
        grid=(KVH,),
        in_specs=[whole, keys, values, *bounds],
        out_specs=[whole, totals],
    )
    return pl.pallas_call(
        attend_kernel,
        grid_spec=spec,
        out_shape=[jax.ShapeDtypeStruct(query.shape, BF16), jax.ShapeDtypeStruct((KVH, pack, 1, wide), F32)],
        compiler_params=pltpu.CompilerParams(dimension_semantics=("arbitrary",), vmem_limit_bytes=40 * 2**20),
        cost_estimate=pl.CostEstimate(flops=work * 1024, bytes_accessed=8 * 2**20, transcendentals=work),
        name="attend",
    )(order, counts, starts, slots, query, keyvalue, keyvalue, first, place)


def attend_back_kernel(
    order, counts, starts, slots, q_ref, g_ref, o_ref, k_ref, v_ref, total_ref, first_ref, place_ref,
    dq_ref, dkv_ref,
):
    head = pl.program_id(0)
    pack, _, wide = first_ref.shape
    span = wide // GROUP

    @pl.when(head == 0)
    def _():
        dq_ref[...] = jnp.zeros_like(dq_ref)

    dkv_ref[...] = jnp.zeros_like(dkv_ref)
    place = place_ref[...]
    for row in range(pack):
        begin = row * span
        query, grad, out = (stacked(ref, slots, head, begin, span) for ref in (q_ref, g_ref, o_ref))
        inner = jnp.sum(grad.astype(F32) * out.astype(F32), axis=0, keepdims=True)
        lift = jnp.log2(total_ref[0, row])
        first = first_ref[row]

        def step(i, acc):
            block = order[row, i]
            key, value = (ref[block, :, begin : begin + span] for ref in (k_ref, v_ref))
            scores = dot(key.T, query, (1, 0))
            keys = starts[block] + lax.broadcasted_iota(jnp.int32, scores.shape, 0)
            probs = jnp.where((keys >= first) & (keys <= place), jnp.exp2(scores * EXP2_SCALE - lift), 0.0)
            grad_probs = dot(value.T, grad, (1, 0))
            grad_scores = (probs * (grad_probs - inner)).astype(BF16)
            dkv_ref[block, 0, :, begin : begin + span] = (
                (dot(grad_scores, query, (1, 1)) * SCALE).T.astype(dkv_ref.dtype)
            )
            dkv_ref[block, 1, :, begin : begin + span] = (
                dot(probs.astype(BF16), grad, (1, 1)).T.astype(dkv_ref.dtype)
            )
            return acc + dot(key, grad_scores, (1, 0))

        acc = lax.fori_loop(0, counts[row], step, jnp.zeros((HEAD_DIM, wide), F32)) * SCALE
        for i in range(GROUP):
            dq_ref[slots[head * GROUP + i], :, begin : begin + span] = acc[:, i * span : (i + 1) * span]


def attend_back(query, grad, out, keyvalue, totals_in, tables):
    order, counts, starts, slots, first, place = tables
    whole, keys, values, totals, bounds, work = attention_specs(query, keyvalue, first)
    blocks, _, lanes = keyvalue.shape
    spec = pltpu.PrefetchScalarGridSpec(
        num_scalar_prefetch=4,
        grid=(KVH,),
        in_specs=[whole, whole, whole, keys, values, totals, *bounds],
        out_specs=[whole, pl.BlockSpec((blocks, 2, HEAD_DIM, lanes), lambda g, *_: (0, 0, g, 0))],
    )
    return pl.pallas_call(
        attend_back_kernel,
        grid_spec=spec,
        out_shape=[
            jax.ShapeDtypeStruct(query.shape, F32),
            jax.ShapeDtypeStruct((blocks, 2, KVH * HEAD_DIM, lanes), BF16),
        ],
        compiler_params=pltpu.CompilerParams(dimension_semantics=("arbitrary",), vmem_limit_bytes=48 * 2**20),
        cost_estimate=pl.CostEstimate(flops=work * 2560, bytes_accessed=16 * 2**20, transcendentals=work),
        name="attend_back",
    )(order, counts, starts, slots, query, grad, out, keyvalue, keyvalue, totals_in, first, place)


def strip_of(ref, index, strip):
    return ref[:, pl.ds(pl.multiple_of(index * strip, strip), strip)]


def rate_of(value):
    return lax.rsqrt(jnp.mean(value * value, axis=-1, keepdims=True) + EPSILON)


def norm_one_kernel(near, tokens_ref, gain_ref, normed_ref, near_ref):
    value = tokens_ref[...].astype(F32)
    normed_ref[...] = (value * rate_of(value) * gain_ref[...]).astype(BF16)
    strip = value.shape[1] // near.shape[0]
    for j in range(near.shape[0]):
        near_ref[:, j * strip : (j + 1) * strip] = strip_of(normed_ref, near[j], strip)


def norm_two_kernel(place, tokens_ref, attended_ref, gain_ref, residual_ref, normed_ref):
    strip = tokens_ref.shape[1] // place.shape[0]
    for i in range(place.shape[0]):
        columns = slice(i * strip, (i + 1) * strip)
        residual_ref[:, columns] = tokens_ref[:, columns].astype(F32) + strip_of(attended_ref, place[i], strip)
    value = residual_ref[...]
    normed_ref[...] = (value * rate_of(value) * gain_ref[...]).astype(BF16)


def norm_back(value, gain, grad):
    rate = rate_of(value)
    normed = value * rate
    scaled = grad * gain
    back = rate * (scaled - normed * jnp.mean(scaled * normed, axis=-1, keepdims=True))
    return back, jnp.sum(grad * normed, axis=0, keepdims=True)


def add_up(ref, value):
    @pl.when(pl.program_id(0) == 0)
    def _():
        ref[...] = jnp.zeros_like(ref)

    ref[...] += value


def back_two_kernel(near, grad_ref, residual_ref, cotangent_ref, gain_ref, out_ref, near_ref, gain_grad_ref):
    back, gain_grad = norm_back(residual_ref[...], gain_ref[...], grad_ref[...])
    out_ref[...] = cotangent_ref[...].astype(F32) + back
    add_up(gain_grad_ref, gain_grad)
    strip = grad_ref.shape[1] // near.shape[0]
    for j in range(near.shape[0]):
        near_ref[:, j * strip : (j + 1) * strip] = strip_of(out_ref, near[j], strip).astype(BF16)


def back_one_kernel(place, grad_ref, near_ref, tokens_ref, above_ref, gain_ref, out_ref, gain_grad_ref):
    strip = tokens_ref.shape[1] // place.shape[0]
    for i in range(place.shape[0]):
        columns = slice(i * strip, (i + 1) * strip)
        out_ref[:, columns] = grad_ref[:, columns] + strip_of(near_ref, place[i], strip)
    back, gain_grad = norm_back(tokens_ref[...].astype(F32), gain_ref[...], out_ref[...])
    out_ref[...] = above_ref[...] + back
    add_up(gain_grad_ref, gain_grad)


def by_tokens(kernel, table, arrays, gain, outs, gain_grad=False):
    tokens, width = arrays[0].shape
    block = tokens // 3
    tile = pl.BlockSpec((block, width), lambda i, *_: (i, 0))
    line = pl.BlockSpec((1, width), lambda i, *_: (0, 0))
    spec = pltpu.PrefetchScalarGridSpec(
        num_scalar_prefetch=1,
        grid=(3,),
        in_specs=[tile] * len(arrays) + [line],
        out_specs=[tile] * len(outs) + [line] * gain_grad,
    )
    shapes = [jax.ShapeDtypeStruct((tokens, width), t) for t in outs]
    shapes += [jax.ShapeDtypeStruct((1, width), F32)] * gain_grad
    return pl.pallas_call(
        kernel,
        grid_spec=spec,
        out_shape=shapes,
        compiler_params=pltpu.CompilerParams(dimension_semantics=("arbitrary",), vmem_limit_bytes=40 * 2**20),
        cost_estimate=pl.CostEstimate(flops=16 * tokens * width, bytes_accessed=16 * tokens * width, transcendentals=0),
    )(table, *arrays, gain[None, :])


def unfold_kernel(place, total_ref, key_ref, value_ref, small_ref):
    width = key_ref.shape[0]
    strip = total_ref.shape[1] // place.shape[0]
    for i in range(place.shape[0]):
        columns = slice(i * strip, (i + 1) * strip)
        block = strip_of(total_ref, place[i], strip).astype(F32)
        key_ref[:, columns] = block[:width]
        value_ref[:, columns] = block[width : 2 * width]
        small_ref[:, columns] = block[2 * width : 2 * width + 16]


def unfold(place, total, width):
    model = total.shape[1]
    spec = pltpu.PrefetchScalarGridSpec(
        num_scalar_prefetch=1,
        grid=(1,),
        in_specs=[pl.BlockSpec(total.shape, lambda i, *_: (0, 0))],
        out_specs=[
            pl.BlockSpec((width, model), lambda i, *_: (0, 0)),
            pl.BlockSpec((width, model), lambda i, *_: (0, 0)),
            pl.BlockSpec((16, model), lambda i, *_: (0, 0)),
        ],
    )
    return pl.pallas_call(
        unfold_kernel,
        grid_spec=spec,
        out_shape=[
            jax.ShapeDtypeStruct((width, model), F32),
            jax.ShapeDtypeStruct((width, model), F32),
            jax.ShapeDtypeStruct((16, model), F32),
        ],
        compiler_params=pltpu.CompilerParams(dimension_semantics=("arbitrary",), vmem_limit_bytes=40 * 2**20),
    )(place, total)


def head_forward(projected, gain, turn):
    cosine, sine = turn
    half = HEAD_DIM // 2
    rate = lax.rsqrt(jnp.mean(projected * projected, axis=1, keepdims=True) + EPSILON)
    value = projected * rate * gain[:, None]
    low, high = value[:, :half], value[:, half:]
    return jnp.concatenate([low * cosine - high * sine, low * sine + high * cosine], axis=1)


def head_back(projected, gain, turn, grad):
    cosine, sine = turn
    half = HEAD_DIM // 2
    low, high = grad[:, :half], grad[:, half:]
    grad = jnp.concatenate([low * cosine + high * sine, high * cosine - low * sine], axis=1)
    rate = lax.rsqrt(jnp.mean(projected * projected, axis=1, keepdims=True) + EPSILON)
    normed = projected * rate
    scaled = grad * gain[:, None]
    back = rate * (scaled - normed * jnp.mean(scaled * normed, axis=1, keepdims=True))
    return back, jnp.sum(grad * normed, axis=(0, 2))


def weight_grad_kernel(*refs):
    out_ref = refs[-1]
    count = len(refs) // 2
    total = sum(dot(refs[i][...], refs[count + i][...], (0, 0)) for i in range(count))
    out_ref[0] = total.astype(out_ref.dtype)


def weight_grad(values, grads, blocks):
    width, hidden = values[0].shape[1], grads[0].shape[1]
    block = width // blocks
    tokens = sum(v.shape[0] for v in values)
    return pl.pallas_call(
        weight_grad_kernel,
        grid=(blocks,),
        in_specs=[pl.BlockSpec((v.shape[0], block), lambda i: (0, i)) for v in values]
        + [pl.BlockSpec(g.shape, lambda i: (0, 0), pipeline_mode=pl.Buffered(1)) for g in grads],
        out_specs=pl.BlockSpec((1, block, hidden), lambda i: (i, 0, 0)),
        out_shape=jax.ShapeDtypeStruct((blocks, block, hidden), BF16),
        compiler_params=pltpu.CompilerParams(dimension_semantics=("arbitrary",), vmem_limit_bytes=56 * 2**20),
        cost_estimate=pl.CostEstimate(
            flops=2 * tokens * width * hidden, bytes_accessed=2 * tokens * (width + hidden), transcendentals=0
        ),
        name="weight_grad",
    )(*values, *grads)


def tall(tile, columns):
    return pl.BlockSpec((tile, columns), lambda i: (i, 0))


def held(weights, which=None):
    blocks = weights.shape[0] if which is None else weights.shape[0] // 2
    return pl.BlockSpec((blocks, *weights.shape[1:]), lambda i: (which or 0, 0, 0), pipeline_mode=pl.Buffered(1))


FFN_PARAMS = pltpu.CompilerParams(dimension_semantics=("arbitrary",), vmem_limit_bytes=56 * 2**20)


def matrix(ref):
    return ref[...].reshape(ref.shape[0] * ref.shape[1], ref.shape[2])


def forward_kernel(tokens_ref, gate_w, up_w, gate_ref, up_ref, hidden_ref):
    tokens = tokens_ref[...]
    gate, up = dot(tokens, matrix(gate_w), (1, 0)), dot(tokens, matrix(up_w), (1, 0))
    gate_ref[...] = gate
    up_ref[...] = up
    hidden_ref[...] = (gate / (1.0 + jnp.exp(-gate)) * up).astype(BF16)


def forward(tokens, gate_up, tile=256):
    count, width = tokens.shape
    hidden = gate_up.shape[2]
    return pl.pallas_call(
        forward_kernel,
        grid=(count // tile,),
        in_specs=[tall(tile, width), held(gate_up, 0), held(gate_up, 1)],
        out_specs=[tall(tile, hidden)] * 3,
        out_shape=[jax.ShapeDtypeStruct((count, hidden), t) for t in (F32, F32, BF16)],
        compiler_params=FFN_PARAMS,
        cost_estimate=pl.CostEstimate(
            flops=4 * count * width * hidden,
            bytes_accessed=4 * width * hidden + 2 * count * width + 10 * count * hidden,
            transcendentals=count * hidden,
        ),
        name="forward",
    )(tokens, gate_up, gate_up)


def hidden_back_kernel(grad_ref, gate_ref, up_ref, down_w, gate_w, up_w, gate_grad_ref, up_grad_ref, part_ref):
    grad = dot(grad_ref[...], matrix(down_w), (1, 0))
    gate = gate_ref[...]
    sigmoid = 1.0 / (1.0 + jnp.exp(-gate))
    gate_grad = (grad * up_ref[...] * sigmoid * (1.0 + gate * (1.0 - sigmoid))).astype(BF16)
    up_grad = (grad * gate * sigmoid).astype(BF16)
    gate_grad_ref[...] = gate_grad
    up_grad_ref[...] = up_grad
    part_ref[...] = (dot(gate_grad, matrix(gate_w), (1, 1)) + dot(up_grad, matrix(up_w), (1, 1))).astype(BF16)


def hidden_back(grad, gate, up, down_w, gate_up, tile=256):
    count, width = grad.shape
    hidden = gate.shape[1]
    return pl.pallas_call(
        hidden_back_kernel,
        grid=(count // tile,),
        in_specs=[
            tall(tile, width), tall(tile, hidden), tall(tile, hidden), held(down_w), held(gate_up, 0), held(gate_up, 1)
        ],
        out_specs=[tall(tile, hidden), tall(tile, hidden), tall(tile, width)],
        out_shape=[jax.ShapeDtypeStruct((count, n), BF16) for n in (hidden, hidden, width)],
        compiler_params=FFN_PARAMS,
        cost_estimate=pl.CostEstimate(
            flops=6 * count * width * hidden,
            bytes_accessed=6 * width * hidden + 16 * count * hidden,
            transcendentals=count * hidden,
        ),
        name="hidden_back",
    )(grad, gate, up, down_w, gate_up, gate_up)


def down_kernel(hidden_ref, down_w, out_ref):
    out_ref[...] = dot(hidden_ref[...], matrix(down_w), (1, 1)).astype(BF16)


def down_product(hidden, down_w, tile=256):
    count, size = hidden.shape
    width = down_w.shape[0] * down_w.shape[1]
    return pl.pallas_call(
        down_kernel,
        grid=(count // tile,),
        in_specs=[tall(tile, size), held(down_w)],
        out_specs=tall(tile, width),
        out_shape=jax.ShapeDtypeStruct((count, width), BF16),
        compiler_params=FFN_PARAMS,
        cost_estimate=pl.CostEstimate(
            flops=2 * count * width * size,
            bytes_accessed=2 * width * size + 2 * count * (width + size),
            transcendentals=0,
        ),
        name="down_product",
    )(hidden, down_w)


def paired():
    return lax.axis_size("tp") == 2 and lax.axis_size("row") == 2


def plane_sum(value):
    return lax.psum_scatter(value, ("row", "core", "tp"), scatter_dimension=0, tiled=True)


def both_cores(chunk):
    return jnp.concatenate([chunk, swap(chunk, "core")])


def other_half(part):
    return part[part.shape[0] // 2 :]


def own_half(part, got):
    return part[: part.shape[0] // 2].astype(F32) + got.astype(F32)


def far_hops(far):
    middle = far.shape[0] // 2
    return swap(far[:middle], "row"), swap(far[middle:], "tp")


def near_sends(near, hop_y, hop_x):
    half = near.shape[0] // 2
    return (
        (near[:half] + hop_y[half:].astype(F32)).astype(BF16),
        (near[half:] + hop_x[half:].astype(F32)).astype(BF16),
    )


def plane_total(own, hop_y, hop_x, top_x, bottom_y):
    half = own.shape[0] // 2
    return own + jnp.concatenate(
        [hop_y[:half].astype(F32) + top_x.astype(F32), hop_x[:half].astype(F32) + bottom_y.astype(F32)]
    )


def stage(*values):
    return lax.optimization_barrier(values)


def body(
    tokens, cotangent, lengths, head_counts, norm1_gain, norm2_gain, q_gain, k_gain,
    w_query, w_key, w_value, w_out, w_gate, w_up, w_down,
):
    pack, span, width = tokens.shape
    rows, cores, ctx, tp = (lax.axis_size(a) for a in ("row", "core", "ctx", "tp"))
    own_tokens = pack * span
    slot_count = w_query.shape[1] // HEAD_DIM
    all_slots = slot_count * tp
    devices = rows * cores * ctx
    strip = width // devices
    row_index, core_index, ctx_index, tp_index = (lax.axis_index(a) for a in ("row", "core", "ctx", "tp"))

    plane = rows * cores

    def ordered(mine, other, index):
        first = index == 0
        return jnp.where(first, mine, other), jnp.where(first, other, mine)

    part = w_gate.shape[1] // plane
    down_turned = w_down.T

    def first_hop(pick):
        mine = jnp.stack([pick(r, core_index) for r in range(rows)])
        return mine, swap(jnp.stack([pick(r, 1 - core_index) for r in range(rows)]), "core")

    def second_hop(mine, got):
        both = ordered(mine, got, core_index)
        mine = jnp.stack([lax.dynamic_index_in_dim(x, row_index, 0, False) for x in both])
        got = swap(jnp.stack([lax.dynamic_index_in_dim(x, 1 - row_index, 0, False) for x in both]), "row")
        low, high = ordered(mine, got, row_index)
        return jnp.concatenate([low, high])

    def pick_columns(r, c):
        return jnp.concatenate(
            [lax.dynamic_slice_in_dim(w, (r * cores + c) * part, part, 1) for w in (w_gate, w_up, down_turned)]
        )

    def by_weight(blocks, first, last):
        return jnp.concatenate([blocks[:, i * strip : (i + 1) * strip] for i in range(first, last)])

    def row_out(grad):
        view = grad.reshape(rows, cores, *grad.shape[1:])
        mine = lax.dynamic_index_in_dim(view, row_index, 0, False)
        got = swap(lax.dynamic_index_in_dim(view, 1 - row_index, 0, False), "row")
        return jnp.stack(ordered(mine, got, row_index))

    def core_out(both):
        mine = lax.dynamic_index_in_dim(both, core_index, 1, False)
        got = swap(lax.dynamic_index_in_dim(both, 1 - core_index, 1, False), "core")
        low, high = ordered(mine, got, core_index)
        return [x for r in range(rows) for x in (low[r], high[r])]

    def from_tp(value, axis):
        if tp == 2:
            return join(value, "tp", axis)
        return lax.all_gather(value, "tp", axis=axis, tiled=True)

    def up(value):
        return lax.ppermute(value, "ctx", [(i, i + 1) for i in range(ctx - 1)])

    def beside(value):
        if tp == 2:
            return jnp.stack([value, swap(value, "tp")])
        return lax.all_gather(value, "tp", axis=0)

    length = span * tp * ctx
    first_end = lengths[:, 0:1]
    second_end = first_end + lengths[:, 1:2]
    own_start = (ctx_index * tp + tp_index) * span
    places = own_start + jnp.arange(span, dtype=jnp.int32)[None, :]
    begins = jnp.where(places >= second_end, second_end, jnp.where(places >= first_end, first_end, 0))
    angles_of = (places - begins).astype(F32)
    frequency = jnp.exp(jnp.arange(HEAD_DIM // 2).astype(F32) * (-2.0 * math.log(THETA) / HEAD_DIM))
    angles = frequency[:, None] * angles_of.reshape(1, own_tokens)
    turn = (jnp.cos(angles), jnp.sin(angles))
    offsets = [jnp.int32(0)]
    for i in range(tp):
        offsets.append(offsets[-1] + head_counts[i])
    heads = jnp.arange(HEADS, dtype=jnp.int32)
    slots = jnp.zeros((HEADS,), jnp.int32)
    for i in range(tp):
        inside = (heads >= offsets[i]) & (heads < offsets[i + 1])
        holder = jnp.bitwise_xor(i, tp_index) if tp == 2 else i
        slots = jnp.where(inside, holder * slot_count + heads - offsets[i], slots)
    ranks = jnp.arange(devices, dtype=jnp.int32)
    near_strips = (
        (jnp.bitwise_xor(ranks // ctx % rows, row_index) * cores + jnp.bitwise_xor(ranks // (ctx * rows), core_index))
        * ctx + jnp.bitwise_xor(ranks % ctx, ctx_index)
    )
    strip_places = (
        (jnp.bitwise_xor(ranks // ctx % cores, core_index) * rows + jnp.bitwise_xor(ranks // (ctx * cores), row_index))
        * ctx + jnp.bitwise_xor(ranks % ctx, ctx_index)
    )
    blocks = ctx * tp
    steps = jnp.arange(blocks, dtype=jnp.int32) // tp
    partner = jnp.arange(blocks, dtype=jnp.int32) % tp
    if tp == 2:
        partner = jnp.bitwise_xor(partner, tp_index)
    starts = ((ctx_index - steps) * tp + partner) * span
    seen = (starts[None, :] >= 0) & (starts[None, :] <= own_start) & (starts[None, :] + span > begins[:, :1])
    counts = jnp.sum(seen.astype(jnp.int32), axis=1)
    turns = jnp.sum(
        (seen[:, None, :] & (jnp.arange(blocks)[None, None, :] < jnp.arange(blocks)[None, :, None])).astype(jnp.int32),
        axis=2,
    )
    order = jnp.sum(
        jnp.where(
            seen[:, None, :] & (turns[:, None, :] == jnp.arange(blocks)[None, :, None]),
            jnp.arange(blocks, dtype=jnp.int32)[None, None, :],
            0,
        ),
        axis=2,
    )
    tables = (
        order,
        counts,
        starts,
        slots,
        jnp.concatenate([begins] * GROUP, axis=1)[:, None, :],
        jnp.concatenate([places] * GROUP, axis=1),
    )

    half = own_tokens // 2
    two = paired()
    key_value = jnp.concatenate([w_key, w_value], axis=1)
    flat = tokens.reshape(own_tokens, width)
    grad_low = cotangent.reshape(own_tokens, width)
    normed_one, normed_near = by_tokens(norm_one_kernel, near_strips, [flat], norm1_gain, [BF16, BF16])
    kv_width = KVH * HEAD_DIM
    projected = dot(key_value, normed_one, (0, 1))
    key_proj = projected[:kv_width].reshape(KVH, HEAD_DIM, own_tokens)
    key_low = head_forward(key_proj, k_gain, turn).astype(BF16).reshape(kv_width, own_tokens)
    own_kv = jnp.concatenate([key_low, projected[kv_width:].astype(BF16)])

    mine, got = first_hop(pick_columns)
    query_part = join(w_query, "ctx", 0)
    out_part = join(w_out, "ctx", 1)
    got, query_part, out_part, own_kv = stage(got, query_part, out_part, own_kv)

    packed = second_hop(mine, got)
    gate_up, packed = by_weight(packed, 0, 2), by_weight(packed, 2, 3)
    going, arrived = up(own_kv), [beside(own_kv)]
    query_part = join(query_part, "ctx", 0, 2)
    packed, gate_up, going, arrived[0], query_part = stage(packed, gate_up, going, arrived[0], query_part)
    gate_up = lax.all_gather(gate_up, "ctx", axis=1, tiled=True)

    arrived.append(beside(going))
    going = up(going)
    query_part = join(query_part, "row", 0)
    going, arrived[1], query_part, packed = stage(going, arrived[1], query_part, packed)

    arrived.append(beside(going))
    going = up(going)
    query_part = from_tp(query_part, 1)
    out_part = join(out_part, "ctx", 1, 2)
    going, arrived[2], query_part, out_part, packed = stage(going, arrived[2], query_part, out_part, packed)

    arrived.append(beside(going))
    query_full = join(query_part, "core", 0)
    out_part = join(out_part, "row", 1)
    arrived[3], query_full, out_part, packed = stage(arrived[3], query_full, out_part, packed)
    keyvalue = jnp.concatenate(arrived)

    query_proj = dot(query_full, normed_near, (0, 1)).reshape(all_slots, HEAD_DIM, own_tokens)
    query_low = head_forward(query_proj, q_gain, turn).astype(BF16)
    out_low, totals = attend(query_low, keyvalue, tables)
    out_part = from_tp(out_part, 0)
    top, bottom = grad_low[:half], grad_low[half:]
    grad_near = (swap(top, "tp"), swap(bottom, "row")) if two else (top, bottom)
    out_low, totals, out_part, grad_near, packed, gate_up = stage(
        out_low, totals, out_part, grad_near, packed, gate_up
    )
    down_full = lax.all_gather(packed, "ctx", axis=1, tiled=True)
    out_full = join(out_part, "core", 1)
    out_flat = out_low.reshape(all_slots * HEAD_DIM, own_tokens)
    attended = dot(out_flat, out_full, (0, 0))
    residual, normed_two = by_tokens(norm_two_kernel, strip_places, [flat, attended], norm2_gain, [F32, BF16])
    normed_two, residual, out_full = stage(normed_two, residual, out_full)

    if two:
        top, bottom = normed_two[:half], normed_two[half:]
        near = swap(top, "tp"), swap(bottom, "row")
        other = swap(normed_two, "core")
        near, other = stage(near, other)
        far = swap(jnp.concatenate([top, near[0]]), "row"), swap(jnp.concatenate([bottom, near[1]]), "tp")
        near = jnp.concatenate(near)
        normed_all = [jnp.concatenate([normed_two, other, near, swap(near, "core")])]
        near = jnp.concatenate(grad_near)
        grad_all = [jnp.concatenate([grad_low, swap(grad_low, "core"), near, swap(near, "core")])]
        ready = [forward(normed_all[0], gate_up)]
        far, normed_all, grad_all, ready, down_full = stage(far, normed_all, grad_all, ready, down_full)
        top, bottom = grad_low[:half], grad_low[half:]
        normed_all.append(both_cores(jnp.concatenate(far)))
        ready.append(forward(normed_all[1], gate_up))
        grad_far = (
            swap(jnp.concatenate([top, grad_near[0]]), "row"), swap(jnp.concatenate([bottom, grad_near[1]]), "tp")
        )
        ready, grad_far, grad_all, normed_all = stage(ready, grad_far, grad_all, normed_all)
        grad_all.append(both_cores(jnp.concatenate(grad_far)))
    else:
        normed_all = [lax.all_gather(normed_two, ("row", "core", "tp"), axis=0, tiled=True)]
        grad_all = [lax.all_gather(grad_low, ("row", "core", "tp"), axis=0, tiled=True)]
        ready = [forward(normed_all[0], gate_up)]
    chunks = range(len(normed_all))
    hidden = [x[2] for x in ready]

    def backward(i):
        return hidden_back(grad_all[i], ready[i][0], ready[i][1], down_full, gate_up)

    def output_part(i):
        return down_product(hidden[i], down_full)

    def scattered(gradient):
        return lax.psum_scatter(gradient, "ctx", scatter_dimension=1, tiled=True)

    if two:
        far_grads = backward(1)
        far_grads, far_send, grad_all = stage(far_grads, other_half(far_grads[2]), grad_all)
        far = own_half(far_grads[2], swap(far_send, "core")).astype(BF16)
        far_part = output_part(1)
        far, grad_all, far_part = stage(far, grad_all, far_part)
        hops = far_hops(far)
        near_grads = backward(0)
        output_far = own_half(far_part, swap(other_half(far_part), "core")).astype(BF16)
        hops, near_grads, hidden, output_far = stage(hops, near_grads, hidden, output_far)
        grads = [near_grads, far_grads]
        own_part, near_part = near_grads[2][: 2 * own_tokens], near_grads[2][2 * own_tokens :]
        near = own_half(near_part, swap(other_half(near_part), "core"))
        own = own_half(own_part, swap(other_half(own_part), "core"))
        sends = near_sends(near, *hops)
        sends, own, normed_all, hidden, grad_all = stage(sends, own, normed_all, hidden, grad_all)
        top_x, bottom_y = swap(sends[0], "tp"), swap(sends[1], "row")
        grad_down = weight_grad(grad_all, hidden, plane)
        top_x, bottom_y, output_far, grads, normed_all, grad_down = stage(
            top_x, bottom_y, output_far, grads, normed_all, grad_down
        )
        output_hops = far_hops(output_far)
        grad_normed_two = plane_total(own, *hops, top_x, bottom_y)
    else:
        grads = [backward(0)]
        grad_down = weight_grad(grad_all, hidden, plane)
        grad_normed_two = plane_sum(grads[0][2]).astype(F32)
        output_hops = grad_normed_two
    grad_down = scattered(grad_down)
    grad_residual, grad_attn, grad_norm_two = by_tokens(
        back_two_kernel, near_strips, [grad_normed_two, residual, grad_low], norm2_gain, [F32, BF16], True
    )

    grad_out = dot(out_full, grad_attn, (1, 1)).astype(BF16).reshape(all_slots, HEAD_DIM, own_tokens)
    grad_query, grad_kv = attend_back(query_low, grad_out, out_low, keyvalue, totals, tables)
    grad_out_w = dot(out_flat, grad_attn, (1, 0)).astype(BF16)
    grad_out_w = fold(grad_out_w, "core", 1)
    output_hops, grad_query, grad_kv, grads, grad_out_w, normed_all, hidden = stage(
        output_hops, grad_query, grad_kv, grads, grad_out_w, normed_all, hidden
    )
    grad_kv = grad_kv.reshape(ctx, tp, 2 * kv_width, own_tokens)

    def to_tp(value, axis):
        if tp == 2:
            return fold(value, "tp", axis)
        return lax.psum_scatter(value, "tp", scatter_dimension=axis, tiled=True)

    def to_owner(value):
        if tp == 2:
            return value[0].astype(F32) + swap(value[1], "tp").astype(F32)
        return lax.psum_scatter(value, "tp", scatter_dimension=0, tiled=False).astype(F32)

    def down(value):
        return lax.ppermute(value.astype(BF16), "ctx", [(j, j - 1) for j in range(1, ctx)]).astype(F32)

    summed = to_owner(grad_kv[ctx - 1])
    grad_gate_w = weight_grad(normed_all, [g[0] for g in grads], plane)
    out_w_low, out_w_high = grad_out_w[: all_slots * 32], grad_out_w[all_slots * 32 :]
    out_w_low = fold(out_w_low, "row", 1)
    summed, grad_kv, grad_query, out_w_low, out_w_high, normed_all, grads, grad_gate_w, grad_down = stage(
        summed, grad_kv, grad_query, out_w_low, out_w_high, normed_all, grads, grad_gate_w, grad_down
    )
    grad_gate_w = scattered(grad_gate_w)

    summed = to_owner(grad_kv[2]) + down(summed)
    grad_up_w = weight_grad(normed_all, [g[1] for g in grads], plane)
    out_w_high = fold(out_w_high, "row", 1)
    summed, grad_kv, grad_query, out_w_low, out_w_high, grad_up_w, grad_down, hidden = stage(
        summed, grad_kv, grad_query, out_w_low, out_w_high, grad_up_w, grad_down, hidden
    )
    grad_up_w = scattered(grad_up_w)

    summed = to_owner(grad_kv[1]) + down(summed)
    grad_query_proj, grad_q_gain = head_back(query_proj, q_gain, turn, grad_query)
    grad_query_low = grad_query_proj.astype(BF16).reshape(all_slots * HEAD_DIM, own_tokens)
    near_part = output_part(0)
    grad_down = row_out(grad_down)
    summed, grad_query_low, grad_q_gain, grad_kv, grad_down, out_w_low, out_w_high, near_part = stage(
        summed, grad_query_low, grad_q_gain, grad_kv, grad_down, out_w_low, out_w_high, near_part
    )

    summed = to_owner(grad_kv[0]) + down(summed)
    grad_query_w = dot(normed_near, grad_query_low, (0, 1)).astype(BF16)
    grad_query_w = fold(grad_query_w, "core", 0)
    grad_normed_near = dot(grad_query_low, query_full, (0, 1))
    grad_down = core_out(grad_down)
    if two:
        own_part, near_part = near_part[: 2 * own_tokens], near_part[2 * own_tokens :]
        near = own_half(near_part, swap(other_half(near_part), "core"))
        own = own_half(own_part, swap(other_half(own_part), "core"))
        sends = near_sends(near, *output_hops)
    else:
        own, sends = near_part, summed
    summed, grad_query_w, grad_normed_near, grad_down, out_w_low, out_w_high, sends, own, grad_gate_w = stage(
        summed, grad_query_w, grad_normed_near, grad_down, out_w_low, out_w_high, sends, own, grad_gate_w
    )

    grad_key_proj, grad_k_gain = head_back(
        key_proj, k_gain, turn, summed[:kv_width].reshape(KVH, HEAD_DIM, own_tokens)
    )
    grad_kv_low = jnp.concatenate(
        [grad_key_proj.reshape(kv_width, own_tokens).astype(BF16), summed[kv_width:].astype(BF16)]
    )
    padded = jnp.pad(grad_kv_low, ((0, 32), (0, 0)))
    total = dot(padded, normed_near if two else normed_one, (1, 0))
    grad_normed_one = dot(grad_kv_low, key_value, (0, 1))
    grad_inputs, grad_norm_one = by_tokens(
        back_one_kernel, strip_places, [grad_normed_one, grad_normed_near, flat, grad_residual], norm1_gain, [F32], True
    )
    gains = jnp.concatenate([grad_q_gain, grad_k_gain, jnp.zeros((width - 2 * HEAD_DIM,), F32)])
    small = jnp.concatenate([grad_norm_one, grad_norm_two, gains[None]])
    moved = (near_strips if two else ranks)[:, None] == ranks[None, :]
    small = jnp.sum(
        jnp.where(moved[None, :, :, None], small.reshape(3, 1, devices, strip), 0.0), axis=2
    ).reshape(3, width)
    total = lax.dynamic_update_slice(total, small, (2 * kv_width, 0)).astype(BF16)
    query_w = fold(grad_query_w[:, : all_slots * 32], "row", 0), grad_query_w[:, all_slots * 32 :]
    grad_out_w = to_tp(jnp.concatenate([out_w_low, out_w_high]), 0)
    total, query_w, grad_out_w, grad_gate_w, own, sends, grad_up_w = stage(
        total, query_w, grad_out_w, grad_gate_w, own, sends, grad_up_w
    )

    def along(value, bit):
        got = swap(value, "ctx", bit)
        return sum32(
            value, jnp.concatenate([got[:, (j ^ bit) * strip : ((j ^ bit) + 1) * strip] for j in range(ctx)], axis=1)
        )

    if not two:
        total = lax.psum(total, ("row", "core", "ctx", "tp"))
        output = residual + plane_sum(own).astype(F32)
        query_w = jnp.concatenate([query_w[0], fold(query_w[1], "row", 0)], axis=1)
        grad_query_w = fold(fold(to_tp(query_w, 1), "ctx", 0, 2), "ctx", 0)
        grad_out_w = fold(fold(grad_out_w, "ctx", 1, 2), "ctx", 1)
        grad_up_w, grad_gate_w = core_out(row_out(grad_up_w)), core_out(row_out(grad_gate_w))
    else:
        total = fold(total, "core", 1)
        total, query_w, grad_out_w, grad_gate_w, own, sends = stage(
            total, query_w, grad_out_w, grad_gate_w, own, sends
        )
        size = total.shape[0] // 2
        got = swap(lax.dynamic_slice_in_dim(total, (1 - tp_index) * size, size, 0), "tp")
        total = sum32(lax.dynamic_slice_in_dim(total, tp_index * size, size, 0), got)
        query_w = jnp.concatenate([query_w[0], fold(query_w[1], "row", 0)], axis=1)
        total, grad_out_w, query_w, grad_gate_w, own, sends = stage(
            total, grad_out_w, query_w, grad_gate_w, own, sends
        )
        total = fold(total, "row", 1)
        query_w = fold(query_w, "tp", 1)
        total, query_w, sends, grad_gate_w, grad_out_w, grad_up_w = stage(
            total, query_w, sends, grad_gate_w, grad_out_w, grad_up_w
        )
        total = along(total, 1)
        top_x, bottom_y = swap(sends[0], "tp"), swap(sends[1], "row")
        grad_out_w = fold(grad_out_w, "ctx", 1, 2)
        total, query_w, grad_gate_w, top_x, bottom_y, grad_out_w, grad_up_w = stage(
            total, query_w, grad_gate_w, top_x, bottom_y, grad_out_w, grad_up_w
        )
        total = along(total, 2)
        output = residual + plane_total(own, *output_hops, top_x, bottom_y)
        grad_gate_w = row_out(grad_gate_w)
        grad_out_w = fold(grad_out_w, "ctx", 1)
        total, query_w, grad_gate_w, grad_up_w, grad_out_w, output = stage(
            total, query_w, grad_gate_w, grad_up_w, grad_out_w, output
        )
        total = join(total, "row", 1)
        query_w = fold(query_w, "ctx", 0, 2)
        grad_gate_w = core_out(grad_gate_w)
        total, grad_up_w, query_w, grad_gate_w = stage(total, grad_up_w, query_w, grad_gate_w)
        other = swap(total, "tp")
        grad_query_w = fold(query_w, "ctx", 0)
        grad_up_w = row_out(grad_up_w)
        first = tp_index == 0
        total = jnp.concatenate([jnp.where(first, total, other), jnp.where(first, other, total)])
        total, grad_up_w, grad_query_w = stage(total, grad_up_w, grad_query_w)
        total = join(total, "core", 1)
        grad_up_w = core_out(grad_up_w)
    grad_key_w, grad_value_w, small = unfold(strip_places if two else ranks, total, kv_width)

    return (
        output.astype(BF16).reshape(pack, span, width),
        grad_inputs.reshape(pack, span, width),
        small[0],
        small[1],
        small[2, :HEAD_DIM],
        small[2, HEAD_DIM : 2 * HEAD_DIM],
        grad_query_w.astype(F32),
        grad_key_w.T,
        grad_value_w.T,
        grad_out_w.astype(F32),
        jnp.concatenate(grad_gate_w, axis=1).astype(F32),
        jnp.concatenate(grad_up_w, axis=1).astype(F32),
        jnp.concatenate([x.T for x in grad_down]).astype(F32),
    )


def solution(mesh):
    dp, ctx, tp = (mesh.shape[a] for a in ("dp", "ctx", "tp"))
    split = Mesh(mesh.devices.reshape(dp // 2, 2, ctx, tp), ("row", "core", "ctx", "tp"))
    dp = ("row", "core")
    every = ("row", "core", "ctx")
    token = P(dp, ("ctx", "tp"), None)
    by_row, by_column = P(every, "tp"), P("tp", every)
    return jax.shard_map(
        body,
        mesh=split,
        in_specs=(
            token, token, P(dp, None), P(), P(), P(), P(), P(),
            by_row, P(), P(), by_column, by_row, by_row, by_column,
        ),
        out_specs=(
            token, token, P(), P(), P(), P(),
            by_row, P(), P(), by_column, by_row, by_row, by_column,
        ),
        check_vma=False,
    )
```

```python
import math

import jax
import jax.numpy as jnp
from jax import lax
from jax.experimental import pallas as pl
from jax.experimental.pallas import tpu as pltpu
from jax.sharding import Mesh
from jax.sharding import PartitionSpec as P

HEADS = 20
KVH = 5
HEAD_DIM = 64
GROUP = HEADS // KVH

EPSILON = 1e-05
THETA = 10000.0
SCALE = HEAD_DIM ** (-0.5)
EXP2_SCALE = SCALE / math.log(2.0)

BF16 = jnp.bfloat16
F32 = jnp.float32


def dot(left, right, contract):
    return lax.dot_general(left, right, ((contract[:1], contract[1:]), ((), ())), preferred_element_type=F32)


def swap(value, axis, bit=1):
    size = lax.axis_size(axis)
    return lax.ppermute(value, axis, [(i, i ^ bit) for i in range(size)])


def join(value, axis, dimension, bit=1):
    return jnp.concatenate([value, swap(value, axis, bit)], axis=dimension)


def fold(value, axis, dimension, bit=1):
    size = value.shape[dimension] // 2
    got = swap(lax.slice_in_dim(value, size, 2 * size, axis=dimension), axis, bit)
    return sum32(lax.slice_in_dim(value, 0, size, axis=dimension), got)


def sum32(left, right):
    return (left.astype(F32) + right.astype(F32)).astype(BF16)


def stacked(ref, slots, head, begin, span):
    return jnp.concatenate(
        [ref[slots[head * GROUP + i], :, begin : begin + span] for i in range(GROUP)], axis=1
    )


def attend_kernel(
    order, counts, starts, slots, q_ref, k_ref, v_ref, first_ref, place_ref, o_ref, total_ref
):
    head = pl.program_id(0)
    pack, _, wide = first_ref.shape
    span = wide // GROUP

    @pl.when(head == 0)
    def _():
        o_ref[...] = jnp.zeros_like(o_ref)

    place = place_ref[...]
    for row in range(pack):
        begin = row * span
        query = stacked(q_ref, slots, head, begin, span)
        first = first_ref[row]

        def step(i, carry):
            acc, total = carry
            block = order[row, i]
            scores = dot(k_ref[block, :, begin : begin + span].T, query, (1, 0))
            keys = starts[block] + lax.broadcasted_iota(jnp.int32, scores.shape, 0)
            weight = jnp.where((keys >= first) & (keys <= place), jnp.exp2(scores * EXP2_SCALE), 0.0)
            total = total + jnp.sum(weight, axis=0, keepdims=True)
            acc = acc + dot(v_ref[block, :, begin : begin + span], weight.astype(BF16), (1, 0))
            return acc, total

        acc, total = lax.fori_loop(
            0, counts[row], step, (jnp.zeros((HEAD_DIM, wide), F32), jnp.zeros((1, wide), F32))
        )
        total_ref[0, row] = total
        acc = (acc / total).astype(o_ref.dtype)
        for i in range(GROUP):
            o_ref[slots[head * GROUP + i], :, begin : begin + span] = acc[:, i * span : (i + 1) * span]


def attention_specs(query, keyvalue, first):
    slot_count, _, lanes = query.shape
    pack, _, wide = first.shape
    blocks = keyvalue.shape[0]
    whole = pl.BlockSpec((slot_count, HEAD_DIM, lanes), lambda g, *_: (0, 0, 0))
    keys = pl.BlockSpec((blocks, HEAD_DIM, lanes), lambda g, *_: (0, g, 0))
    values = pl.BlockSpec((blocks, HEAD_DIM, lanes), lambda g, *_: (0, KVH + g, 0))
    totals = pl.BlockSpec((1, pack, 1, wide), lambda g, *_: (g, 0, 0, 0))
    bounds = [
        pl.BlockSpec((pack, 1, wide), lambda g, *_: (0, 0, 0)),
        pl.BlockSpec((1, wide), lambda g, *_: (0, 0)),
    ]
    work = HEADS * lanes * blocks * (wide // GROUP)
    return whole, keys, values, totals, bounds, work


def attend(query, keyvalue, tables):
    order, counts, starts, slots, first, place = tables
    pack, _, wide = first.shape
    whole, keys, values, totals, bounds, work = attention_specs(query, keyvalue, first)
    spec = pltpu.PrefetchScalarGridSpec(
        num_scalar_prefetch=4,
        grid=(KVH,),
        in_specs=[whole, keys, values, *bounds],
        out_specs=[whole, totals],
    )
    return pl.pallas_call(
        attend_kernel,
        grid_spec=spec,
        out_shape=[jax.ShapeDtypeStruct(query.shape, BF16), jax.ShapeDtypeStruct((KVH, pack, 1, wide), F32)],
        compiler_params=pltpu.CompilerParams(dimension_semantics=("arbitrary",), vmem_limit_bytes=40 * 2**20),
        cost_estimate=pl.CostEstimate(flops=work * 1024, bytes_accessed=8 * 2**20, transcendentals=work),
        name="attend",
    )(order, counts, starts, slots, query, keyvalue, keyvalue, first, place)


def attend_back_kernel(
    order, counts, starts, slots, q_ref, g_ref, o_ref, k_ref, v_ref, total_ref, first_ref, place_ref,
    dq_ref, dkv_ref,
):
    head = pl.program_id(0)
    pack, _, wide = first_ref.shape
    span = wide // GROUP

    @pl.when(head == 0)
    def _():
        dq_ref[...] = jnp.zeros_like(dq_ref)

    dkv_ref[...] = jnp.zeros_like(dkv_ref)
    place = place_ref[...]
    for row in range(pack):
        begin = row * span
        query, grad, out = (stacked(ref, slots, head, begin, span) for ref in (q_ref, g_ref, o_ref))
        inner = jnp.sum(grad.astype(F32) * out.astype(F32), axis=0, keepdims=True)
        lift = jnp.log2(total_ref[0, row])
        first = first_ref[row]

        def step(i, acc):
            block = order[row, i]
            key, value = (ref[block, :, begin : begin + span] for ref in (k_ref, v_ref))
            scores = dot(key.T, query, (1, 0))
            keys = starts[block] + lax.broadcasted_iota(jnp.int32, scores.shape, 0)
            probs = jnp.where((keys >= first) & (keys <= place), jnp.exp2(scores * EXP2_SCALE - lift), 0.0)
            grad_probs = dot(value.T, grad, (1, 0))
            grad_scores = (probs * (grad_probs - inner)).astype(BF16)
            dkv_ref[block, 0, :, begin : begin + span] = (
                (dot(grad_scores, query, (1, 1)) * SCALE).T.astype(dkv_ref.dtype)
            )
            dkv_ref[block, 1, :, begin : begin + span] = (
                dot(probs.astype(BF16), grad, (1, 1)).T.astype(dkv_ref.dtype)
            )
            return acc + dot(key, grad_scores, (1, 0))

        acc = lax.fori_loop(0, counts[row], step, jnp.zeros((HEAD_DIM, wide), F32)) * SCALE
        for i in range(GROUP):
            dq_ref[slots[head * GROUP + i], :, begin : begin + span] = acc[:, i * span : (i + 1) * span]


def attend_back(query, grad, out, keyvalue, totals_in, tables):
    order, counts, starts, slots, first, place = tables
    whole, keys, values, totals, bounds, work = attention_specs(query, keyvalue, first)
    blocks, _, lanes = keyvalue.shape
    spec = pltpu.PrefetchScalarGridSpec(
        num_scalar_prefetch=4,
        grid=(KVH,),
        in_specs=[whole, whole, whole, keys, values, totals, *bounds],
        out_specs=[whole, pl.BlockSpec((blocks, 2, HEAD_DIM, lanes), lambda g, *_: (0, 0, g, 0))],
    )
    return pl.pallas_call(
        attend_back_kernel,
        grid_spec=spec,
        out_shape=[
            jax.ShapeDtypeStruct(query.shape, F32),
            jax.ShapeDtypeStruct((blocks, 2, KVH * HEAD_DIM, lanes), BF16),
        ],
        compiler_params=pltpu.CompilerParams(dimension_semantics=("arbitrary",), vmem_limit_bytes=48 * 2**20),
        cost_estimate=pl.CostEstimate(flops=work * 2560, bytes_accessed=16 * 2**20, transcendentals=work),
        name="attend_back",
    )(order, counts, starts, slots, query, grad, out, keyvalue, keyvalue, totals_in, first, place)


def strip_of(ref, index, strip):
    return ref[:, pl.ds(pl.multiple_of(index * strip, strip), strip)]


def rate_of(value):
    return lax.rsqrt(jnp.mean(value * value, axis=-1, keepdims=True) + EPSILON)


def norm_one_kernel(near, tokens_ref, gain_ref, normed_ref, near_ref):
    value = tokens_ref[...].astype(F32)
    normed_ref[...] = (value * rate_of(value) * gain_ref[...]).astype(BF16)
    strip = value.shape[1] // near.shape[0]
    for j in range(near.shape[0]):
        near_ref[:, j * strip : (j + 1) * strip] = strip_of(normed_ref, near[j], strip)


def norm_two_kernel(place, tokens_ref, attended_ref, gain_ref, residual_ref, normed_ref):
    strip = tokens_ref.shape[1] // place.shape[0]
    for i in range(place.shape[0]):
        columns = slice(i * strip, (i + 1) * strip)
        residual_ref[:, columns] = tokens_ref[:, columns].astype(F32) + strip_of(attended_ref, place[i], strip)
    value = residual_ref[...]
    normed_ref[...] = (value * rate_of(value) * gain_ref[...]).astype(BF16)


def norm_back(value, gain, grad):
    rate = rate_of(value)
    normed = value * rate
    scaled = grad * gain
    back = rate * (scaled - normed * jnp.mean(scaled * normed, axis=-1, keepdims=True))
    return back, jnp.sum(grad * normed, axis=0, keepdims=True)


def add_up(ref, value):
    @pl.when(pl.program_id(0) == 0)
    def _():
        ref[...] = jnp.zeros_like(ref)

    ref[...] += value


def back_two_kernel(near, grad_ref, residual_ref, cotangent_ref, gain_ref, out_ref, near_ref, gain_grad_ref):
    back, gain_grad = norm_back(residual_ref[...], gain_ref[...], grad_ref[...])
    out_ref[...] = cotangent_ref[...].astype(F32) + back
    add_up(gain_grad_ref, gain_grad)
    strip = grad_ref.shape[1] // near.shape[0]
    for j in range(near.shape[0]):
        near_ref[:, j * strip : (j + 1) * strip] = strip_of(out_ref, near[j], strip).astype(BF16)


def back_one_kernel(place, grad_ref, near_ref, tokens_ref, above_ref, gain_ref, out_ref, gain_grad_ref):
    strip = tokens_ref.shape[1] // place.shape[0]
    for i in range(place.shape[0]):
        columns = slice(i * strip, (i + 1) * strip)
        out_ref[:, columns] = grad_ref[:, columns] + strip_of(near_ref, place[i], strip)
    back, gain_grad = norm_back(tokens_ref[...].astype(F32), gain_ref[...], out_ref[...])
    out_ref[...] = above_ref[...] + back
    add_up(gain_grad_ref, gain_grad)


def by_tokens(kernel, table, arrays, gain, outs, gain_grad=False):
    tokens, width = arrays[0].shape
    block = tokens // 3
    tile = pl.BlockSpec((block, width), lambda i, *_: (i, 0))
    line = pl.BlockSpec((1, width), lambda i, *_: (0, 0))
    spec = pltpu.PrefetchScalarGridSpec(
        num_scalar_prefetch=1,
        grid=(3,),
        in_specs=[tile] * len(arrays) + [line],
        out_specs=[tile] * len(outs) + [line] * gain_grad,
    )
    shapes = [jax.ShapeDtypeStruct((tokens, width), t) for t in outs]
    shapes += [jax.ShapeDtypeStruct((1, width), F32)] * gain_grad
    return pl.pallas_call(
        kernel,
        grid_spec=spec,
        out_shape=shapes,
        compiler_params=pltpu.CompilerParams(dimension_semantics=("arbitrary",), vmem_limit_bytes=40 * 2**20),
        cost_estimate=pl.CostEstimate(flops=16 * tokens * width, bytes_accessed=16 * tokens * width, transcendentals=0),
    )(table, *arrays, gain[None, :])


def unfold_kernel(place, total_ref, key_ref, value_ref, small_ref):
    width = key_ref.shape[0]
    strip = total_ref.shape[1] // place.shape[0]
    for i in range(place.shape[0]):
        columns = slice(i * strip, (i + 1) * strip)
        block = strip_of(total_ref, place[i], strip).astype(F32)
        key_ref[:, columns] = block[:width]
        value_ref[:, columns] = block[width : 2 * width]
        small_ref[:, columns] = block[2 * width : 2 * width + 16]


def unfold(place, total, width):
    model = total.shape[1]
    spec = pltpu.PrefetchScalarGridSpec(
        num_scalar_prefetch=1,
        grid=(1,),
        in_specs=[pl.BlockSpec(total.shape, lambda i, *_: (0, 0))],
        out_specs=[
            pl.BlockSpec((width, model), lambda i, *_: (0, 0)),
            pl.BlockSpec((width, model), lambda i, *_: (0, 0)),
            pl.BlockSpec((16, model), lambda i, *_: (0, 0)),
        ],
    )
    return pl.pallas_call(
        unfold_kernel,
        grid_spec=spec,
        out_shape=[
            jax.ShapeDtypeStruct((width, model), F32),
            jax.ShapeDtypeStruct((width, model), F32),
            jax.ShapeDtypeStruct((16, model), F32),
        ],
        compiler_params=pltpu.CompilerParams(dimension_semantics=("arbitrary",), vmem_limit_bytes=40 * 2**20),
    )(place, total)


def head_forward(projected, gain, turn):
    cosine, sine = turn
    half = HEAD_DIM // 2
    rate = lax.rsqrt(jnp.mean(projected * projected, axis=1, keepdims=True) + EPSILON)
    value = projected * rate * gain[:, None]
    low, high = value[:, :half], value[:, half:]
    return jnp.concatenate([low * cosine - high * sine, low * sine + high * cosine], axis=1)


def head_back(projected, gain, turn, grad):
    cosine, sine = turn
    half = HEAD_DIM // 2
    low, high = grad[:, :half], grad[:, half:]
    grad = jnp.concatenate([low * cosine + high * sine, high * cosine - low * sine], axis=1)
    rate = lax.rsqrt(jnp.mean(projected * projected, axis=1, keepdims=True) + EPSILON)
    normed = projected * rate
    scaled = grad * gain[:, None]
    back = rate * (scaled - normed * jnp.mean(scaled * normed, axis=1, keepdims=True))
    return back, jnp.sum(grad * normed, axis=(0, 2))


def weight_grad_kernel(*refs):
    out_ref = refs[-1]
    count = len(refs) // 2
    total = sum(dot(refs[i][...], refs[count + i][...], (0, 0)) for i in range(count))
    out_ref[0] = total.astype(out_ref.dtype)


def weight_grad(values, grads, blocks):
    width, hidden = values[0].shape[1], grads[0].shape[1]
    block = width // blocks
    tokens = sum(v.shape[0] for v in values)
    return pl.pallas_call(
        weight_grad_kernel,
        grid=(blocks,),
        in_specs=[pl.BlockSpec((v.shape[0], block), lambda i: (0, i)) for v in values]
        + [pl.BlockSpec(g.shape, lambda i: (0, 0), pipeline_mode=pl.Buffered(1)) for g in grads],
        out_specs=pl.BlockSpec((1, block, hidden), lambda i: (i, 0, 0)),
        out_shape=jax.ShapeDtypeStruct((blocks, block, hidden), BF16),
        compiler_params=pltpu.CompilerParams(dimension_semantics=("arbitrary",), vmem_limit_bytes=56 * 2**20),
        cost_estimate=pl.CostEstimate(
            flops=2 * tokens * width * hidden, bytes_accessed=2 * tokens * (width + hidden), transcendentals=0
        ),
        name="weight_grad",
    )(*values, *grads)


def tall(tile, columns):
    return pl.BlockSpec((tile, columns), lambda i: (i, 0))


def held(weights, which=None):
    blocks = weights.shape[0] if which is None else weights.shape[0] // 2
    return pl.BlockSpec((blocks, *weights.shape[1:]), lambda i: (which or 0, 0, 0), pipeline_mode=pl.Buffered(1))


FFN_PARAMS = pltpu.CompilerParams(dimension_semantics=("arbitrary",), vmem_limit_bytes=56 * 2**20)


def matrix(ref):
    return ref[...].reshape(ref.shape[0] * ref.shape[1], ref.shape[2])


def forward_kernel(tokens_ref, gate_w, up_w, gate_ref, up_ref, hidden_ref):
    tokens = tokens_ref[...]
    gate, up = dot(tokens, matrix(gate_w), (1, 0)), dot(tokens, matrix(up_w), (1, 0))
    gate_ref[...] = gate
    up_ref[...] = up
    hidden_ref[...] = (gate / (1.0 + jnp.exp(-gate)) * up).astype(BF16)


def forward(tokens, gate_up, tile=256):
    count, width = tokens.shape
    hidden = gate_up.shape[2]
    return pl.pallas_call(
        forward_kernel,
        grid=(count // tile,),
        in_specs=[tall(tile, width), held(gate_up, 0), held(gate_up, 1)],
        out_specs=[tall(tile, hidden)] * 3,
        out_shape=[jax.ShapeDtypeStruct((count, hidden), t) for t in (F32, F32, BF16)],
        compiler_params=FFN_PARAMS,
        cost_estimate=pl.CostEstimate(
            flops=4 * count * width * hidden,
            bytes_accessed=4 * width * hidden + 2 * count * width + 10 * count * hidden,
            transcendentals=count * hidden,
        ),
        name="forward",
    )(tokens, gate_up, gate_up)


def hidden_back_kernel(grad_ref, gate_ref, up_ref, down_w, gate_w, up_w, gate_grad_ref, up_grad_ref, part_ref):
    grad = dot(grad_ref[...], matrix(down_w), (1, 0))
    gate = gate_ref[...]
    sigmoid = 1.0 / (1.0 + jnp.exp(-gate))
    gate_grad = (grad * up_ref[...] * sigmoid * (1.0 + gate * (1.0 - sigmoid))).astype(BF16)
    up_grad = (grad * gate * sigmoid).astype(BF16)
    gate_grad_ref[...] = gate_grad
    up_grad_ref[...] = up_grad
    part_ref[...] = (dot(gate_grad, matrix(gate_w), (1, 1)) + dot(up_grad, matrix(up_w), (1, 1))).astype(BF16)


def hidden_back(grad, gate, up, down_w, gate_up, tile=256):
    count, width = grad.shape
    hidden = gate.shape[1]
    return pl.pallas_call(
        hidden_back_kernel,
        grid=(count // tile,),
        in_specs=[
            tall(tile, width), tall(tile, hidden), tall(tile, hidden), held(down_w), held(gate_up, 0), held(gate_up, 1)
        ],
        out_specs=[tall(tile, hidden), tall(tile, hidden), tall(tile, width)],
        out_shape=[jax.ShapeDtypeStruct((count, n), BF16) for n in (hidden, hidden, width)],
        compiler_params=FFN_PARAMS,
        cost_estimate=pl.CostEstimate(
            flops=6 * count * width * hidden,
            bytes_accessed=6 * width * hidden + 16 * count * hidden,
            transcendentals=count * hidden,
        ),
        name="hidden_back",
    )(grad, gate, up, down_w, gate_up, gate_up)


def down_kernel(hidden_ref, down_w, out_ref):
    out_ref[...] = dot(hidden_ref[...], matrix(down_w), (1, 1)).astype(BF16)


def down_product(hidden, down_w, tile=256):
    count, size = hidden.shape
    width = down_w.shape[0] * down_w.shape[1]
    return pl.pallas_call(
        down_kernel,
        grid=(count // tile,),
        in_specs=[tall(tile, size), held(down_w)],
        out_specs=tall(tile, width),
        out_shape=jax.ShapeDtypeStruct((count, width), BF16),
        compiler_params=FFN_PARAMS,
        cost_estimate=pl.CostEstimate(
            flops=2 * count * width * size,
            bytes_accessed=2 * width * size + 2 * count * (width + size),
            transcendentals=0,
        ),
        name="down_product",
    )(hidden, down_w)


def paired():
    return lax.axis_size("tp") == 2 and lax.axis_size("row") == 2


def plane_sum(value):
    return lax.psum_scatter(value, ("row", "core", "tp"), scatter_dimension=0, tiled=True)


def both_cores(chunk):
    return jnp.concatenate([chunk, swap(chunk, "core")])


def other_half(part):
    return part[part.shape[0] // 2 :]


def own_half(part, got):
    return part[: part.shape[0] // 2].astype(F32) + got.astype(F32)


def far_hops(far):
    middle = far.shape[0] // 2
    return swap(far[:middle], "row"), swap(far[middle:], "tp")


def near_sends(near, hop_y, hop_x):
    half = near.shape[0] // 2
    return (
        (near[:half] + hop_y[half:].astype(F32)).astype(BF16),
        (near[half:] + hop_x[half:].astype(F32)).astype(BF16),
    )


def plane_total(own, hop_y, hop_x, top_x, bottom_y):
    half = own.shape[0] // 2
    return own + jnp.concatenate(
        [hop_y[:half].astype(F32) + top_x.astype(F32), hop_x[:half].astype(F32) + bottom_y.astype(F32)]
    )


def stage(*values):
    return lax.optimization_barrier(values)


def body(
    tokens, cotangent, lengths, head_counts, norm1_gain, norm2_gain, q_gain, k_gain,
    w_query, w_key, w_value, w_out, w_gate, w_up, w_down,
):
    pack, span, width = tokens.shape
    rows, cores, ctx, tp = (lax.axis_size(a) for a in ("row", "core", "ctx", "tp"))
    own_tokens = pack * span
    slot_count = w_query.shape[1] // HEAD_DIM
    all_slots = slot_count * tp
    devices = rows * cores * ctx
    strip = width // devices
    row_index, core_index, ctx_index, tp_index = (lax.axis_index(a) for a in ("row", "core", "ctx", "tp"))

    plane = rows * cores

    def ordered(mine, other, index):
        first = index == 0
        return jnp.where(first, mine, other), jnp.where(first, other, mine)

    part = w_gate.shape[1] // plane
    down_turned = w_down.T

    def first_hop(pick):
        mine = jnp.stack([pick(r, core_index) for r in range(rows)])
        return mine, swap(jnp.stack([pick(r, 1 - core_index) for r in range(rows)]), "core")

    def second_hop(mine, got):
        both = ordered(mine, got, core_index)
        mine = jnp.stack([lax.dynamic_index_in_dim(x, row_index, 0, False) for x in both])
        got = swap(jnp.stack([lax.dynamic_index_in_dim(x, 1 - row_index, 0, False) for x in both]), "row")
        low, high = ordered(mine, got, row_index)
        return jnp.concatenate([low, high])

    def pick_columns(r, c):
        return jnp.concatenate(
            [lax.dynamic_slice_in_dim(w, (r * cores + c) * part, part, 1) for w in (w_gate, w_up, down_turned)]
        )

    def by_weight(blocks, first, last):
        return jnp.concatenate([blocks[:, i * strip : (i + 1) * strip] for i in range(first, last)])

    def row_out(grad):
        view = grad.reshape(rows, cores, *grad.shape[1:])
        mine = lax.dynamic_index_in_dim(view, row_index, 0, False)
        got = swap(lax.dynamic_index_in_dim(view, 1 - row_index, 0, False), "row")
        return jnp.stack(ordered(mine, got, row_index))

    def core_out(both):
        mine = lax.dynamic_index_in_dim(both, core_index, 1, False)
        got = swap(lax.dynamic_index_in_dim(both, 1 - core_index, 1, False), "core")
        low, high = ordered(mine, got, core_index)
        return [x for r in range(rows) for x in (low[r], high[r])]

    def from_tp(value, axis):
        if tp == 2:
            return join(value, "tp", axis)
        return lax.all_gather(value, "tp", axis=axis, tiled=True)

    def up(value):
        return lax.ppermute(value, "ctx", [(i, i + 1) for i in range(ctx - 1)])

    def beside(value):
        if tp == 2:
            return jnp.stack([value, swap(value, "tp")])
        return lax.all_gather(value, "tp", axis=0)

    length = span * tp * ctx
    first_end = lengths[:, 0:1]
    second_end = first_end + lengths[:, 1:2]
    own_start = (ctx_index * tp + tp_index) * span
    places = own_start + jnp.arange(span, dtype=jnp.int32)[None, :]
    begins = jnp.where(places >= second_end, second_end, jnp.where(places >= first_end, first_end, 0))
    angles_of = (places - begins).astype(F32)
    frequency = jnp.exp(jnp.arange(HEAD_DIM // 2).astype(F32) * (-2.0 * math.log(THETA) / HEAD_DIM))
    angles = frequency[:, None] * angles_of.reshape(1, own_tokens)
    turn = (jnp.cos(angles), jnp.sin(angles))
    offsets = [jnp.int32(0)]
    for i in range(tp):
        offsets.append(offsets[-1] + head_counts[i])
    heads = jnp.arange(HEADS, dtype=jnp.int32)
    slots = jnp.zeros((HEADS,), jnp.int32)
    for i in range(tp):
        inside = (heads >= offsets[i]) & (heads < offsets[i + 1])
        holder = jnp.bitwise_xor(i, tp_index) if tp == 2 else i
        slots = jnp.where(inside, holder * slot_count + heads - offsets[i], slots)
    ranks = jnp.arange(devices, dtype=jnp.int32)
    near_strips = (
        (jnp.bitwise_xor(ranks // ctx % rows, row_index) * cores + jnp.bitwise_xor(ranks // (ctx * rows), core_index))
        * ctx + jnp.bitwise_xor(ranks % ctx, ctx_index)
    )
    strip_places = (
        (jnp.bitwise_xor(ranks // ctx % cores, core_index) * rows + jnp.bitwise_xor(ranks // (ctx * cores), row_index))
        * ctx + jnp.bitwise_xor(ranks % ctx, ctx_index)
    )
    blocks = ctx * tp
    steps = jnp.arange(blocks, dtype=jnp.int32) // tp
    partner = jnp.arange(blocks, dtype=jnp.int32) % tp
    if tp == 2:
        partner = jnp.bitwise_xor(partner, tp_index)
    starts = ((ctx_index - steps) * tp + partner) * span
    seen = (starts[None, :] >= 0) & (starts[None, :] <= own_start) & (starts[None, :] + span > begins[:, :1])
    counts = jnp.sum(seen.astype(jnp.int32), axis=1)
    turns = jnp.sum(
        (seen[:, None, :] & (jnp.arange(blocks)[None, None, :] < jnp.arange(blocks)[None, :, None])).astype(jnp.int32),
        axis=2,
    )
    order = jnp.sum(
        jnp.where(
            seen[:, None, :] & (turns[:, None, :] == jnp.arange(blocks)[None, :, None]),
            jnp.arange(blocks, dtype=jnp.int32)[None, None, :],
            0,
        ),
        axis=2,
    )
    tables = (
        order,
        counts,
        starts,
        slots,
        jnp.concatenate([begins] * GROUP, axis=1)[:, None, :],
        jnp.concatenate([places] * GROUP, axis=1),
    )

    half = own_tokens // 2
    two = paired()
    key_value = jnp.concatenate([w_key, w_value], axis=1)
    flat = tokens.reshape(own_tokens, width)
    grad_low = cotangent.reshape(own_tokens, width)
    normed_one, normed_near = by_tokens(norm_one_kernel, near_strips, [flat], norm1_gain, [BF16, BF16])
    kv_width = KVH * HEAD_DIM
    projected = dot(key_value, normed_one, (0, 1))
    key_proj = projected[:kv_width].reshape(KVH, HEAD_DIM, own_tokens)
    key_low = head_forward(key_proj, k_gain, turn).astype(BF16).reshape(kv_width, own_tokens)
    own_kv = jnp.concatenate([key_low, projected[kv_width:].astype(BF16)])

    mine, got = first_hop(pick_columns)
    query_part = join(w_query, "ctx", 0)
    out_part = join(w_out, "ctx", 1)
    got, query_part, out_part, own_kv = stage(got, query_part, out_part, own_kv)

    packed = second_hop(mine, got)
    gate_up, packed = by_weight(packed, 0, 2), by_weight(packed, 2, 3)
    going, arrived = up(own_kv), [beside(own_kv)]
    query_part = join(query_part, "ctx", 0, 2)
    packed, gate_up, going, arrived[0], query_part = stage(packed, gate_up, going, arrived[0], query_part)
    gate_up = lax.all_gather(gate_up, "ctx", axis=1, tiled=True)

    arrived.append(beside(going))
    going = up(going)
    query_part = join(query_part, "row", 0)
    going, arrived[1], query_part, packed = stage(going, arrived[1], query_part, packed)

    arrived.append(beside(going))
    going = up(going)
    query_part = from_tp(query_part, 1)
    out_part = join(out_part, "ctx", 1, 2)
    going, arrived[2], query_part, out_part, packed = stage(going, arrived[2], query_part, out_part, packed)

    arrived.append(beside(going))
    query_full = join(query_part, "core", 0)
    out_part = join(out_part, "row", 1)
    arrived[3], query_full, out_part, packed = stage(arrived[3], query_full, out_part, packed)
    keyvalue = jnp.concatenate(arrived)

    query_proj = dot(query_full, normed_near, (0, 1)).reshape(all_slots, HEAD_DIM, own_tokens)
    query_low = head_forward(query_proj, q_gain, turn).astype(BF16)
    out_low, totals = attend(query_low, keyvalue, tables)
    out_part = from_tp(out_part, 0)
    top, bottom = grad_low[:half], grad_low[half:]
    grad_near = (swap(top, "tp"), swap(bottom, "row")) if two else (top, bottom)
    out_low, totals, out_part, grad_near, packed, gate_up = stage(
        out_low, totals, out_part, grad_near, packed, gate_up
    )
    down_full = lax.all_gather(packed, "ctx", axis=1, tiled=True)
    out_full = join(out_part, "core", 1)
    out_flat = out_low.reshape(all_slots * HEAD_DIM, own_tokens)
    attended = dot(out_flat, out_full, (0, 0))
    residual, normed_two = by_tokens(norm_two_kernel, strip_places, [flat, attended], norm2_gain, [F32, BF16])
    normed_two, residual, out_full = stage(normed_two, residual, out_full)

    if two:
        top, bottom = normed_two[:half], normed_two[half:]
        near = swap(top, "tp"), swap(bottom, "row")
        other = swap(normed_two, "core")
        near, other = stage(near, other)
        far = swap(jnp.concatenate([top, near[0]]), "row"), swap(jnp.concatenate([bottom, near[1]]), "tp")
        near = jnp.concatenate(near)
        normed_all = [jnp.concatenate([normed_two, other, near, swap(near, "core")])]
        near = jnp.concatenate(grad_near)
        grad_all = [jnp.concatenate([grad_low, swap(grad_low, "core"), near, swap(near, "core")])]
        ready = [forward(normed_all[0], gate_up)]
        far, normed_all, grad_all, ready, down_full = stage(far, normed_all, grad_all, ready, down_full)
        top, bottom = grad_low[:half], grad_low[half:]
        normed_all.append(both_cores(jnp.concatenate(far)))
        ready.append(forward(normed_all[1], gate_up))
        grad_far = (
            swap(jnp.concatenate([top, grad_near[0]]), "row"), swap(jnp.concatenate([bottom, grad_near[1]]), "tp")
        )
        ready, grad_far, grad_all, normed_all = stage(ready, grad_far, grad_all, normed_all)
        grad_all.append(both_cores(jnp.concatenate(grad_far)))
    else:
        normed_all = [lax.all_gather(normed_two, ("row", "core", "tp"), axis=0, tiled=True)]
        grad_all = [lax.all_gather(grad_low, ("row", "core", "tp"), axis=0, tiled=True)]
        ready = [forward(normed_all[0], gate_up)]
    chunks = range(len(normed_all))
    hidden = [x[2] for x in ready]

    def backward(i):
        return hidden_back(grad_all[i], ready[i][0], ready[i][1], down_full, gate_up)

    def output_part(i):
        return down_product(hidden[i], down_full)

    def scattered(gradient):
        return lax.psum_scatter(gradient, "ctx", scatter_dimension=1, tiled=True)

    if two:
        far_grads = backward(1)
        far_grads, far_send, grad_all = stage(far_grads, other_half(far_grads[2]), grad_all)
        far = own_half(far_grads[2], swap(far_send, "core")).astype(BF16)
        far_part = output_part(1)
        far, grad_all, far_part = stage(far, grad_all, far_part)
        hops = far_hops(far)
        near_grads = backward(0)
        output_far = own_half(far_part, swap(other_half(far_part), "core")).astype(BF16)
        hops, near_grads, hidden, output_far = stage(hops, near_grads, hidden, output_far)
        grads = [near_grads, far_grads]
        own_part, near_part = near_grads[2][: 2 * own_tokens], near_grads[2][2 * own_tokens :]
        near = own_half(near_part, swap(other_half(near_part), "core"))
        own = own_half(own_part, swap(other_half(own_part), "core"))
        sends = near_sends(near, *hops)
        sends, own, normed_all, hidden, grad_all = stage(sends, own, normed_all, hidden, grad_all)
        top_x, bottom_y = swap(sends[0], "tp"), swap(sends[1], "row")
        grad_down = weight_grad(grad_all, hidden, plane)
        top_x, bottom_y, output_far, grads, normed_all, grad_down = stage(
            top_x, bottom_y, output_far, grads, normed_all, grad_down
        )
        output_hops = far_hops(output_far)
        grad_normed_two = plane_total(own, *hops, top_x, bottom_y)
    else:
        grads = [backward(0)]
        grad_down = weight_grad(grad_all, hidden, plane)
        grad_normed_two = plane_sum(grads[0][2]).astype(F32)
        output_hops = grad_normed_two
    grad_down = scattered(grad_down)
    grad_residual, grad_attn, grad_norm_two = by_tokens(
        back_two_kernel, near_strips, [grad_normed_two, residual, grad_low], norm2_gain, [F32, BF16], True
    )

    grad_out = dot(out_full, grad_attn, (1, 1)).astype(BF16).reshape(all_slots, HEAD_DIM, own_tokens)
    grad_query, grad_kv = attend_back(query_low, grad_out, out_low, keyvalue, totals, tables)
    grad_out_w = dot(out_flat, grad_attn, (1, 0)).astype(BF16)
    grad_out_w = fold(grad_out_w, "core", 1)
    output_hops, grad_query, grad_kv, grads, grad_out_w, normed_all, hidden = stage(
        output_hops, grad_query, grad_kv, grads, grad_out_w, normed_all, hidden
    )
    grad_kv = grad_kv.reshape(ctx, tp, 2 * kv_width, own_tokens)

    def to_tp(value, axis):
        if tp == 2:
            return fold(value, "tp", axis)
        return lax.psum_scatter(value, "tp", scatter_dimension=axis, tiled=True)

    def to_owner(value):
        if tp == 2:
            return value[0].astype(F32) + swap(value[1], "tp").astype(F32)
        return lax.psum_scatter(value, "tp", scatter_dimension=0, tiled=False).astype(F32)

    def down(value):
        return lax.ppermute(value.astype(BF16), "ctx", [(j, j - 1) for j in range(1, ctx)]).astype(F32)

    summed = to_owner(grad_kv[ctx - 1])
    grad_gate_w = weight_grad(normed_all, [g[0] for g in grads], plane)
    out_w_low, out_w_high = grad_out_w[: all_slots * 32], grad_out_w[all_slots * 32 :]
    out_w_low = fold(out_w_low, "row", 1)
    summed, grad_kv, grad_query, out_w_low, out_w_high, normed_all, grads, grad_gate_w, grad_down = stage(
        summed, grad_kv, grad_query, out_w_low, out_w_high, normed_all, grads, grad_gate_w, grad_down
    )

    summed = to_owner(grad_kv[2]) + down(summed)
    out_w_high = fold(out_w_high, "row", 1)
    summed, grad_kv, grad_query, out_w_low, out_w_high, grad_gate_w, grad_down = stage(
        summed, grad_kv, grad_query, out_w_low, out_w_high, grad_gate_w, grad_down
    )

    summed = to_owner(grad_kv[1]) + down(summed)
    grad_query_proj, grad_q_gain = head_back(query_proj, q_gain, turn, grad_query)
    grad_query_low = grad_query_proj.astype(BF16).reshape(all_slots * HEAD_DIM, own_tokens)
    grad_down = row_out(grad_down)
    summed, grad_query_low, grad_q_gain, grad_kv, grad_down, out_w_low, out_w_high, grad_gate_w = stage(
        summed, grad_query_low, grad_q_gain, grad_kv, grad_down, out_w_low, out_w_high, grad_gate_w
    )
    grad_gate_w = scattered(grad_gate_w)

    summed = to_owner(grad_kv[0]) + down(summed)
    grad_query_w = dot(normed_near, grad_query_low, (0, 1)).astype(BF16)
    grad_query_w = fold(grad_query_w, "core", 0)
    grad_normed_near = dot(grad_query_low, query_full, (0, 1))
    grad_down = core_out(grad_down)
    summed, grad_query_w, grad_normed_near, grad_down, out_w_low, out_w_high, normed_all, grads, hidden = stage(
        summed, grad_query_w, grad_normed_near, grad_down, out_w_low, out_w_high, normed_all, grads, hidden
    )

    grad_key_proj, grad_k_gain = head_back(
        key_proj, k_gain, turn, summed[:kv_width].reshape(KVH, HEAD_DIM, own_tokens)
    )
    grad_kv_low = jnp.concatenate(
        [grad_key_proj.reshape(kv_width, own_tokens).astype(BF16), summed[kv_width:].astype(BF16)]
    )
    padded = jnp.pad(grad_kv_low, ((0, 32), (0, 0)))
    total = dot(padded, normed_near if two else normed_one, (1, 0))
    grad_normed_one = dot(grad_kv_low, key_value, (0, 1))
    grad_inputs, grad_norm_one = by_tokens(
        back_one_kernel, strip_places, [grad_normed_one, grad_normed_near, flat, grad_residual], norm1_gain, [F32], True
    )
    gains = jnp.concatenate([grad_q_gain, grad_k_gain, jnp.zeros((width - 2 * HEAD_DIM,), F32)])
    small = jnp.concatenate([grad_norm_one, grad_norm_two, gains[None]])
    moved = (near_strips if two else ranks)[:, None] == ranks[None, :]
    small = jnp.sum(
        jnp.where(moved[None, :, :, None], small.reshape(3, 1, devices, strip), 0.0), axis=2
    ).reshape(3, width)
    total = lax.dynamic_update_slice(total, small, (2 * kv_width, 0)).astype(BF16)
    query_w = fold(grad_query_w[:, : all_slots * 32], "row", 0), grad_query_w[:, all_slots * 32 :]
    grad_out_w = to_tp(jnp.concatenate([out_w_low, out_w_high]), 0)
    total, query_w, grad_out_w, hidden, normed_all, grads = stage(
        total, query_w, grad_out_w, hidden, normed_all, grads
    )

    def along(value, bit):
        got = swap(value, "ctx", bit)
        return sum32(
            value, jnp.concatenate([got[:, (j ^ bit) * strip : ((j ^ bit) + 1) * strip] for j in range(ctx)], axis=1)
        )

    if not two:
        total = lax.psum(total, ("row", "core", "ctx", "tp"))
        output = residual + plane_sum(output_part(0)).astype(F32)
        grad_up_w = scattered(weight_grad(normed_all, [g[1] for g in grads], plane))
        query_w = jnp.concatenate([query_w[0], fold(query_w[1], "row", 0)], axis=1)
        grad_query_w = fold(fold(to_tp(query_w, 1), "ctx", 0, 2), "ctx", 0)
        grad_out_w = fold(fold(grad_out_w, "ctx", 1, 2), "ctx", 1)
        grad_up_w, grad_gate_w = core_out(row_out(grad_up_w)), core_out(row_out(grad_gate_w))
    else:
        total = fold(total, "core", 1)
        total, query_w, grad_out_w, hidden, normed_all, grads = stage(
            total, query_w, grad_out_w, hidden, normed_all, grads
        )
        size = total.shape[0] // 2
        got = swap(lax.dynamic_slice_in_dim(total, (1 - tp_index) * size, size, 0), "tp")
        total = sum32(lax.dynamic_slice_in_dim(total, tp_index * size, size, 0), got)
        query_w = jnp.concatenate([query_w[0], fold(query_w[1], "row", 0)], axis=1)
        grad_up_w = weight_grad(normed_all, [g[1] for g in grads], plane)
        total, grad_out_w, query_w, hidden, grad_up_w, grad_gate_w = stage(
            total, grad_out_w, query_w, hidden, grad_up_w, grad_gate_w
        )
        grad_up_w = scattered(grad_up_w)
        total = fold(total, "row", 1)
        query_w = fold(query_w, "tp", 1)
        near_part = output_part(0)
        own_part, near_part = near_part[: 2 * own_tokens], near_part[2 * own_tokens :]
        near = own_half(near_part, swap(other_half(near_part), "core"))
        own = own_half(own_part, swap(other_half(own_part), "core"))
        sends = near_sends(near, *output_hops)
        total, query_w, sends, own, grad_gate_w, grad_out_w = stage(
            total, query_w, sends, own, grad_gate_w, grad_out_w
        )
        total = along(total, 1)
        top_x, bottom_y = swap(sends[0], "tp"), swap(sends[1], "row")
        grad_out_w = fold(grad_out_w, "ctx", 1, 2)
        total, query_w, grad_gate_w, top_x, bottom_y, grad_out_w = stage(
            total, query_w, grad_gate_w, top_x, bottom_y, grad_out_w
        )
        total = along(total, 2)
        output = residual + plane_total(own, *output_hops, top_x, bottom_y)
        grad_gate_w = row_out(grad_gate_w)
        grad_out_w = fold(grad_out_w, "ctx", 1)
        total, query_w, grad_gate_w, grad_out_w, output = stage(total, query_w, grad_gate_w, grad_out_w, output)
        total = join(total, "row", 1)
        query_w = fold(query_w, "ctx", 0, 2)
        grad_gate_w = core_out(grad_gate_w)
        total, grad_up_w, query_w, grad_gate_w = stage(total, grad_up_w, query_w, grad_gate_w)
        other = swap(total, "tp")
        grad_query_w = fold(query_w, "ctx", 0)
        grad_up_w = row_out(grad_up_w)
        first = tp_index == 0
        total = jnp.concatenate([jnp.where(first, total, other), jnp.where(first, other, total)])
        total, grad_up_w, grad_query_w = stage(total, grad_up_w, grad_query_w)
        total = join(total, "core", 1)
        grad_up_w = core_out(grad_up_w)
    grad_key_w, grad_value_w, small = unfold(strip_places if two else ranks, total, kv_width)

    return (
        output.astype(BF16).reshape(pack, span, width),
        grad_inputs.reshape(pack, span, width),
        small[0],
        small[1],
        small[2, :HEAD_DIM],
        small[2, HEAD_DIM : 2 * HEAD_DIM],
        grad_query_w.astype(F32),
        grad_key_w.T,
        grad_value_w.T,
        grad_out_w.astype(F32),
        jnp.concatenate(grad_gate_w, axis=1).astype(F32),
        jnp.concatenate(grad_up_w, axis=1).astype(F32),
        jnp.concatenate([x.T for x in grad_down]).astype(F32),
    )


def solution(mesh):
    dp, ctx, tp = (mesh.shape[a] for a in ("dp", "ctx", "tp"))
    split = Mesh(mesh.devices.reshape(dp // 2, 2, ctx, tp), ("row", "core", "ctx", "tp"))
    dp = ("row", "core")
    every = ("row", "core", "ctx")
    token = P(dp, ("ctx", "tp"), None)
    by_row, by_column = P(every, "tp"), P("tp", every)
    return jax.shard_map(
        body,
        mesh=split,
        in_specs=(
            token, token, P(dp, None), P(), P(), P(), P(), P(),
            by_row, P(), P(), by_column, by_row, by_row, by_column,
        ),
        out_specs=(
            token, token, P(), P(), P(), P(),
            by_row, P(), P(), by_column, by_row, by_row, by_column,
        ),
        check_vma=False,
    )
```

```python
import math

import jax
import jax.numpy as jnp
from jax import lax
from jax.experimental import pallas as pl
from jax.experimental.pallas import tpu as pltpu
from jax.sharding import Mesh
from jax.sharding import PartitionSpec as P

HEADS = 20
KVH = 5
HEAD_DIM = 64
GROUP = HEADS // KVH

EPSILON = 1e-05
THETA = 10000.0
SCALE = HEAD_DIM ** (-0.5)
EXP2_SCALE = SCALE / math.log(2.0)

BF16 = jnp.bfloat16
F32 = jnp.float32


def dot(left, right, contract):
    return lax.dot_general(left, right, ((contract[:1], contract[1:]), ((), ())), preferred_element_type=F32)


def swap(value, axis, bit=1):
    size = lax.axis_size(axis)
    return lax.ppermute(value, axis, [(i, i ^ bit) for i in range(size)])


def join(value, axis, dimension, bit=1):
    return jnp.concatenate([value, swap(value, axis, bit)], axis=dimension)


def fold(value, axis, dimension, bit=1):
    size = value.shape[dimension] // 2
    got = swap(lax.slice_in_dim(value, size, 2 * size, axis=dimension), axis, bit)
    return sum32(lax.slice_in_dim(value, 0, size, axis=dimension), got)


def sum32(left, right):
    return (left.astype(F32) + right.astype(F32)).astype(BF16)


def stacked(ref, slots, head, begin, span):
    return jnp.concatenate(
        [ref[slots[head * GROUP + i], :, begin : begin + span] for i in range(GROUP)], axis=1
    )


def attend_kernel(
    order, counts, starts, slots, q_ref, k_ref, v_ref, first_ref, place_ref, o_ref, total_ref
):
    head = pl.program_id(0)
    pack, _, wide = first_ref.shape
    span = wide // GROUP

    @pl.when(head == 0)
    def _():
        o_ref[...] = jnp.zeros_like(o_ref)

    place = place_ref[...]
    for row in range(pack):
        begin = row * span
        query = stacked(q_ref, slots, head, begin, span)
        first = first_ref[row]

        def step(i, carry):
            acc, total = carry
            block = order[row, i]
            scores = dot(k_ref[block, :, begin : begin + span].T, query, (1, 0))
            keys = starts[block] + lax.broadcasted_iota(jnp.int32, scores.shape, 0)
            weight = jnp.where((keys >= first) & (keys <= place), jnp.exp2(scores * EXP2_SCALE), 0.0)
            total = total + jnp.sum(weight, axis=0, keepdims=True)
            acc = acc + dot(v_ref[block, :, begin : begin + span], weight.astype(BF16), (1, 0))
            return acc, total

        acc, total = lax.fori_loop(
            0, counts[row], step, (jnp.zeros((HEAD_DIM, wide), F32), jnp.zeros((1, wide), F32))
        )
        total_ref[0, row] = total
        acc = (acc / total).astype(o_ref.dtype)
        for i in range(GROUP):
            o_ref[slots[head * GROUP + i], :, begin : begin + span] = acc[:, i * span : (i + 1) * span]


def attention_specs(query, keyvalue, first):
    slot_count, _, lanes = query.shape
    pack, _, wide = first.shape
    blocks = keyvalue.shape[0]
    whole = pl.BlockSpec((slot_count, HEAD_DIM, lanes), lambda g, *_: (0, 0, 0))
    keys = pl.BlockSpec((blocks, HEAD_DIM, lanes), lambda g, *_: (0, g, 0))
    values = pl.BlockSpec((blocks, HEAD_DIM, lanes), lambda g, *_: (0, KVH + g, 0))
    totals = pl.BlockSpec((1, pack, 1, wide), lambda g, *_: (g, 0, 0, 0))
    bounds = [
        pl.BlockSpec((pack, 1, wide), lambda g, *_: (0, 0, 0)),
        pl.BlockSpec((1, wide), lambda g, *_: (0, 0)),
    ]
    work = HEADS * lanes * blocks * (wide // GROUP)
    return whole, keys, values, totals, bounds, work


def attend(query, keyvalue, tables):
    order, counts, starts, slots, first, place = tables
    pack, _, wide = first.shape
    whole, keys, values, totals, bounds, work = attention_specs(query, keyvalue, first)
    spec = pltpu.PrefetchScalarGridSpec(
        num_scalar_prefetch=4,
        grid=(KVH,),
        in_specs=[whole, keys, values, *bounds],
        out_specs=[whole, totals],
    )
    return pl.pallas_call(
        attend_kernel,
        grid_spec=spec,
        out_shape=[jax.ShapeDtypeStruct(query.shape, BF16), jax.ShapeDtypeStruct((KVH, pack, 1, wide), F32)],
        compiler_params=pltpu.CompilerParams(dimension_semantics=("arbitrary",), vmem_limit_bytes=40 * 2**20),
        cost_estimate=pl.CostEstimate(flops=work * 1024, bytes_accessed=8 * 2**20, transcendentals=work),
        name="attend",
    )(order, counts, starts, slots, query, keyvalue, keyvalue, first, place)


def attend_back_kernel(
    order, counts, starts, slots, q_ref, g_ref, o_ref, k_ref, v_ref, total_ref, first_ref, place_ref,
    dq_ref, dkv_ref,
):
    head = pl.program_id(0)
    pack, _, wide = first_ref.shape
    span = wide // GROUP

    @pl.when(head == 0)
    def _():
        dq_ref[...] = jnp.zeros_like(dq_ref)

    dkv_ref[...] = jnp.zeros_like(dkv_ref)
    place = place_ref[...]
    for row in range(pack):
        begin = row * span
        query, grad, out = (stacked(ref, slots, head, begin, span) for ref in (q_ref, g_ref, o_ref))
        inner = jnp.sum(grad.astype(F32) * out.astype(F32), axis=0, keepdims=True)
        lift = jnp.log2(total_ref[0, row])
        first = first_ref[row]

        def step(i, acc):
            block = order[row, i]
            key, value = (ref[block, :, begin : begin + span] for ref in (k_ref, v_ref))
            scores = dot(key.T, query, (1, 0))
            keys = starts[block] + lax.broadcasted_iota(jnp.int32, scores.shape, 0)
            probs = jnp.where((keys >= first) & (keys <= place), jnp.exp2(scores * EXP2_SCALE - lift), 0.0)
            grad_probs = dot(value.T, grad, (1, 0))
            grad_scores = (probs * (grad_probs - inner)).astype(BF16)
            dkv_ref[block, 0, :, begin : begin + span] = (
                (dot(grad_scores, query, (1, 1)) * SCALE).T.astype(dkv_ref.dtype)
            )
            dkv_ref[block, 1, :, begin : begin + span] = (
                dot(probs.astype(BF16), grad, (1, 1)).T.astype(dkv_ref.dtype)
            )
            return acc + dot(key, grad_scores, (1, 0))

        acc = lax.fori_loop(0, counts[row], step, jnp.zeros((HEAD_DIM, wide), F32)) * SCALE
        for i in range(GROUP):
            dq_ref[slots[head * GROUP + i], :, begin : begin + span] = acc[:, i * span : (i + 1) * span]


def attend_back(query, grad, out, keyvalue, totals_in, tables):
    order, counts, starts, slots, first, place = tables
    whole, keys, values, totals, bounds, work = attention_specs(query, keyvalue, first)
    blocks, _, lanes = keyvalue.shape
    spec = pltpu.PrefetchScalarGridSpec(
        num_scalar_prefetch=4,
        grid=(KVH,),
        in_specs=[whole, whole, whole, keys, values, totals, *bounds],
        out_specs=[whole, pl.BlockSpec((blocks, 2, HEAD_DIM, lanes), lambda g, *_: (0, 0, g, 0))],
    )
    return pl.pallas_call(
        attend_back_kernel,
        grid_spec=spec,
        out_shape=[
            jax.ShapeDtypeStruct(query.shape, F32),
            jax.ShapeDtypeStruct((blocks, 2, KVH * HEAD_DIM, lanes), BF16),
        ],
        compiler_params=pltpu.CompilerParams(dimension_semantics=("arbitrary",), vmem_limit_bytes=48 * 2**20),
        cost_estimate=pl.CostEstimate(flops=work * 2560, bytes_accessed=16 * 2**20, transcendentals=work),
        name="attend_back",
    )(order, counts, starts, slots, query, grad, out, keyvalue, keyvalue, totals_in, first, place)


def strip_of(ref, index, strip):
    return ref[:, pl.ds(pl.multiple_of(index * strip, strip), strip)]


def rate_of(value):
    return lax.rsqrt(jnp.mean(value * value, axis=-1, keepdims=True) + EPSILON)


def norm_one_kernel(near, tokens_ref, gain_ref, normed_ref, near_ref):
    value = tokens_ref[...].astype(F32)
    normed_ref[...] = (value * rate_of(value) * gain_ref[...]).astype(BF16)
    strip = value.shape[1] // near.shape[0]
    for j in range(near.shape[0]):
        near_ref[:, j * strip : (j + 1) * strip] = strip_of(normed_ref, near[j], strip)


def norm_two_kernel(place, tokens_ref, attended_ref, gain_ref, residual_ref, normed_ref):
    strip = tokens_ref.shape[1] // place.shape[0]
    for i in range(place.shape[0]):
        columns = slice(i * strip, (i + 1) * strip)
        residual_ref[:, columns] = tokens_ref[:, columns].astype(F32) + strip_of(attended_ref, place[i], strip)
    value = residual_ref[...]
    normed_ref[...] = (value * rate_of(value) * gain_ref[...]).astype(BF16)


def norm_back(value, gain, grad):
    rate = rate_of(value)
    normed = value * rate
    scaled = grad * gain
    back = rate * (scaled - normed * jnp.mean(scaled * normed, axis=-1, keepdims=True))
    return back, jnp.sum(grad * normed, axis=0, keepdims=True)


def add_up(ref, value):
    @pl.when(pl.program_id(0) == 0)
    def _():
        ref[...] = jnp.zeros_like(ref)

    ref[...] += value


def back_two_kernel(near, grad_ref, residual_ref, cotangent_ref, gain_ref, out_ref, near_ref, gain_grad_ref):
    back, gain_grad = norm_back(residual_ref[...], gain_ref[...], grad_ref[...])
    out_ref[...] = cotangent_ref[...].astype(F32) + back
    add_up(gain_grad_ref, gain_grad)
    strip = grad_ref.shape[1] // near.shape[0]
    for j in range(near.shape[0]):
        near_ref[:, j * strip : (j + 1) * strip] = strip_of(out_ref, near[j], strip).astype(BF16)


def back_one_kernel(place, grad_ref, near_ref, tokens_ref, above_ref, gain_ref, out_ref, gain_grad_ref):
    strip = tokens_ref.shape[1] // place.shape[0]
    for i in range(place.shape[0]):
        columns = slice(i * strip, (i + 1) * strip)
        out_ref[:, columns] = grad_ref[:, columns] + strip_of(near_ref, place[i], strip)
    back, gain_grad = norm_back(tokens_ref[...].astype(F32), gain_ref[...], out_ref[...])
    out_ref[...] = above_ref[...] + back
    add_up(gain_grad_ref, gain_grad)


def by_tokens(kernel, table, arrays, gain, outs, gain_grad=False):
    tokens, width = arrays[0].shape
    block = tokens // 3
    tile = pl.BlockSpec((block, width), lambda i, *_: (i, 0))
    line = pl.BlockSpec((1, width), lambda i, *_: (0, 0))
    spec = pltpu.PrefetchScalarGridSpec(
        num_scalar_prefetch=1,
        grid=(3,),
        in_specs=[tile] * len(arrays) + [line],
        out_specs=[tile] * len(outs) + [line] * gain_grad,
    )
    shapes = [jax.ShapeDtypeStruct((tokens, width), t) for t in outs]
    shapes += [jax.ShapeDtypeStruct((1, width), F32)] * gain_grad
    return pl.pallas_call(
        kernel,
        grid_spec=spec,
        out_shape=shapes,
        compiler_params=pltpu.CompilerParams(dimension_semantics=("arbitrary",), vmem_limit_bytes=40 * 2**20),
        cost_estimate=pl.CostEstimate(flops=16 * tokens * width, bytes_accessed=16 * tokens * width, transcendentals=0),
    )(table, *arrays, gain[None, :])


def unfold_kernel(place, total_ref, key_ref, value_ref, small_ref):
    width = key_ref.shape[0]
    strip = total_ref.shape[1] // place.shape[0]
    for i in range(place.shape[0]):
        columns = slice(i * strip, (i + 1) * strip)
        block = strip_of(total_ref, place[i], strip).astype(F32)
        key_ref[:, columns] = block[:width]
        value_ref[:, columns] = block[width : 2 * width]
        small_ref[:, columns] = block[2 * width : 2 * width + 16]


def unfold(place, total, width):
    model = total.shape[1]
    spec = pltpu.PrefetchScalarGridSpec(
        num_scalar_prefetch=1,
        grid=(1,),
        in_specs=[pl.BlockSpec(total.shape, lambda i, *_: (0, 0))],
        out_specs=[
            pl.BlockSpec((width, model), lambda i, *_: (0, 0)),
            pl.BlockSpec((width, model), lambda i, *_: (0, 0)),
            pl.BlockSpec((16, model), lambda i, *_: (0, 0)),
        ],
    )
    return pl.pallas_call(
        unfold_kernel,
        grid_spec=spec,
        out_shape=[
            jax.ShapeDtypeStruct((width, model), F32),
            jax.ShapeDtypeStruct((width, model), F32),
            jax.ShapeDtypeStruct((16, model), F32),
        ],
        compiler_params=pltpu.CompilerParams(dimension_semantics=("arbitrary",), vmem_limit_bytes=40 * 2**20),
    )(place, total)


def head_forward(projected, gain, turn):
    cosine, sine = turn
    half = HEAD_DIM // 2
    rate = lax.rsqrt(jnp.mean(projected * projected, axis=1, keepdims=True) + EPSILON)
    value = projected * rate * gain[:, None]
    low, high = value[:, :half], value[:, half:]
    return jnp.concatenate([low * cosine - high * sine, low * sine + high * cosine], axis=1)


def head_back(projected, gain, turn, grad):
    cosine, sine = turn
    half = HEAD_DIM // 2
    low, high = grad[:, :half], grad[:, half:]
    grad = jnp.concatenate([low * cosine + high * sine, high * cosine - low * sine], axis=1)
    rate = lax.rsqrt(jnp.mean(projected * projected, axis=1, keepdims=True) + EPSILON)
    normed = projected * rate
    scaled = grad * gain[:, None]
    back = rate * (scaled - normed * jnp.mean(scaled * normed, axis=1, keepdims=True))
    return back, jnp.sum(grad * normed, axis=(0, 2))


def weight_grad_kernel(*refs):
    out_ref = refs[-1]
    count = len(refs) // 2
    total = sum(dot(refs[i][...], refs[count + i][...], (0, 0)) for i in range(count))
    out_ref[0] = total.astype(out_ref.dtype)


def weight_grad(values, grads, blocks):
    width, hidden = values[0].shape[1], grads[0].shape[1]
    block = width // blocks
    tokens = sum(v.shape[0] for v in values)
    return pl.pallas_call(
        weight_grad_kernel,
        grid=(blocks,),
        in_specs=[pl.BlockSpec((v.shape[0], block), lambda i: (0, i)) for v in values]
        + [pl.BlockSpec(g.shape, lambda i: (0, 0), pipeline_mode=pl.Buffered(1)) for g in grads],
        out_specs=pl.BlockSpec((1, block, hidden), lambda i: (i, 0, 0)),
        out_shape=jax.ShapeDtypeStruct((blocks, block, hidden), BF16),
        compiler_params=pltpu.CompilerParams(dimension_semantics=("arbitrary",), vmem_limit_bytes=56 * 2**20),
        cost_estimate=pl.CostEstimate(
            flops=2 * tokens * width * hidden, bytes_accessed=2 * tokens * (width + hidden), transcendentals=0
        ),
        name="weight_grad",
    )(*values, *grads)


def tall(tile, columns):
    return pl.BlockSpec((tile, columns), lambda i: (i, 0))


def held(weights, which=None):
    blocks = weights.shape[0] if which is None else weights.shape[0] // 2
    return pl.BlockSpec((blocks, *weights.shape[1:]), lambda i: (which or 0, 0, 0), pipeline_mode=pl.Buffered(1))


FFN_PARAMS = pltpu.CompilerParams(dimension_semantics=("arbitrary",), vmem_limit_bytes=56 * 2**20)


def matrix(ref):
    return ref[...].reshape(ref.shape[0] * ref.shape[1], ref.shape[2])


def forward_kernel(tokens_ref, gate_w, up_w, gate_ref, up_ref, hidden_ref):
    tokens = tokens_ref[...]
    gate, up = dot(tokens, matrix(gate_w), (1, 0)), dot(tokens, matrix(up_w), (1, 0))
    gate_ref[...] = gate
    up_ref[...] = up
    hidden_ref[...] = (gate / (1.0 + jnp.exp(-gate)) * up).astype(BF16)


def forward(tokens, gate_up, tile=256):
    count, width = tokens.shape
    hidden = gate_up.shape[2]
    return pl.pallas_call(
        forward_kernel,
        grid=(count // tile,),
        in_specs=[tall(tile, width), held(gate_up, 0), held(gate_up, 1)],
        out_specs=[tall(tile, hidden)] * 3,
        out_shape=[jax.ShapeDtypeStruct((count, hidden), t) for t in (F32, F32, BF16)],
        compiler_params=FFN_PARAMS,
        cost_estimate=pl.CostEstimate(
            flops=4 * count * width * hidden,
            bytes_accessed=4 * width * hidden + 2 * count * width + 10 * count * hidden,
            transcendentals=count * hidden,
        ),
        name="forward",
    )(tokens, gate_up, gate_up)


def hidden_back_kernel(grad_ref, gate_ref, up_ref, down_w, gate_w, up_w, gate_grad_ref, up_grad_ref, part_ref):
    grad = dot(grad_ref[...], matrix(down_w), (1, 0))
    gate = gate_ref[...]
    sigmoid = 1.0 / (1.0 + jnp.exp(-gate))
    gate_grad = (grad * up_ref[...] * sigmoid * (1.0 + gate * (1.0 - sigmoid))).astype(BF16)
    up_grad = (grad * gate * sigmoid).astype(BF16)
    gate_grad_ref[...] = gate_grad
    up_grad_ref[...] = up_grad
    part_ref[...] = (dot(gate_grad, matrix(gate_w), (1, 1)) + dot(up_grad, matrix(up_w), (1, 1))).astype(BF16)


def hidden_back(grad, gate, up, down_w, gate_up, tile=256):
    count, width = grad.shape
    hidden = gate.shape[1]
    return pl.pallas_call(
        hidden_back_kernel,
        grid=(count // tile,),
        in_specs=[
            tall(tile, width), tall(tile, hidden), tall(tile, hidden), held(down_w), held(gate_up, 0), held(gate_up, 1)
        ],
        out_specs=[tall(tile, hidden), tall(tile, hidden), tall(tile, width)],
        out_shape=[jax.ShapeDtypeStruct((count, n), BF16) for n in (hidden, hidden, width)],
        compiler_params=FFN_PARAMS,
        cost_estimate=pl.CostEstimate(
            flops=6 * count * width * hidden,
            bytes_accessed=6 * width * hidden + 16 * count * hidden,
            transcendentals=count * hidden,
        ),
        name="hidden_back",
    )(grad, gate, up, down_w, gate_up, gate_up)


def down_kernel(hidden_ref, down_w, out_ref):
    out_ref[...] = dot(hidden_ref[...], matrix(down_w), (1, 1)).astype(BF16)


def down_product(hidden, down_w, tile=256):
    count, size = hidden.shape
    width = down_w.shape[0] * down_w.shape[1]
    return pl.pallas_call(
        down_kernel,
        grid=(count // tile,),
        in_specs=[tall(tile, size), held(down_w)],
        out_specs=tall(tile, width),
        out_shape=jax.ShapeDtypeStruct((count, width), BF16),
        compiler_params=FFN_PARAMS,
        cost_estimate=pl.CostEstimate(
            flops=2 * count * width * size,
            bytes_accessed=2 * width * size + 2 * count * (width + size),
            transcendentals=0,
        ),
        name="down_product",
    )(hidden, down_w)


def paired():
    return lax.axis_size("tp") == 2 and lax.axis_size("row") == 2


def plane_sum(value):
    return lax.psum_scatter(value, ("row", "core", "tp"), scatter_dimension=0, tiled=True)


def both_cores(chunk):
    return jnp.concatenate([chunk, swap(chunk, "core")])


def other_half(part):
    return part[part.shape[0] // 2 :]


def own_half(part, got):
    return part[: part.shape[0] // 2].astype(F32) + got.astype(F32)


def far_hops(far):
    middle = far.shape[0] // 2
    return swap(far[:middle], "row"), swap(far[middle:], "tp")


def near_sends(near, hop_y, hop_x):
    half = near.shape[0] // 2
    return (
        (near[:half] + hop_y[half:].astype(F32)).astype(BF16),
        (near[half:] + hop_x[half:].astype(F32)).astype(BF16),
    )


def plane_total(own, hop_y, hop_x, top_x, bottom_y):
    half = own.shape[0] // 2
    return own + jnp.concatenate(
        [hop_y[:half].astype(F32) + top_x.astype(F32), hop_x[:half].astype(F32) + bottom_y.astype(F32)]
    )


def stage(*values):
    return lax.optimization_barrier(values)


def body(
    tokens, cotangent, lengths, head_counts, norm1_gain, norm2_gain, q_gain, k_gain,
    w_query, w_key, w_value, w_out, w_gate, w_up, w_down,
):
    pack, span, width = tokens.shape
    rows, cores, ctx, tp = (lax.axis_size(a) for a in ("row", "core", "ctx", "tp"))
    own_tokens = pack * span
    slot_count = w_query.shape[1] // HEAD_DIM
    all_slots = slot_count * tp
    devices = rows * cores * ctx
    strip = width // devices
    row_index, core_index, ctx_index, tp_index = (lax.axis_index(a) for a in ("row", "core", "ctx", "tp"))

    plane = rows * cores

    def ordered(mine, other, index):
        first = index == 0
        return jnp.where(first, mine, other), jnp.where(first, other, mine)

    part = w_gate.shape[1] // plane
    down_turned = w_down.T

    def first_hop(pick):
        mine = jnp.stack([pick(r, core_index) for r in range(rows)])
        return mine, swap(jnp.stack([pick(r, 1 - core_index) for r in range(rows)]), "core")

    def second_hop(mine, got):
        both = ordered(mine, got, core_index)
        mine = jnp.stack([lax.dynamic_index_in_dim(x, row_index, 0, False) for x in both])
        got = swap(jnp.stack([lax.dynamic_index_in_dim(x, 1 - row_index, 0, False) for x in both]), "row")
        low, high = ordered(mine, got, row_index)
        return jnp.concatenate([low, high])

    def pick_columns(r, c):
        return jnp.concatenate(
            [lax.dynamic_slice_in_dim(w, (r * cores + c) * part, part, 1) for w in (w_gate, w_up, down_turned)]
        )

    def by_weight(blocks, first, last):
        return jnp.concatenate([blocks[:, i * strip : (i + 1) * strip] for i in range(first, last)])

    def row_out(grad):
        view = grad.reshape(rows, cores, *grad.shape[1:])
        mine = lax.dynamic_index_in_dim(view, row_index, 0, False)
        got = swap(lax.dynamic_index_in_dim(view, 1 - row_index, 0, False), "row")
        return jnp.stack(ordered(mine, got, row_index))

    def core_out(both):
        mine = lax.dynamic_index_in_dim(both, core_index, 1, False)
        got = swap(lax.dynamic_index_in_dim(both, 1 - core_index, 1, False), "core")
        low, high = ordered(mine, got, core_index)
        return [x for r in range(rows) for x in (low[r], high[r])]

    def from_tp(value, axis):
        if tp == 2:
            return join(value, "tp", axis)
        return lax.all_gather(value, "tp", axis=axis, tiled=True)

    def up(value):
        return lax.ppermute(value, "ctx", [(i, i + 1) for i in range(ctx - 1)])

    def beside(value):
        if tp == 2:
            return jnp.stack([value, swap(value, "tp")])
        return lax.all_gather(value, "tp", axis=0)

    length = span * tp * ctx
    first_end = lengths[:, 0:1]
    second_end = first_end + lengths[:, 1:2]
    own_start = (ctx_index * tp + tp_index) * span
    places = own_start + jnp.arange(span, dtype=jnp.int32)[None, :]
    begins = jnp.where(places >= second_end, second_end, jnp.where(places >= first_end, first_end, 0))
    angles_of = (places - begins).astype(F32)
    frequency = jnp.exp(jnp.arange(HEAD_DIM // 2).astype(F32) * (-2.0 * math.log(THETA) / HEAD_DIM))
    angles = frequency[:, None] * angles_of.reshape(1, own_tokens)
    turn = (jnp.cos(angles), jnp.sin(angles))
    offsets = [jnp.int32(0)]
    for i in range(tp):
        offsets.append(offsets[-1] + head_counts[i])
    heads = jnp.arange(HEADS, dtype=jnp.int32)
    slots = jnp.zeros((HEADS,), jnp.int32)
    for i in range(tp):
        inside = (heads >= offsets[i]) & (heads < offsets[i + 1])
        holder = jnp.bitwise_xor(i, tp_index) if tp == 2 else i
        slots = jnp.where(inside, holder * slot_count + heads - offsets[i], slots)
    ranks = jnp.arange(devices, dtype=jnp.int32)
    near_strips = (
        (jnp.bitwise_xor(ranks // ctx % rows, row_index) * cores + jnp.bitwise_xor(ranks // (ctx * rows), core_index))
        * ctx + jnp.bitwise_xor(ranks % ctx, ctx_index)
    )
    strip_places = (
        (jnp.bitwise_xor(ranks // ctx % cores, core_index) * rows + jnp.bitwise_xor(ranks // (ctx * cores), row_index))
        * ctx + jnp.bitwise_xor(ranks % ctx, ctx_index)
    )
    blocks = ctx * tp
    steps = jnp.arange(blocks, dtype=jnp.int32) // tp
    partner = jnp.arange(blocks, dtype=jnp.int32) % tp
    if tp == 2:
        partner = jnp.bitwise_xor(partner, tp_index)
    starts = ((ctx_index - steps) * tp + partner) * span
    seen = (starts[None, :] >= 0) & (starts[None, :] <= own_start) & (starts[None, :] + span > begins[:, :1])
    counts = jnp.sum(seen.astype(jnp.int32), axis=1)
    turns = jnp.sum(
        (seen[:, None, :] & (jnp.arange(blocks)[None, None, :] < jnp.arange(blocks)[None, :, None])).astype(jnp.int32),
        axis=2,
    )
    order = jnp.sum(
        jnp.where(
            seen[:, None, :] & (turns[:, None, :] == jnp.arange(blocks)[None, :, None]),
            jnp.arange(blocks, dtype=jnp.int32)[None, None, :],
            0,
        ),
        axis=2,
    )
    tables = (
        order,
        counts,
        starts,
        slots,
        jnp.concatenate([begins] * GROUP, axis=1)[:, None, :],
        jnp.concatenate([places] * GROUP, axis=1),
    )

    half = own_tokens // 2
    two = paired()
    key_value = jnp.concatenate([w_key, w_value], axis=1)
    flat = tokens.reshape(own_tokens, width)
    grad_low = cotangent.reshape(own_tokens, width)
    normed_one, normed_near = by_tokens(norm_one_kernel, near_strips, [flat], norm1_gain, [BF16, BF16])
    kv_width = KVH * HEAD_DIM
    projected = dot(key_value, normed_one, (0, 1))
    key_proj = projected[:kv_width].reshape(KVH, HEAD_DIM, own_tokens)
    key_low = head_forward(key_proj, k_gain, turn).astype(BF16).reshape(kv_width, own_tokens)
    own_kv = jnp.concatenate([key_low, projected[kv_width:].astype(BF16)])

    mine, got = first_hop(pick_columns)
    query_part = join(w_query, "ctx", 0)
    out_part = join(w_out, "ctx", 1)
    got, query_part, out_part, own_kv = stage(got, query_part, out_part, own_kv)

    packed = second_hop(mine, got)
    gate_up, packed = by_weight(packed, 0, 2), by_weight(packed, 2, 3)
    going, arrived = up(own_kv), [beside(own_kv)]
    query_part = join(query_part, "ctx", 0, 2)
    packed, gate_up, going, arrived[0], query_part = stage(packed, gate_up, going, arrived[0], query_part)
    gate_up = lax.all_gather(gate_up, "ctx", axis=1, tiled=True)

    arrived.append(beside(going))
    going = up(going)
    query_part = join(query_part, "row", 0)
    going, arrived[1], query_part, packed = stage(going, arrived[1], query_part, packed)

    arrived.append(beside(going))
    going = up(going)
    query_part = from_tp(query_part, 1)
    out_part = join(out_part, "ctx", 1, 2)
    going, arrived[2], query_part, out_part, packed = stage(going, arrived[2], query_part, out_part, packed)

    arrived.append(beside(going))
    query_full = join(query_part, "core", 0)
    out_part = join(out_part, "row", 1)
    arrived[3], query_full, out_part, packed = stage(arrived[3], query_full, out_part, packed)
    keyvalue = jnp.concatenate(arrived)

    query_proj = dot(query_full, normed_near, (0, 1)).reshape(all_slots, HEAD_DIM, own_tokens)
    query_low = head_forward(query_proj, q_gain, turn).astype(BF16)
    out_low, totals = attend(query_low, keyvalue, tables)
    out_part = from_tp(out_part, 0)
    top, bottom = grad_low[:half], grad_low[half:]
    grad_near = (swap(top, "tp"), swap(bottom, "row")) if two else (top, bottom)
    out_low, totals, out_part, grad_near, packed, gate_up = stage(
        out_low, totals, out_part, grad_near, packed, gate_up
    )
    down_full = lax.all_gather(packed, "ctx", axis=1, tiled=True)
    out_full = join(out_part, "core", 1)
    out_flat = out_low.reshape(all_slots * HEAD_DIM, own_tokens)
    attended = dot(out_flat, out_full, (0, 0))
    residual, normed_two = by_tokens(norm_two_kernel, strip_places, [flat, attended], norm2_gain, [F32, BF16])
    normed_two, residual, out_full = stage(normed_two, residual, out_full)

    if two:
        top, bottom = normed_two[:half], normed_two[half:]
        near = swap(top, "tp"), swap(bottom, "row")
        other = swap(normed_two, "core")
        near, other = stage(near, other)
        far = swap(jnp.concatenate([top, near[0]]), "row"), swap(jnp.concatenate([bottom, near[1]]), "tp")
        near = jnp.concatenate(near)
        normed_all = [jnp.concatenate([normed_two, other, near, swap(near, "core")])]
        near = jnp.concatenate(grad_near)
        grad_all = [jnp.concatenate([grad_low, swap(grad_low, "core"), near, swap(near, "core")])]
        ready = [forward(normed_all[0], gate_up)]
        far, normed_all, grad_all, ready, down_full = stage(far, normed_all, grad_all, ready, down_full)
        top, bottom = grad_low[:half], grad_low[half:]
        normed_all.append(both_cores(jnp.concatenate(far)))
        ready.append(forward(normed_all[1], gate_up))
        grad_far = (
            swap(jnp.concatenate([top, grad_near[0]]), "row"), swap(jnp.concatenate([bottom, grad_near[1]]), "tp")
        )
        ready, grad_far, grad_all, normed_all = stage(ready, grad_far, grad_all, normed_all)
        grad_all.append(both_cores(jnp.concatenate(grad_far)))
    else:
        normed_all = [lax.all_gather(normed_two, ("row", "core", "tp"), axis=0, tiled=True)]
        grad_all = [lax.all_gather(grad_low, ("row", "core", "tp"), axis=0, tiled=True)]
        ready = [forward(normed_all[0], gate_up)]
    chunks = range(len(normed_all))
    hidden = [x[2] for x in ready]

    def backward(i):
        return hidden_back(grad_all[i], ready[i][0], ready[i][1], down_full, gate_up)

    def output_part(i):
        return down_product(hidden[i], down_full)

    def scattered(gradient):
        return lax.psum_scatter(gradient, "ctx", scatter_dimension=1, tiled=True)

    if two:
        far_grads = backward(1)
        far_grads, far_send, grad_all = stage(far_grads, other_half(far_grads[2]), grad_all)
        far = own_half(far_grads[2], swap(far_send, "core")).astype(BF16)
        far_part = output_part(1)
        far, grad_all, far_part = stage(far, grad_all, far_part)
        hops = far_hops(far)
        near_grads = backward(0)
        output_far = own_half(far_part, swap(other_half(far_part), "core")).astype(BF16)
        hops, near_grads, hidden, output_far = stage(hops, near_grads, hidden, output_far)
        grads = [near_grads, far_grads]
        own_part, near_part = near_grads[2][: 2 * own_tokens], near_grads[2][2 * own_tokens :]
        near = own_half(near_part, swap(other_half(near_part), "core"))
        own = own_half(own_part, swap(other_half(own_part), "core"))
        sends = near_sends(near, *hops)
        sends, own, normed_all, hidden, grad_all = stage(sends, own, normed_all, hidden, grad_all)
        top_x, bottom_y = swap(sends[0], "tp"), swap(sends[1], "row")
        grad_down = weight_grad(grad_all, hidden, plane)
        top_x, bottom_y, output_far, grads, normed_all, grad_down = stage(
            top_x, bottom_y, output_far, grads, normed_all, grad_down
        )
        output_hops = far_hops(output_far)
        grad_normed_two = plane_total(own, *hops, top_x, bottom_y)
    else:
        grads = [backward(0)]
        grad_down = weight_grad(grad_all, hidden, plane)
        grad_normed_two = plane_sum(grads[0][2]).astype(F32)
        output_hops = grad_normed_two
    grad_down = scattered(grad_down)
    grad_residual, grad_attn, grad_norm_two = by_tokens(
        back_two_kernel, near_strips, [grad_normed_two, residual, grad_low], norm2_gain, [F32, BF16], True
    )

    grad_out = dot(out_full, grad_attn, (1, 1)).astype(BF16).reshape(all_slots, HEAD_DIM, own_tokens)
    grad_query, grad_kv = attend_back(query_low, grad_out, out_low, keyvalue, totals, tables)
    grad_out_w = dot(out_flat, grad_attn, (1, 0)).astype(BF16)
    grad_out_w = fold(grad_out_w, "core", 1)
    output_hops, grad_query, grad_kv, grads, grad_out_w, normed_all, hidden = stage(
        output_hops, grad_query, grad_kv, grads, grad_out_w, normed_all, hidden
    )
    grad_kv = grad_kv.reshape(ctx, tp, 2 * kv_width, own_tokens)

    def to_tp(value, axis):
        if tp == 2:
            return fold(value, "tp", axis)
        return lax.psum_scatter(value, "tp", scatter_dimension=axis, tiled=True)

    def to_owner(value):
        if tp == 2:
            return value[0].astype(F32) + swap(value[1], "tp").astype(F32)
        return lax.psum_scatter(value, "tp", scatter_dimension=0, tiled=False).astype(F32)

    def down(value):
        return lax.ppermute(value.astype(BF16), "ctx", [(j, j - 1) for j in range(1, ctx)]).astype(F32)

    summed = to_owner(grad_kv[ctx - 1])
    grad_gate_w = weight_grad(normed_all, [g[0] for g in grads], plane)
    out_w_low, out_w_high = grad_out_w[: all_slots * 32], grad_out_w[all_slots * 32 :]
    out_w_low = fold(out_w_low, "row", 1)
    summed, grad_kv, grad_query, out_w_low, out_w_high, normed_all, grads, grad_gate_w, grad_down = stage(
        summed, grad_kv, grad_query, out_w_low, out_w_high, normed_all, grads, grad_gate_w, grad_down
    )

    summed = to_owner(grad_kv[2]) + down(summed)
    out_w_high = fold(out_w_high, "row", 1)
    summed, grad_kv, grad_query, out_w_low, out_w_high, grad_gate_w, grad_down = stage(
        summed, grad_kv, grad_query, out_w_low, out_w_high, grad_gate_w, grad_down
    )

    summed = to_owner(grad_kv[1]) + down(summed)
    grad_query_proj, grad_q_gain = head_back(query_proj, q_gain, turn, grad_query)
    grad_query_low = grad_query_proj.astype(BF16).reshape(all_slots * HEAD_DIM, own_tokens)
    grad_down = row_out(grad_down)
    summed, grad_query_low, grad_q_gain, grad_kv, grad_down, out_w_low, out_w_high, grad_gate_w = stage(
        summed, grad_query_low, grad_q_gain, grad_kv, grad_down, out_w_low, out_w_high, grad_gate_w
    )

    summed = to_owner(grad_kv[0]) + down(summed)
    grad_query_w = dot(normed_near, grad_query_low, (0, 1)).astype(BF16)
    grad_query_w = fold(grad_query_w, "core", 0)
    grad_normed_near = dot(grad_query_low, query_full, (0, 1))
    grad_down = core_out(grad_down)
    summed, grad_query_w, grad_normed_near, grad_down, out_w_low, out_w_high, grad_gate_w, normed_all, grads, hidden = stage(
        summed, grad_query_w, grad_normed_near, grad_down, out_w_low, out_w_high, grad_gate_w, normed_all, grads, hidden
    )
    grad_gate_w = scattered(grad_gate_w)

    grad_key_proj, grad_k_gain = head_back(
        key_proj, k_gain, turn, summed[:kv_width].reshape(KVH, HEAD_DIM, own_tokens)
    )
    grad_kv_low = jnp.concatenate(
        [grad_key_proj.reshape(kv_width, own_tokens).astype(BF16), summed[kv_width:].astype(BF16)]
    )
    padded = jnp.pad(grad_kv_low, ((0, 32), (0, 0)))
    total = dot(padded, normed_near if two else normed_one, (1, 0))
    grad_normed_one = dot(grad_kv_low, key_value, (0, 1))
    grad_inputs, grad_norm_one = by_tokens(
        back_one_kernel, strip_places, [grad_normed_one, grad_normed_near, flat, grad_residual], norm1_gain, [F32], True
    )
    gains = jnp.concatenate([grad_q_gain, grad_k_gain, jnp.zeros((width - 2 * HEAD_DIM,), F32)])
    small = jnp.concatenate([grad_norm_one, grad_norm_two, gains[None]])
    moved = (near_strips if two else ranks)[:, None] == ranks[None, :]
    small = jnp.sum(
        jnp.where(moved[None, :, :, None], small.reshape(3, 1, devices, strip), 0.0), axis=2
    ).reshape(3, width)
    total = lax.dynamic_update_slice(total, small, (2 * kv_width, 0)).astype(BF16)
    query_w = fold(grad_query_w[:, : all_slots * 32], "row", 0), grad_query_w[:, all_slots * 32 :]
    grad_out_w = to_tp(jnp.concatenate([out_w_low, out_w_high]), 0)
    total, query_w, grad_out_w, hidden, normed_all, grads = stage(
        total, query_w, grad_out_w, hidden, normed_all, grads
    )

    def along(value, bit):
        got = swap(value, "ctx", bit)
        return sum32(
            value, jnp.concatenate([got[:, (j ^ bit) * strip : ((j ^ bit) + 1) * strip] for j in range(ctx)], axis=1)
        )

    if not two:
        total = lax.psum(total, ("row", "core", "ctx", "tp"))
        output = residual + plane_sum(output_part(0)).astype(F32)
        grad_up_w = scattered(weight_grad(normed_all, [g[1] for g in grads], plane))
        query_w = jnp.concatenate([query_w[0], fold(query_w[1], "row", 0)], axis=1)
        grad_query_w = fold(fold(to_tp(query_w, 1), "ctx", 0, 2), "ctx", 0)
        grad_out_w = fold(fold(grad_out_w, "ctx", 1, 2), "ctx", 1)
        grad_up_w, grad_gate_w = core_out(row_out(grad_up_w)), core_out(row_out(grad_gate_w))
    else:
        total = fold(total, "core", 1)
        total, query_w, grad_out_w, hidden, normed_all, grads = stage(
            total, query_w, grad_out_w, hidden, normed_all, grads
        )
        size = total.shape[0] // 2
        got = swap(lax.dynamic_slice_in_dim(total, (1 - tp_index) * size, size, 0), "tp")
        total = sum32(lax.dynamic_slice_in_dim(total, tp_index * size, size, 0), got)
        query_w = jnp.concatenate([query_w[0], fold(query_w[1], "row", 0)], axis=1)
        grad_up_w = weight_grad(normed_all, [g[1] for g in grads], plane)
        total, grad_out_w, query_w, hidden, grad_up_w = stage(total, grad_out_w, query_w, hidden, grad_up_w)
        grad_up_w = scattered(grad_up_w)
        total = fold(total, "row", 1)
        query_w = fold(query_w, "tp", 1)
        near_part = output_part(0)
        own_part, near_part = near_part[: 2 * own_tokens], near_part[2 * own_tokens :]
        near = own_half(near_part, swap(other_half(near_part), "core"))
        own = own_half(own_part, swap(other_half(own_part), "core"))
        sends = near_sends(near, *output_hops)
        total, query_w, sends, own, grad_gate_w, grad_out_w = stage(
            total, query_w, sends, own, grad_gate_w, grad_out_w
        )
        total = along(total, 1)
        top_x, bottom_y = swap(sends[0], "tp"), swap(sends[1], "row")
        grad_out_w = fold(grad_out_w, "ctx", 1, 2)
        total, query_w, grad_gate_w, top_x, bottom_y, grad_out_w = stage(
            total, query_w, grad_gate_w, top_x, bottom_y, grad_out_w
        )
        total = along(total, 2)
        output = residual + plane_total(own, *output_hops, top_x, bottom_y)
        grad_gate_w = row_out(grad_gate_w)
        grad_out_w = fold(grad_out_w, "ctx", 1)
        total, query_w, grad_gate_w, grad_out_w, output = stage(total, query_w, grad_gate_w, grad_out_w, output)
        total = join(total, "row", 1)
        query_w = fold(query_w, "ctx", 0, 2)
        grad_gate_w = core_out(grad_gate_w)
        total, grad_up_w, query_w, grad_gate_w = stage(total, grad_up_w, query_w, grad_gate_w)
        other = swap(total, "tp")
        grad_query_w = fold(query_w, "ctx", 0)
        grad_up_w = row_out(grad_up_w)
        first = tp_index == 0
        total = jnp.concatenate([jnp.where(first, total, other), jnp.where(first, other, total)])
        total, grad_up_w, grad_query_w = stage(total, grad_up_w, grad_query_w)
        total = join(total, "core", 1)
        grad_up_w = core_out(grad_up_w)
    grad_key_w, grad_value_w, small = unfold(strip_places if two else ranks, total, kv_width)

    return (
        output.astype(BF16).reshape(pack, span, width),
        grad_inputs.reshape(pack, span, width),
        small[0],
        small[1],
        small[2, :HEAD_DIM],
        small[2, HEAD_DIM : 2 * HEAD_DIM],
        grad_query_w.astype(F32),
        grad_key_w.T,
        grad_value_w.T,
        grad_out_w.astype(F32),
        jnp.concatenate(grad_gate_w, axis=1).astype(F32),
        jnp.concatenate(grad_up_w, axis=1).astype(F32),
        jnp.concatenate([x.T for x in grad_down]).astype(F32),
    )


def solution(mesh):
    dp, ctx, tp = (mesh.shape[a] for a in ("dp", "ctx", "tp"))
    split = Mesh(mesh.devices.reshape(dp // 2, 2, ctx, tp), ("row", "core", "ctx", "tp"))
    dp = ("row", "core")
    every = ("row", "core", "ctx")
    token = P(dp, ("ctx", "tp"), None)
    by_row, by_column = P(every, "tp"), P("tp", every)
    return jax.shard_map(
        body,
        mesh=split,
        in_specs=(
            token, token, P(dp, None), P(), P(), P(), P(), P(),
            by_row, P(), P(), by_column, by_row, by_row, by_column,
        ),
        out_specs=(
            token, token, P(), P(), P(), P(),
            by_row, P(), P(), by_column, by_row, by_row, by_column,
        ),
        check_vma=False,
    )
```

```python
import math

import jax
import jax.numpy as jnp
from jax import lax
from jax.experimental import pallas as pl
from jax.experimental.pallas import tpu as pltpu
from jax.sharding import Mesh
from jax.sharding import PartitionSpec as P

HEADS = 20
KVH = 5
HEAD_DIM = 64
GROUP = HEADS // KVH

EPSILON = 1e-05
THETA = 10000.0
SCALE = HEAD_DIM ** (-0.5)
EXP2_SCALE = SCALE / math.log(2.0)

BF16 = jnp.bfloat16
F32 = jnp.float32


def dot(left, right, contract):
    return lax.dot_general(left, right, ((contract[:1], contract[1:]), ((), ())), preferred_element_type=F32)


def swap(value, axis, bit=1):
    size = lax.axis_size(axis)
    return lax.ppermute(value, axis, [(i, i ^ bit) for i in range(size)])


def join(value, axis, dimension, bit=1):
    return jnp.concatenate([value, swap(value, axis, bit)], axis=dimension)


def fold(value, axis, dimension, bit=1):
    size = value.shape[dimension] // 2
    got = swap(lax.slice_in_dim(value, size, 2 * size, axis=dimension), axis, bit)
    return sum32(lax.slice_in_dim(value, 0, size, axis=dimension), got)


def sum32(left, right):
    return (left.astype(F32) + right.astype(F32)).astype(BF16)


def stacked(ref, slots, head, begin, span):
    return jnp.concatenate(
        [ref[slots[head * GROUP + i], :, begin : begin + span] for i in range(GROUP)], axis=1
    )


def attend_kernel(
    order, counts, starts, slots, q_ref, k_ref, v_ref, first_ref, place_ref, o_ref, total_ref
):
    head = pl.program_id(0)
    pack, _, wide = first_ref.shape
    span = wide // GROUP

    @pl.when(head == 0)
    def _():
        o_ref[...] = jnp.zeros_like(o_ref)

    place = place_ref[...]
    for row in range(pack):
        begin = row * span
        query = stacked(q_ref, slots, head, begin, span)
        first = first_ref[row]

        def step(i, carry):
            acc, total = carry
            block = order[row, i]
            scores = dot(k_ref[block, :, begin : begin + span].T, query, (1, 0))
            keys = starts[block] + lax.broadcasted_iota(jnp.int32, scores.shape, 0)
            weight = jnp.where((keys >= first) & (keys <= place), jnp.exp2(scores * EXP2_SCALE), 0.0)
            total = total + jnp.sum(weight, axis=0, keepdims=True)
            acc = acc + dot(v_ref[block, :, begin : begin + span], weight.astype(BF16), (1, 0))
            return acc, total

        acc, total = lax.fori_loop(
            0, counts[row], step, (jnp.zeros((HEAD_DIM, wide), F32), jnp.zeros((1, wide), F32))
        )
        total_ref[0, row] = total
        acc = (acc / total).astype(o_ref.dtype)
        for i in range(GROUP):
            o_ref[slots[head * GROUP + i], :, begin : begin + span] = acc[:, i * span : (i + 1) * span]


def attention_specs(query, keyvalue, first):
    slot_count, _, lanes = query.shape
    pack, _, wide = first.shape
    blocks = keyvalue.shape[0]
    whole = pl.BlockSpec((slot_count, HEAD_DIM, lanes), lambda g, *_: (0, 0, 0))
    keys = pl.BlockSpec((blocks, HEAD_DIM, lanes), lambda g, *_: (0, g, 0))
    values = pl.BlockSpec((blocks, HEAD_DIM, lanes), lambda g, *_: (0, KVH + g, 0))
    totals = pl.BlockSpec((1, pack, 1, wide), lambda g, *_: (g, 0, 0, 0))
    bounds = [
        pl.BlockSpec((pack, 1, wide), lambda g, *_: (0, 0, 0)),
        pl.BlockSpec((1, wide), lambda g, *_: (0, 0)),
    ]
    work = HEADS * lanes * blocks * (wide // GROUP)
    return whole, keys, values, totals, bounds, work


def attend(query, keyvalue, tables):
    order, counts, starts, slots, first, place = tables
    pack, _, wide = first.shape
    whole, keys, values, totals, bounds, work = attention_specs(query, keyvalue, first)
    spec = pltpu.PrefetchScalarGridSpec(
        num_scalar_prefetch=4,
        grid=(KVH,),
        in_specs=[whole, keys, values, *bounds],
        out_specs=[whole, totals],
    )
    return pl.pallas_call(
        attend_kernel,
        grid_spec=spec,
        out_shape=[jax.ShapeDtypeStruct(query.shape, BF16), jax.ShapeDtypeStruct((KVH, pack, 1, wide), F32)],
        compiler_params=pltpu.CompilerParams(dimension_semantics=("arbitrary",), vmem_limit_bytes=40 * 2**20),
        cost_estimate=pl.CostEstimate(flops=work * 1024, bytes_accessed=8 * 2**20, transcendentals=work),
        name="attend",
    )(order, counts, starts, slots, query, keyvalue, keyvalue, first, place)


def attend_back_kernel(
    order, counts, starts, slots, q_ref, g_ref, o_ref, k_ref, v_ref, total_ref, first_ref, place_ref,
    dq_ref, dkv_ref,
):
    head = pl.program_id(0)
    pack, _, wide = first_ref.shape
    span = wide // GROUP

    @pl.when(head == 0)
    def _():
        dq_ref[...] = jnp.zeros_like(dq_ref)

    dkv_ref[...] = jnp.zeros_like(dkv_ref)
    place = place_ref[...]
    for row in range(pack):
        begin = row * span
        query, grad, out = (stacked(ref, slots, head, begin, span) for ref in (q_ref, g_ref, o_ref))
        inner = jnp.sum(grad.astype(F32) * out.astype(F32), axis=0, keepdims=True)
        lift = jnp.log2(total_ref[0, row])
        first = first_ref[row]

        def step(i, acc):
            block = order[row, i]
            key, value = (ref[block, :, begin : begin + span] for ref in (k_ref, v_ref))
            scores = dot(key.T, query, (1, 0))
            keys = starts[block] + lax.broadcasted_iota(jnp.int32, scores.shape, 0)
            probs = jnp.where((keys >= first) & (keys <= place), jnp.exp2(scores * EXP2_SCALE - lift), 0.0)
            grad_probs = dot(value.T, grad, (1, 0))
            grad_scores = (probs * (grad_probs - inner)).astype(BF16)
            dkv_ref[block, 0, :, begin : begin + span] = (
                (dot(grad_scores, query, (1, 1)) * SCALE).T.astype(dkv_ref.dtype)
            )
            dkv_ref[block, 1, :, begin : begin + span] = (
                dot(probs.astype(BF16), grad, (1, 1)).T.astype(dkv_ref.dtype)
            )
            return acc + dot(key, grad_scores, (1, 0))

        acc = lax.fori_loop(0, counts[row], step, jnp.zeros((HEAD_DIM, wide), F32)) * SCALE
        for i in range(GROUP):
            dq_ref[slots[head * GROUP + i], :, begin : begin + span] = acc[:, i * span : (i + 1) * span]


def attend_back(query, grad, out, keyvalue, totals_in, tables):
    order, counts, starts, slots, first, place = tables
    whole, keys, values, totals, bounds, work = attention_specs(query, keyvalue, first)
    blocks, _, lanes = keyvalue.shape
    spec = pltpu.PrefetchScalarGridSpec(
        num_scalar_prefetch=4,
        grid=(KVH,),
        in_specs=[whole, whole, whole, keys, values, totals, *bounds],
        out_specs=[whole, pl.BlockSpec((blocks, 2, HEAD_DIM, lanes), lambda g, *_: (0, 0, g, 0))],
    )
    return pl.pallas_call(
        attend_back_kernel,
        grid_spec=spec,
        out_shape=[
            jax.ShapeDtypeStruct(query.shape, F32),
            jax.ShapeDtypeStruct((blocks, 2, KVH * HEAD_DIM, lanes), BF16),
        ],
        compiler_params=pltpu.CompilerParams(dimension_semantics=("arbitrary",), vmem_limit_bytes=48 * 2**20),
        cost_estimate=pl.CostEstimate(flops=work * 2560, bytes_accessed=16 * 2**20, transcendentals=work),
        name="attend_back",
    )(order, counts, starts, slots, query, grad, out, keyvalue, keyvalue, totals_in, first, place)


def strip_of(ref, index, strip):
    return ref[:, pl.ds(pl.multiple_of(index * strip, strip), strip)]


def rate_of(value):
    return lax.rsqrt(jnp.mean(value * value, axis=-1, keepdims=True) + EPSILON)


def norm_one_kernel(near, tokens_ref, gain_ref, normed_ref, near_ref):
    value = tokens_ref[...].astype(F32)
    normed_ref[...] = (value * rate_of(value) * gain_ref[...]).astype(BF16)
    strip = value.shape[1] // near.shape[0]
    for j in range(near.shape[0]):
        near_ref[:, j * strip : (j + 1) * strip] = strip_of(normed_ref, near[j], strip)


def norm_two_kernel(place, tokens_ref, attended_ref, gain_ref, residual_ref, normed_ref):
    strip = tokens_ref.shape[1] // place.shape[0]
    for i in range(place.shape[0]):
        columns = slice(i * strip, (i + 1) * strip)
        residual_ref[:, columns] = tokens_ref[:, columns].astype(F32) + strip_of(attended_ref, place[i], strip)
    value = residual_ref[...]
    normed_ref[...] = (value * rate_of(value) * gain_ref[...]).astype(BF16)


def norm_back(value, gain, grad):
    rate = rate_of(value)
    normed = value * rate
    scaled = grad * gain
    back = rate * (scaled - normed * jnp.mean(scaled * normed, axis=-1, keepdims=True))
    return back, jnp.sum(grad * normed, axis=0, keepdims=True)


def add_up(ref, value):
    @pl.when(pl.program_id(0) == 0)
    def _():
        ref[...] = jnp.zeros_like(ref)

    ref[...] += value


def back_two_kernel(near, grad_ref, residual_ref, cotangent_ref, gain_ref, out_ref, near_ref, gain_grad_ref):
    back, gain_grad = norm_back(residual_ref[...], gain_ref[...], grad_ref[...])
    out_ref[...] = cotangent_ref[...].astype(F32) + back
    add_up(gain_grad_ref, gain_grad)
    strip = grad_ref.shape[1] // near.shape[0]
    for j in range(near.shape[0]):
        near_ref[:, j * strip : (j + 1) * strip] = strip_of(out_ref, near[j], strip).astype(BF16)


def back_one_kernel(place, grad_ref, near_ref, tokens_ref, above_ref, gain_ref, out_ref, gain_grad_ref):
    strip = tokens_ref.shape[1] // place.shape[0]
    for i in range(place.shape[0]):
        columns = slice(i * strip, (i + 1) * strip)
        out_ref[:, columns] = grad_ref[:, columns] + strip_of(near_ref, place[i], strip)
    back, gain_grad = norm_back(tokens_ref[...].astype(F32), gain_ref[...], out_ref[...])
    out_ref[...] = above_ref[...] + back
    add_up(gain_grad_ref, gain_grad)


def by_tokens(kernel, table, arrays, gain, outs, gain_grad=False):
    tokens, width = arrays[0].shape
    block = tokens // 3
    tile = pl.BlockSpec((block, width), lambda i, *_: (i, 0))
    line = pl.BlockSpec((1, width), lambda i, *_: (0, 0))
    spec = pltpu.PrefetchScalarGridSpec(
        num_scalar_prefetch=1,
        grid=(3,),
        in_specs=[tile] * len(arrays) + [line],
        out_specs=[tile] * len(outs) + [line] * gain_grad,
    )
    shapes = [jax.ShapeDtypeStruct((tokens, width), t) for t in outs]
    shapes += [jax.ShapeDtypeStruct((1, width), F32)] * gain_grad
    return pl.pallas_call(
        kernel,
        grid_spec=spec,
        out_shape=shapes,
        compiler_params=pltpu.CompilerParams(dimension_semantics=("arbitrary",), vmem_limit_bytes=40 * 2**20),
        cost_estimate=pl.CostEstimate(flops=16 * tokens * width, bytes_accessed=16 * tokens * width, transcendentals=0),
    )(table, *arrays, gain[None, :])


def unfold_kernel(place, total_ref, key_ref, value_ref, small_ref):
    width = key_ref.shape[0]
    strip = total_ref.shape[1] // place.shape[0]
    for i in range(place.shape[0]):
        columns = slice(i * strip, (i + 1) * strip)
        block = strip_of(total_ref, place[i], strip).astype(F32)
        key_ref[:, columns] = block[:width]
        value_ref[:, columns] = block[width : 2 * width]
        small_ref[:, columns] = block[2 * width : 2 * width + 16]


def unfold(place, total, width):
    model = total.shape[1]
    spec = pltpu.PrefetchScalarGridSpec(
        num_scalar_prefetch=1,
        grid=(1,),
        in_specs=[pl.BlockSpec(total.shape, lambda i, *_: (0, 0))],
        out_specs=[
            pl.BlockSpec((width, model), lambda i, *_: (0, 0)),
            pl.BlockSpec((width, model), lambda i, *_: (0, 0)),
            pl.BlockSpec((16, model), lambda i, *_: (0, 0)),
        ],
    )
    return pl.pallas_call(
        unfold_kernel,
        grid_spec=spec,
        out_shape=[
            jax.ShapeDtypeStruct((width, model), F32),
            jax.ShapeDtypeStruct((width, model), F32),
            jax.ShapeDtypeStruct((16, model), F32),
        ],
        compiler_params=pltpu.CompilerParams(dimension_semantics=("arbitrary",), vmem_limit_bytes=40 * 2**20),
    )(place, total)


def head_forward(projected, gain, turn):
    cosine, sine = turn
    half = HEAD_DIM // 2
    rate = lax.rsqrt(jnp.mean(projected * projected, axis=1, keepdims=True) + EPSILON)
    value = projected * rate * gain[:, None]
    low, high = value[:, :half], value[:, half:]
    return jnp.concatenate([low * cosine - high * sine, low * sine + high * cosine], axis=1)


def head_back(projected, gain, turn, grad):
    cosine, sine = turn
    half = HEAD_DIM // 2
    low, high = grad[:, :half], grad[:, half:]
    grad = jnp.concatenate([low * cosine + high * sine, high * cosine - low * sine], axis=1)
    rate = lax.rsqrt(jnp.mean(projected * projected, axis=1, keepdims=True) + EPSILON)
    normed = projected * rate
    scaled = grad * gain[:, None]
    back = rate * (scaled - normed * jnp.mean(scaled * normed, axis=1, keepdims=True))
    return back, jnp.sum(grad * normed, axis=(0, 2))


def weight_grad_kernel(*refs):
    out_ref = refs[-1]
    count = len(refs) // 2
    total = sum(dot(refs[i][...], refs[count + i][...], (0, 0)) for i in range(count))
    out_ref[0] = total.astype(out_ref.dtype)


def weight_grad(values, grads, blocks):
    width, hidden = values[0].shape[1], grads[0].shape[1]
    block = width // blocks
    tokens = sum(v.shape[0] for v in values)
    return pl.pallas_call(
        weight_grad_kernel,
        grid=(blocks,),
        in_specs=[pl.BlockSpec((v.shape[0], block), lambda i: (0, i)) for v in values]
        + [pl.BlockSpec(g.shape, lambda i: (0, 0), pipeline_mode=pl.Buffered(1)) for g in grads],
        out_specs=pl.BlockSpec((1, block, hidden), lambda i: (i, 0, 0)),
        out_shape=jax.ShapeDtypeStruct((blocks, block, hidden), BF16),
        compiler_params=pltpu.CompilerParams(dimension_semantics=("arbitrary",), vmem_limit_bytes=56 * 2**20),
        cost_estimate=pl.CostEstimate(
            flops=2 * tokens * width * hidden, bytes_accessed=2 * tokens * (width + hidden), transcendentals=0
        ),
        name="weight_grad",
    )(*values, *grads)


def tall(tile, columns):
    return pl.BlockSpec((tile, columns), lambda i: (i, 0))


def held(weights, which=None):
    blocks = weights.shape[0] if which is None else weights.shape[0] // 2
    return pl.BlockSpec((blocks, *weights.shape[1:]), lambda i: (which or 0, 0, 0), pipeline_mode=pl.Buffered(1))


FFN_PARAMS = pltpu.CompilerParams(dimension_semantics=("arbitrary",), vmem_limit_bytes=56 * 2**20)


def matrix(ref):
    return ref[...].reshape(ref.shape[0] * ref.shape[1], ref.shape[2])


def forward_kernel(tokens_ref, gate_w, up_w, gate_ref, up_ref, hidden_ref):
    tokens = tokens_ref[...]
    gate, up = dot(tokens, matrix(gate_w), (1, 0)), dot(tokens, matrix(up_w), (1, 0))
    gate_ref[...] = gate
    up_ref[...] = up
    hidden_ref[...] = (gate / (1.0 + jnp.exp(-gate)) * up).astype(BF16)


def forward(tokens, gate_up, tile=256):
    count, width = tokens.shape
    hidden = gate_up.shape[2]
    return pl.pallas_call(
        forward_kernel,
        grid=(count // tile,),
        in_specs=[tall(tile, width), held(gate_up, 0), held(gate_up, 1)],
        out_specs=[tall(tile, hidden)] * 3,
        out_shape=[jax.ShapeDtypeStruct((count, hidden), t) for t in (F32, F32, BF16)],
        compiler_params=FFN_PARAMS,
        cost_estimate=pl.CostEstimate(
            flops=4 * count * width * hidden,
            bytes_accessed=4 * width * hidden + 2 * count * width + 10 * count * hidden,
            transcendentals=count * hidden,
        ),
        name="forward",
    )(tokens, gate_up, gate_up)


def hidden_back_kernel(grad_ref, gate_ref, up_ref, down_w, gate_w, up_w, gate_grad_ref, up_grad_ref, part_ref):
    grad = dot(grad_ref[...], matrix(down_w), (1, 0))
    gate = gate_ref[...]
    sigmoid = 1.0 / (1.0 + jnp.exp(-gate))
    gate_grad = (grad * up_ref[...] * sigmoid * (1.0 + gate * (1.0 - sigmoid))).astype(BF16)
    up_grad = (grad * gate * sigmoid).astype(BF16)
    gate_grad_ref[...] = gate_grad
    up_grad_ref[...] = up_grad
    part_ref[...] = (dot(gate_grad, matrix(gate_w), (1, 1)) + dot(up_grad, matrix(up_w), (1, 1))).astype(BF16)


def hidden_back(grad, gate, up, down_w, gate_up, tile=256):
    count, width = grad.shape
    hidden = gate.shape[1]
    return pl.pallas_call(
        hidden_back_kernel,
        grid=(count // tile,),
        in_specs=[
            tall(tile, width), tall(tile, hidden), tall(tile, hidden), held(down_w), held(gate_up, 0), held(gate_up, 1)
        ],
        out_specs=[tall(tile, hidden), tall(tile, hidden), tall(tile, width)],
        out_shape=[jax.ShapeDtypeStruct((count, n), BF16) for n in (hidden, hidden, width)],
        compiler_params=FFN_PARAMS,
        cost_estimate=pl.CostEstimate(
            flops=6 * count * width * hidden,
            bytes_accessed=6 * width * hidden + 16 * count * hidden,
            transcendentals=count * hidden,
        ),
        name="hidden_back",
    )(grad, gate, up, down_w, gate_up, gate_up)


def down_kernel(hidden_ref, down_w, out_ref):
    out_ref[...] = dot(hidden_ref[...], matrix(down_w), (1, 1)).astype(BF16)


def down_product(hidden, down_w, tile=256):
    count, size = hidden.shape
    width = down_w.shape[0] * down_w.shape[1]
    return pl.pallas_call(
        down_kernel,
        grid=(count // tile,),
        in_specs=[tall(tile, size), held(down_w)],
        out_specs=tall(tile, width),
        out_shape=jax.ShapeDtypeStruct((count, width), BF16),
        compiler_params=FFN_PARAMS,
        cost_estimate=pl.CostEstimate(
            flops=2 * count * width * size,
            bytes_accessed=2 * width * size + 2 * count * (width + size),
            transcendentals=0,
        ),
        name="down_product",
    )(hidden, down_w)


def paired():
    return lax.axis_size("tp") == 2 and lax.axis_size("row") == 2


def plane_sum(value):
    return lax.psum_scatter(value, ("row", "core", "tp"), scatter_dimension=0, tiled=True)


def both_cores(chunk):
    return jnp.concatenate([chunk, swap(chunk, "core")])


def other_half(part):
    return part[part.shape[0] // 2 :]


def own_half(part, got):
    return part[: part.shape[0] // 2].astype(F32) + got.astype(F32)


def far_hops(far):
    middle = far.shape[0] // 2
    return swap(far[:middle], "row"), swap(far[middle:], "tp")


def near_sends(near, hop_y, hop_x):
    half = near.shape[0] // 2
    return (
        (near[:half] + hop_y[half:].astype(F32)).astype(BF16),
        (near[half:] + hop_x[half:].astype(F32)).astype(BF16),
    )


def plane_total(own, hop_y, hop_x, top_x, bottom_y):
    half = own.shape[0] // 2
    return own + jnp.concatenate(
        [hop_y[:half].astype(F32) + top_x.astype(F32), hop_x[:half].astype(F32) + bottom_y.astype(F32)]
    )


def stage(*values):
    return lax.optimization_barrier(values)


def body(
    tokens, cotangent, lengths, head_counts, norm1_gain, norm2_gain, q_gain, k_gain,
    w_query, w_key, w_value, w_out, w_gate, w_up, w_down,
):
    pack, span, width = tokens.shape
    rows, cores, ctx, tp = (lax.axis_size(a) for a in ("row", "core", "ctx", "tp"))
    own_tokens = pack * span
    slot_count = w_query.shape[1] // HEAD_DIM
    all_slots = slot_count * tp
    devices = rows * cores * ctx
    strip = width // devices
    row_index, core_index, ctx_index, tp_index = (lax.axis_index(a) for a in ("row", "core", "ctx", "tp"))

    plane = rows * cores

    def ordered(mine, other, index):
        first = index == 0
        return jnp.where(first, mine, other), jnp.where(first, other, mine)

    part = w_gate.shape[1] // plane
    down_turned = w_down.T

    def first_hop(pick):
        mine = jnp.stack([pick(r, core_index) for r in range(rows)])
        return mine, swap(jnp.stack([pick(r, 1 - core_index) for r in range(rows)]), "core")

    def second_hop(mine, got):
        both = ordered(mine, got, core_index)
        mine = jnp.stack([lax.dynamic_index_in_dim(x, row_index, 0, False) for x in both])
        got = swap(jnp.stack([lax.dynamic_index_in_dim(x, 1 - row_index, 0, False) for x in both]), "row")
        low, high = ordered(mine, got, row_index)
        return jnp.concatenate([low, high])

    def pick_columns(r, c):
        return jnp.concatenate(
            [lax.dynamic_slice_in_dim(w, (r * cores + c) * part, part, 1) for w in (w_gate, w_up, down_turned)]
        )

    def by_weight(blocks, first, last):
        return jnp.concatenate([blocks[:, i * strip : (i + 1) * strip] for i in range(first, last)])

    def row_out(grad):
        view = grad.reshape(rows, cores, *grad.shape[1:])
        mine = lax.dynamic_index_in_dim(view, row_index, 0, False)
        got = swap(lax.dynamic_index_in_dim(view, 1 - row_index, 0, False), "row")
        return jnp.stack(ordered(mine, got, row_index))

    def core_out(both):
        mine = lax.dynamic_index_in_dim(both, core_index, 1, False)
        got = swap(lax.dynamic_index_in_dim(both, 1 - core_index, 1, False), "core")
        low, high = ordered(mine, got, core_index)
        return [x for r in range(rows) for x in (low[r], high[r])]

    def from_tp(value, axis):
        if tp == 2:
            return join(value, "tp", axis)
        return lax.all_gather(value, "tp", axis=axis, tiled=True)

    def up(value):
        return lax.ppermute(value, "ctx", [(i, i + 1) for i in range(ctx - 1)])

    def beside(value):
        if tp == 2:
            return jnp.stack([value, swap(value, "tp")])
        return lax.all_gather(value, "tp", axis=0)

    length = span * tp * ctx
    first_end = lengths[:, 0:1]
    second_end = first_end + lengths[:, 1:2]
    own_start = (ctx_index * tp + tp_index) * span
    places = own_start + jnp.arange(span, dtype=jnp.int32)[None, :]
    begins = jnp.where(places >= second_end, second_end, jnp.where(places >= first_end, first_end, 0))
    angles_of = (places - begins).astype(F32)
    frequency = jnp.exp(jnp.arange(HEAD_DIM // 2).astype(F32) * (-2.0 * math.log(THETA) / HEAD_DIM))
    angles = frequency[:, None] * angles_of.reshape(1, own_tokens)
    turn = (jnp.cos(angles), jnp.sin(angles))
    offsets = [jnp.int32(0)]
    for i in range(tp):
        offsets.append(offsets[-1] + head_counts[i])
    heads = jnp.arange(HEADS, dtype=jnp.int32)
    slots = jnp.zeros((HEADS,), jnp.int32)
    for i in range(tp):
        inside = (heads >= offsets[i]) & (heads < offsets[i + 1])
        holder = jnp.bitwise_xor(i, tp_index) if tp == 2 else i
        slots = jnp.where(inside, holder * slot_count + heads - offsets[i], slots)
    ranks = jnp.arange(devices, dtype=jnp.int32)
    near_strips = (
        (jnp.bitwise_xor(ranks // ctx % rows, row_index) * cores + jnp.bitwise_xor(ranks // (ctx * rows), core_index))
        * ctx + jnp.bitwise_xor(ranks % ctx, ctx_index)
    )
    strip_places = (
        (jnp.bitwise_xor(ranks // ctx % cores, core_index) * rows + jnp.bitwise_xor(ranks // (ctx * cores), row_index))
        * ctx + jnp.bitwise_xor(ranks % ctx, ctx_index)
    )
    blocks = ctx * tp
    steps = jnp.arange(blocks, dtype=jnp.int32) // tp
    partner = jnp.arange(blocks, dtype=jnp.int32) % tp
    if tp == 2:
        partner = jnp.bitwise_xor(partner, tp_index)
    starts = ((ctx_index - steps) * tp + partner) * span
    seen = (starts[None, :] >= 0) & (starts[None, :] <= own_start) & (starts[None, :] + span > begins[:, :1])
    counts = jnp.sum(seen.astype(jnp.int32), axis=1)
    turns = jnp.sum(
        (seen[:, None, :] & (jnp.arange(blocks)[None, None, :] < jnp.arange(blocks)[None, :, None])).astype(jnp.int32),
        axis=2,
    )
    order = jnp.sum(
        jnp.where(
            seen[:, None, :] & (turns[:, None, :] == jnp.arange(blocks)[None, :, None]),
            jnp.arange(blocks, dtype=jnp.int32)[None, None, :],
            0,
        ),
        axis=2,
    )
    tables = (
        order,
        counts,
        starts,
        slots,
        jnp.concatenate([begins] * GROUP, axis=1)[:, None, :],
        jnp.concatenate([places] * GROUP, axis=1),
    )

    half = own_tokens // 2
    two = paired()
    key_value = jnp.concatenate([w_key, w_value], axis=1)
    flat = tokens.reshape(own_tokens, width)
    grad_low = cotangent.reshape(own_tokens, width)
    normed_one, normed_near = by_tokens(norm_one_kernel, near_strips, [flat], norm1_gain, [BF16, BF16])
    kv_width = KVH * HEAD_DIM
    projected = dot(key_value, normed_one, (0, 1))
    key_proj = projected[:kv_width].reshape(KVH, HEAD_DIM, own_tokens)
    key_low = head_forward(key_proj, k_gain, turn).astype(BF16).reshape(kv_width, own_tokens)
    own_kv = jnp.concatenate([key_low, projected[kv_width:].astype(BF16)])

    mine, got = first_hop(pick_columns)
    query_part = join(w_query, "ctx", 0)
    out_part = join(w_out, "ctx", 1)
    got, query_part, out_part, own_kv = stage(got, query_part, out_part, own_kv)

    packed = second_hop(mine, got)
    gate_up, packed = by_weight(packed, 0, 2), by_weight(packed, 2, 3)
    going, arrived = up(own_kv), [beside(own_kv)]
    query_part = join(query_part, "ctx", 0, 2)
    packed, gate_up, going, arrived[0], query_part = stage(packed, gate_up, going, arrived[0], query_part)
    gate_up = lax.all_gather(gate_up, "ctx", axis=1, tiled=True)

    arrived.append(beside(going))
    going = up(going)
    query_part = join(query_part, "row", 0)
    going, arrived[1], query_part, packed = stage(going, arrived[1], query_part, packed)

    arrived.append(beside(going))
    going = up(going)
    query_part = from_tp(query_part, 1)
    out_part = join(out_part, "ctx", 1, 2)
    going, arrived[2], query_part, out_part, packed = stage(going, arrived[2], query_part, out_part, packed)

    arrived.append(beside(going))
    query_full = join(query_part, "core", 0)
    out_part = join(out_part, "row", 1)
    arrived[3], query_full, out_part, packed = stage(arrived[3], query_full, out_part, packed)
    keyvalue = jnp.concatenate(arrived)

    query_proj = dot(query_full, normed_near, (0, 1)).reshape(all_slots, HEAD_DIM, own_tokens)
    query_low = head_forward(query_proj, q_gain, turn).astype(BF16)
    out_low, totals = attend(query_low, keyvalue, tables)
    out_part = from_tp(out_part, 0)
    top, bottom = grad_low[:half], grad_low[half:]
    grad_near = (swap(top, "tp"), swap(bottom, "row")) if two else (top, bottom)
    out_low, totals, packed, gate_up = stage(out_low, totals, packed, gate_up)
    down_full = lax.all_gather(packed, "ctx", axis=1, tiled=True)
    out_low, totals, out_part, grad_near = stage(out_low, totals, out_part, grad_near)
    out_full = join(out_part, "core", 1)
    out_flat = out_low.reshape(all_slots * HEAD_DIM, own_tokens)
    attended = dot(out_flat, out_full, (0, 0))
    residual, normed_two = by_tokens(norm_two_kernel, strip_places, [flat, attended], norm2_gain, [F32, BF16])
    normed_two, residual, out_full = stage(normed_two, residual, out_full)

    if two:
        top, bottom = normed_two[:half], normed_two[half:]
        near = swap(top, "tp"), swap(bottom, "row")
        other = swap(normed_two, "core")
        near, other = stage(near, other)
        far = swap(jnp.concatenate([top, near[0]]), "row"), swap(jnp.concatenate([bottom, near[1]]), "tp")
        near = jnp.concatenate(near)
        normed_all = [jnp.concatenate([normed_two, other, near, swap(near, "core")])]
        near = jnp.concatenate(grad_near)
        grad_all = [jnp.concatenate([grad_low, swap(grad_low, "core"), near, swap(near, "core")])]
        ready = [forward(normed_all[0], gate_up)]
        far, normed_all, grad_all, ready, down_full = stage(far, normed_all, grad_all, ready, down_full)
        top, bottom = grad_low[:half], grad_low[half:]
        normed_all.append(both_cores(jnp.concatenate(far)))
        ready.append(forward(normed_all[1], gate_up))
        grad_far = (
            swap(jnp.concatenate([top, grad_near[0]]), "row"), swap(jnp.concatenate([bottom, grad_near[1]]), "tp")
        )
        ready, grad_far, grad_all, normed_all = stage(ready, grad_far, grad_all, normed_all)
        grad_all.append(both_cores(jnp.concatenate(grad_far)))
    else:
        normed_all = [lax.all_gather(normed_two, ("row", "core", "tp"), axis=0, tiled=True)]
        grad_all = [lax.all_gather(grad_low, ("row", "core", "tp"), axis=0, tiled=True)]
        ready = [forward(normed_all[0], gate_up)]
    chunks = range(len(normed_all))
    hidden = [x[2] for x in ready]

    def backward(i):
        return hidden_back(grad_all[i], ready[i][0], ready[i][1], down_full, gate_up)

    def output_part(i):
        return down_product(hidden[i], down_full)

    def scattered(gradient):
        return lax.psum_scatter(gradient, "ctx", scatter_dimension=1, tiled=True)

    if two:
        far_grads = backward(1)
        far_grads, far_send, grad_all = stage(far_grads, other_half(far_grads[2]), grad_all)
        far = own_half(far_grads[2], swap(far_send, "core")).astype(BF16)
        far_part = output_part(1)
        far, grad_all, far_part = stage(far, grad_all, far_part)
        hops = far_hops(far)
        near_grads = backward(0)
        output_far = own_half(far_part, swap(other_half(far_part), "core")).astype(BF16)
        hops, near_grads, hidden, output_far = stage(hops, near_grads, hidden, output_far)
        grads = [near_grads, far_grads]
        own_part, near_part = near_grads[2][: 2 * own_tokens], near_grads[2][2 * own_tokens :]
        near = own_half(near_part, swap(other_half(near_part), "core"))
        own = own_half(own_part, swap(other_half(own_part), "core"))
        sends = near_sends(near, *hops)
        sends, own, normed_all, hidden, grad_all = stage(sends, own, normed_all, hidden, grad_all)
        top_x, bottom_y = swap(sends[0], "tp"), swap(sends[1], "row")
        grad_down = weight_grad(grad_all, hidden, plane)
        top_x, bottom_y, output_far, grads, normed_all, grad_down = stage(
            top_x, bottom_y, output_far, grads, normed_all, grad_down
        )
        output_hops = far_hops(output_far)
        grad_normed_two = plane_total(own, *hops, top_x, bottom_y)
    else:
        grads = [backward(0)]
        grad_down = weight_grad(grad_all, hidden, plane)
        grad_normed_two = plane_sum(grads[0][2]).astype(F32)
        output_hops = grad_normed_two
    grad_down = scattered(grad_down)
    grad_residual, grad_attn, grad_norm_two = by_tokens(
        back_two_kernel, near_strips, [grad_normed_two, residual, grad_low], norm2_gain, [F32, BF16], True
    )

    grad_out = dot(out_full, grad_attn, (1, 1)).astype(BF16).reshape(all_slots, HEAD_DIM, own_tokens)
    grad_query, grad_kv = attend_back(query_low, grad_out, out_low, keyvalue, totals, tables)
    grad_out_w = dot(out_flat, grad_attn, (1, 0)).astype(BF16)
    grad_out_w = fold(grad_out_w, "core", 1)
    output_hops, grad_query, grad_kv, grads, grad_out_w, normed_all, hidden = stage(
        output_hops, grad_query, grad_kv, grads, grad_out_w, normed_all, hidden
    )
    grad_kv = grad_kv.reshape(ctx, tp, 2 * kv_width, own_tokens)

    def to_tp(value, axis):
        if tp == 2:
            return fold(value, "tp", axis)
        return lax.psum_scatter(value, "tp", scatter_dimension=axis, tiled=True)

    def to_owner(value):
        if tp == 2:
            return value[0].astype(F32) + swap(value[1], "tp").astype(F32)
        return lax.psum_scatter(value, "tp", scatter_dimension=0, tiled=False).astype(F32)

    def down(value):
        return lax.ppermute(value.astype(BF16), "ctx", [(j, j - 1) for j in range(1, ctx)]).astype(F32)

    summed = to_owner(grad_kv[ctx - 1])
    grad_gate_w = weight_grad(normed_all, [g[0] for g in grads], plane)
    out_w_low, out_w_high = grad_out_w[: all_slots * 32], grad_out_w[all_slots * 32 :]
    out_w_low = fold(out_w_low, "row", 1)
    summed, grad_kv, grad_query, out_w_low, out_w_high, normed_all, grads, grad_gate_w, grad_down = stage(
        summed, grad_kv, grad_query, out_w_low, out_w_high, normed_all, grads, grad_gate_w, grad_down
    )

    summed = to_owner(grad_kv[2]) + down(summed)
    out_w_high = fold(out_w_high, "row", 1)
    summed, grad_kv, grad_query, out_w_low, out_w_high, grad_gate_w, grad_down = stage(
        summed, grad_kv, grad_query, out_w_low, out_w_high, grad_gate_w, grad_down
    )

    summed = to_owner(grad_kv[1]) + down(summed)
    grad_query_proj, grad_q_gain = head_back(query_proj, q_gain, turn, grad_query)
    grad_query_low = grad_query_proj.astype(BF16).reshape(all_slots * HEAD_DIM, own_tokens)
    grad_down = row_out(grad_down)
    summed, grad_query_low, grad_q_gain, grad_kv, grad_down, out_w_low, out_w_high, grad_gate_w = stage(
        summed, grad_query_low, grad_q_gain, grad_kv, grad_down, out_w_low, out_w_high, grad_gate_w
    )

    summed = to_owner(grad_kv[0]) + down(summed)
    grad_query_w = dot(normed_near, grad_query_low, (0, 1)).astype(BF16)
    grad_query_w = fold(grad_query_w, "core", 0)
    grad_normed_near = dot(grad_query_low, query_full, (0, 1))
    grad_down = core_out(grad_down)
    summed, grad_query_w, grad_normed_near, grad_down, out_w_low, out_w_high, grad_gate_w, normed_all, grads, hidden = stage(
        summed, grad_query_w, grad_normed_near, grad_down, out_w_low, out_w_high, grad_gate_w, normed_all, grads, hidden
    )
    grad_gate_w = scattered(grad_gate_w)

    grad_key_proj, grad_k_gain = head_back(
        key_proj, k_gain, turn, summed[:kv_width].reshape(KVH, HEAD_DIM, own_tokens)
    )
    grad_kv_low = jnp.concatenate(
        [grad_key_proj.reshape(kv_width, own_tokens).astype(BF16), summed[kv_width:].astype(BF16)]
    )
    padded = jnp.pad(grad_kv_low, ((0, 32), (0, 0)))
    total = dot(padded, normed_near if two else normed_one, (1, 0))
    grad_normed_one = dot(grad_kv_low, key_value, (0, 1))
    grad_inputs, grad_norm_one = by_tokens(
        back_one_kernel, strip_places, [grad_normed_one, grad_normed_near, flat, grad_residual], norm1_gain, [F32], True
    )
    gains = jnp.concatenate([grad_q_gain, grad_k_gain, jnp.zeros((width - 2 * HEAD_DIM,), F32)])
    small = jnp.concatenate([grad_norm_one, grad_norm_two, gains[None]])
    moved = (near_strips if two else ranks)[:, None] == ranks[None, :]
    small = jnp.sum(
        jnp.where(moved[None, :, :, None], small.reshape(3, 1, devices, strip), 0.0), axis=2
    ).reshape(3, width)
    total = lax.dynamic_update_slice(total, small, (2 * kv_width, 0)).astype(BF16)
    query_w = fold(grad_query_w[:, : all_slots * 32], "row", 0), grad_query_w[:, all_slots * 32 :]
    grad_out_w = to_tp(jnp.concatenate([out_w_low, out_w_high]), 0)
    total, query_w, grad_out_w, hidden, normed_all, grads = stage(
        total, query_w, grad_out_w, hidden, normed_all, grads
    )

    def along(value, bit):
        got = swap(value, "ctx", bit)
        return sum32(
            value, jnp.concatenate([got[:, (j ^ bit) * strip : ((j ^ bit) + 1) * strip] for j in range(ctx)], axis=1)
        )

    if not two:
        total = lax.psum(total, ("row", "core", "ctx", "tp"))
        output = residual + plane_sum(output_part(0)).astype(F32)
        grad_up_w = scattered(weight_grad(normed_all, [g[1] for g in grads], plane))
        query_w = jnp.concatenate([query_w[0], fold(query_w[1], "row", 0)], axis=1)
        grad_query_w = fold(fold(to_tp(query_w, 1), "ctx", 0, 2), "ctx", 0)
        grad_out_w = fold(fold(grad_out_w, "ctx", 1, 2), "ctx", 1)
        grad_up_w, grad_gate_w = core_out(row_out(grad_up_w)), core_out(row_out(grad_gate_w))
    else:
        total = fold(total, "core", 1)
        total, query_w, grad_out_w, hidden, normed_all, grads = stage(
            total, query_w, grad_out_w, hidden, normed_all, grads
        )
        size = total.shape[0] // 2
        got = swap(lax.dynamic_slice_in_dim(total, (1 - tp_index) * size, size, 0), "tp")
        total = sum32(lax.dynamic_slice_in_dim(total, tp_index * size, size, 0), got)
        query_w = jnp.concatenate([query_w[0], fold(query_w[1], "row", 0)], axis=1)
        grad_up_w = weight_grad(normed_all, [g[1] for g in grads], plane)
        total, grad_out_w, query_w, hidden, grad_up_w = stage(total, grad_out_w, query_w, hidden, grad_up_w)
        grad_up_w = scattered(grad_up_w)
        total = fold(total, "row", 1)
        query_w = fold(query_w, "tp", 1)
        near_part = output_part(0)
        own_part, near_part = near_part[: 2 * own_tokens], near_part[2 * own_tokens :]
        near = own_half(near_part, swap(other_half(near_part), "core"))
        own = own_half(own_part, swap(other_half(own_part), "core"))
        sends = near_sends(near, *output_hops)
        total, query_w, sends, own, grad_gate_w, grad_out_w = stage(
            total, query_w, sends, own, grad_gate_w, grad_out_w
        )
        total = along(total, 1)
        top_x, bottom_y = swap(sends[0], "tp"), swap(sends[1], "row")
        grad_out_w = fold(grad_out_w, "ctx", 1, 2)
        total, query_w, grad_gate_w, top_x, bottom_y, grad_out_w = stage(
            total, query_w, grad_gate_w, top_x, bottom_y, grad_out_w
        )
        total = along(total, 2)
        output = residual + plane_total(own, *output_hops, top_x, bottom_y)
        grad_gate_w = row_out(grad_gate_w)
        grad_out_w = fold(grad_out_w, "ctx", 1)
        total, query_w, grad_gate_w, grad_out_w, output = stage(total, query_w, grad_gate_w, grad_out_w, output)
        total = join(total, "row", 1)
        query_w = fold(query_w, "ctx", 0, 2)
        grad_gate_w = core_out(grad_gate_w)
        total, grad_up_w, query_w, grad_gate_w = stage(total, grad_up_w, query_w, grad_gate_w)
        other = swap(total, "tp")
        grad_query_w = fold(query_w, "ctx", 0)
        grad_up_w = row_out(grad_up_w)
        first = tp_index == 0
        total = jnp.concatenate([jnp.where(first, total, other), jnp.where(first, other, total)])
        total, grad_up_w, grad_query_w = stage(total, grad_up_w, grad_query_w)
        total = join(total, "core", 1)
        grad_up_w = core_out(grad_up_w)
    grad_key_w, grad_value_w, small = unfold(strip_places if two else ranks, total, kv_width)

    return (
        output.astype(BF16).reshape(pack, span, width),
        grad_inputs.reshape(pack, span, width),
        small[0],
        small[1],
        small[2, :HEAD_DIM],
        small[2, HEAD_DIM : 2 * HEAD_DIM],
        grad_query_w.astype(F32),
        grad_key_w.T,
        grad_value_w.T,
        grad_out_w.astype(F32),
        jnp.concatenate(grad_gate_w, axis=1).astype(F32),
        jnp.concatenate(grad_up_w, axis=1).astype(F32),
        jnp.concatenate([x.T for x in grad_down]).astype(F32),
    )


def solution(mesh):
    dp, ctx, tp = (mesh.shape[a] for a in ("dp", "ctx", "tp"))
    split = Mesh(mesh.devices.reshape(dp // 2, 2, ctx, tp), ("row", "core", "ctx", "tp"))
    dp = ("row", "core")
    every = ("row", "core", "ctx")
    token = P(dp, ("ctx", "tp"), None)
    by_row, by_column = P(every, "tp"), P("tp", every)
    return jax.shard_map(
        body,
        mesh=split,
        in_specs=(
            token, token, P(dp, None), P(), P(), P(), P(), P(),
            by_row, P(), P(), by_column, by_row, by_row, by_column,
        ),
        out_specs=(
            token, token, P(), P(), P(), P(),
            by_row, P(), P(), by_column, by_row, by_row, by_column,
        ),
        check_vma=False,
    )
```
